32 devices in a mesh: dp: 4 (over x, core), row: 2 (over y), col: 4 (over z).
Axes of the slice: x: 2, y: 2, z: 4, core: 2. Of those that a mesh axis runs over, the one named last changes fastest.
Arguments:
- layer_input: bfloat16 [32768, 1024], P(('dp', 'row', 'col')), may hold values from -6 to 6
- segment_ids: int32 [32, 1024], P(('dp', 'row', 'col')), may hold values from 0 to 7, never falling along the last dimension, each value on 1 to 512 neighbouring positions
- norm1_gain: bfloat16 [1024], P(('row', 'col')), may hold values from 0.5 to 1.5
- query_weight: bfloat16 [1024, 512], P('row', 'col')
- key_weight: bfloat16 [1024, 512], P('row', 'col')
- value_weight: bfloat16 [1024, 1024], P('row', 'col'), may hold values from -0.1875 to 0.1875
- outgate_weight: bfloat16 [1024, 1024], P('row', 'col'), may hold values from -0.1875 to 0.1875
- decay_down: bfloat16 [1024, 16], P('row', 'col'), may hold values from -0.1875 to 0.1875
- decay_up: bfloat16 [16, 512], P('row', 'col'), may hold values from -1.5 to 1.5
- decay_bias: bfloat16 [512], P(('row', 'col')), may hold values from -1 to 4
- head_gain: bfloat16 [256], P(('row', 'col')), may hold values from 0.5 to 1.5
- out_weight: bfloat16 [1024, 1024], P('row', 'col'), may hold values from -0.375 to 0.375
- norm2_gain: bfloat16 [1024], P(('row', 'col')), may hold values from 0.5 to 1.5
- swiglu_gate: bfloat16 [1024, 2816], P('row', 'col'), may hold values from -0.1875 to 0.1875
- swiglu_up: bfloat16 [1024, 2816], P('row', 'col'), may hold values from -0.1875 to 0.1875
- swiglu_down: bfloat16 [2816, 1024], P('row', 'col'), may hold values from -0.109375 to 0.109375
- cotangent: bfloat16 [32768, 1024], P(('dp', 'row', 'col')), may hold values from -6 to 6
Outputs:
- layer_output: bfloat16 [32768, 1024], P(('dp', 'row', 'col'))
- input_grad: float32 [32768, 1024], P(('dp', 'row', 'col'))
- grad_norm1_gain: float32 [1024], P(('row', 'col'))
- grad_query_weight: float32 [1024, 512], P('row', 'col')
- grad_key_weight: float32 [1024, 512], P('row', 'col')
- grad_value_weight: float32 [1024, 1024], P('row', 'col')
- grad_outgate_weight: float32 [1024, 1024], P('row', 'col')
- grad_decay_down: float32 [1024, 16], P('row', 'col')
- grad_decay_up: float32 [16, 512], P('row', 'col')
- grad_decay_bias: float32 [512], P(('row', 'col'))
- grad_head_gain: float32 [256], P(('row', 'col'))
- grad_out_weight: float32 [1024, 1024], P('row', 'col')
- grad_norm2_gain: float32 [1024], P(('row', 'col'))
- grad_swiglu_gate: float32 [1024, 2816], P('row', 'col')
- grad_swiglu_up: float32 [1024, 2816], P('row', 'col')
- grad_swiglu_down: float32 [2816, 1024], P('row', 'col')
The draws below stay inside these ranges and needn't reach their ends.
Inputs may be any that keep to these rules, and one draw needn't show every extreme that they name: `segment_ids`: within each packed row the ids never fall; a document covers at most 512 positions and one covers exactly that many; every row holds all eight ids.
All inputs are finite; a program needn't handle non-finite values.
Results may differ from the reference program's by a relative error of at most 0.02.
Values may be sent and summed in bfloat16 or wider, within the bound.
No kernel may reach another device: no remote copies, remote signals or barrier semaphores. Data moves between devices by JAX's collectives and lax.ppermute only.
A program may use at most 320 MiB of HBM per device.

```python
import math
import jax
import jax.numpy as jnp
import numpy as np
from jax import lax

D = 1024
HEADS = 4
HK = 128
HV = 256
LOW = 16
FF = 2816
CH = 64
LEN = 1024
K = 512
V = 1024
SEQS = 32
TOKENS = 32768


def projection_pair(key):
    first = jax.random.normal(jax.random.fold_in(key, 7101), (D, K), jnp.float32)
    second = jax.random.normal(jax.random.fold_in(key, 7102), (D, K), jnp.float32)
    first = jnp.clip(first, -6.0, 6.0) * D ** (-0.5)
    second = jnp.clip(second, -6.0, 6.0) * D ** (-0.5)
    return (first, 0.6 * first + 0.8 * second)


def draw_query_weight(key, part):
    return projection_pair(key)[0].astype(jnp.bfloat16)


def draw_key_weight(key, part):
    return projection_pair(key)[1].astype(jnp.bfloat16)


def strengthened(entries, own_key, source, target, parts, factor):
    def block_of(position):
        return (jnp.arange(entries.shape[position]) // (entries.shape[position] // parts)).reshape((-1,) + (1,) * (entries.ndim - 1 - position))

    first = jax.random.permutation(own_key, parts)[block_of(target)]
    far = (block_of(target) + parts // 2) % parts
    return jnp.where((block_of(source) == first) | (block_of(source) == far), factor * entries, entries)


def block_levels(own_key, dims, cuts, smallest, largest):
    level = 1.0
    for position, shards_of in cuts:
        steps = jax.random.uniform(jax.random.fold_in(jax.random.fold_in(own_key, 6), position), (shards_of,), jnp.float32, smallest / len(cuts), largest / len(cuts))
        level = level * jnp.repeat(jnp.exp(steps), dims[position] // shards_of).reshape((-1,) + (1,) * (len(dims) - 1 - position))
    return level


def length_profile(count, total, reach, slope):
    weights = [(1 << 20) // math.isqrt(grade ** slope) + 1 for grade in range(2, count + 1)]
    surplus, counts = total - reach - (count - 1), [1] * (count - 1)
    while surplus > 0:
        free = [i for i in range(count - 1) if counts[i] < reach]
        whole, budget = sum([weights[i] for i in free]), surplus
        for i in free:
            addition = min(reach - counts[i], max(1, budget * weights[i] // whole), surplus)
            counts[i] = counts[i] + addition
            surplus = surplus - addition
    return np.array([reach] + counts)


def uneven(key, amount, total, most, lean):
    if amount == 2:
        one = jax.random.randint(key, (), max(1, total - most), min(most, total - 1) + 1)
        return jnp.stack([one, total - one])
    tallies = jnp.asarray(length_profile(amount, total, most, lean), jnp.int32)
    pairs = (amount - 1) // 2
    giver, receiver = tallies[1:1 + 2 * pairs:2], tallies[2:2 + 2 * pairs:2]
    margin = jnp.minimum(giver - 1, most - receiver)
    shifted = jax.random.randint(jax.random.fold_in(key, 1), (pairs,), 0, 1 << 20) % (margin + 1)
    tallies = tallies.at[1:1 + 2 * pairs:2].set(giver - shifted).at[2:2 + 2 * pairs:2].set(receiver + shifted)
    return tallies[jax.random.permutation(jax.random.fold_in(key, 2), amount)]


def gaussian(key, dims, deviation, most, pieces=(), kind=jnp.bfloat16):
    factor_of = block_levels(key, dims, pieces, -0.22, 0.18) if pieces else 1.0
    values = jax.random.normal(key, dims, jnp.float32) * deviation * factor_of
    return jnp.minimum(jnp.maximum(values, -most), most).astype(kind)


def bell_draw_with(own_key, extent, width, limit, split, heavy, held_as=jnp.bfloat16):
    drawn = width * jax.random.normal(own_key, extent, jnp.float32)
    if split:
        drawn = drawn * block_levels(own_key, extent, split, -0.22, 0.18)
    return jnp.clip(strengthened(drawn, jax.random.fold_in(own_key, 3), *heavy), -limit, limit).astype(held_as)


def setup_inputs(seed: int = 0) -> dict:
    arg_keys = jax.random.split(jax.random.key(seed), 18)
    layer_input = gaussian(arg_keys[0], (TOKENS, D), 1.0, 6.0, ((0, 32),))
    segment_ids = jax.vmap(lambda own: jnp.searchsorted(jnp.cumsum(uneven(own, 8, LEN, LEN // 2, 1)), jnp.arange(LEN), side="right"))(jax.random.split(arg_keys[1], SEQS)).reshape((SEQS, LEN)).astype(jnp.int32)
    norm1_gain = jnp.clip(1.0 + 0.1 * jax.random.normal(arg_keys[2], (D,), jnp.float32), 0.5, 1.5).astype(jnp.bfloat16)
    query_weight = draw_query_weight(jax.random.fold_in(arg_keys[17], 71), 0)
    key_weight = draw_key_weight(jax.random.fold_in(arg_keys[17], 71), 0)
    value_weight = gaussian(arg_keys[5], (D, V), D ** -0.5, 0.1875, ((0, 2), (1, 4)))
    outgate_weight = gaussian(arg_keys[6], (D, V), D ** -0.5, 0.1875, ((0, 2), (1, 4)))
    decay_down = gaussian(arg_keys[7], (D, LOW), D ** -0.5, 0.1875, ((0, 2), (1, 4)))
    decay_up = gaussian(arg_keys[8], (LOW, K), LOW ** -0.5, 1.5, ((0, 2), (1, 4)))
    decay_bias = jnp.clip(-1.0 + 5.0 * jax.random.uniform(arg_keys[9], (K,), jnp.float32) ** block_levels(arg_keys[9], (K,), ((0, 8),), -0.2, 0.2), -1.0, 4.0).astype(jnp.bfloat16)
    head_gain = jnp.clip(1.0 + 0.1 * jax.random.normal(arg_keys[10], (HV,), jnp.float32), 0.5, 1.5).astype(jnp.bfloat16)
    out_weight = gaussian(arg_keys[11], (V, D), (V // 4) ** -0.5, 0.375, ((0, 2), (1, 4)))
    norm2_gain = jnp.clip(1.0 + 0.1 * jax.random.normal(arg_keys[12], (D,), jnp.float32), 0.5, 1.5).astype(jnp.bfloat16)
    swiglu_gate = gaussian(arg_keys[13], (D, FF), D ** -0.5, 0.1875, ((0, 2), (1, 4)))
    swiglu_up = gaussian(arg_keys[14], (D, FF), D ** -0.5, 0.1875, ((0, 2), (1, 4)))
    swiglu_down = gaussian(arg_keys[15], (FF, D), FF ** -0.5, 0.109375, ((0, 2), (1, 4)))
    cotangent = bell_draw_with(arg_keys[16], (TOKENS, D), 1.0, 6.0, ((0, 32),), (0, 1, 32, 2.75))
    return dict(layer_input=layer_input, segment_ids=segment_ids, norm1_gain=norm1_gain, query_weight=query_weight, key_weight=key_weight, value_weight=value_weight, outgate_weight=outgate_weight, decay_down=decay_down, decay_up=decay_up, decay_bias=decay_bias, head_gain=head_gain, out_weight=out_weight, norm2_gain=norm2_gain, swiglu_gate=swiglu_gate, swiglu_up=swiglu_up, swiglu_down=swiglu_down, cotangent=cotangent)


EPS = 1e-05
HIGH = lax.Precision.HIGHEST

@jax.custom_vjp
def low(v):
    return lax.optimization_barrier(v.astype(jnp.bfloat16)).astype(jnp.float32)

@jax.custom_vjp
def low_back(v):
    return v

def low_keep(v):
    return (low(v), None)

def low_pass(kept, grad):
    return (grad,)

def back_keep(v):
    return (v, None)

def back_low(kept, grad):
    return (low(grad),)
low.defvjp(low_keep, low_pass)
low_back.defvjp(back_keep, back_low)

def product(left, right):
    return jnp.dot(left, right, precision=HIGH)

def rms_scale(values, gain):
    return values * lax.rsqrt(lax.optimization_barrier(jnp.mean(values * values, axis=-1, keepdims=True)) + EPS) * gain

def attention(query, keys, values, log_decay, documents):
    key_scale = HK ** (-0.5)
    spans = LEN // CH
    query_c = query.reshape(spans, CH, HEADS, HK)
    key_c = keys.reshape(spans, CH, HEADS, HK)
    value_c = values.reshape(spans, CH, HEADS, HV)
    decay_c = log_decay.reshape(spans, CH, HEADS, HK)
    doc_c = documents.astype(jnp.int32).reshape(spans, CH)
    places = jnp.arange(CH, dtype=jnp.int32)

    def step(carried, inputs):
        state_now, prev_doc = carried
        query_part, key_part, value_part, decay_part, doc_part = inputs
        cumul = jnp.cumsum(decay_part, axis=0)
        allowed = (places[:, None] >= places[None, :]) & (doc_part[:, None] == doc_part[None, :])
        pair_mask = allowed[:, :, None, None]
        spread = cumul[:, None] - cumul[None, :]
        decays = jnp.where(pair_mask, jnp.exp(jnp.where(pair_mask, spread, 0.0)), 0.0)
        scores = jnp.einsum('thi,shi,tshi->hts', query_part, key_part, decays, precision=HIGH) * key_scale
        local_out = jnp.einsum('hts,shj->thj', scores, value_part, precision=HIGH)
        enter = (doc_part == prev_doc).astype(jnp.float32)[:, None, None]
        growth = jnp.exp(cumul)
        carried_out = jnp.einsum('thi,hij->thj', query_part * growth * enter, state_now, precision=HIGH) * key_scale
        last_doc = doc_part[CH - 1].astype(jnp.int32)
        carry_on = (last_doc == prev_doc).astype(jnp.float32)
        same_doc = (doc_part == last_doc).astype(jnp.float32)[:, None, None]
        to_end = jnp.exp(cumul[CH - 1:] - cumul)
        next_state = carry_on * growth[CH - 1][:, :, None] * state_now + jnp.einsum('shi,shj->hij', key_part * to_end * same_doc, value_part, precision=HIGH)
        return ((next_state, last_doc), local_out + carried_out)
    start = (jnp.zeros((HEADS, HK, HV), jnp.float32), jnp.full((), -1, jnp.int32))
    final_carry, outputs = lax.scan(jax.checkpoint(step), start, (query_c, key_c, value_c, decay_c, doc_c))
    return outputs.reshape(LEN, HEADS * HV)

def residual_block(inputs, documents, gain_one, query_mat, key_mat, value_mat, outgate_mat, down_mat, up_mat, bias_vec, head_vec, output_mat, gain_two, gate_mat, lift_mat, lower_mat):
    normed_one = low(rms_scale(inputs, gain_one))
    query = low_back(low(product(normed_one, query_mat)))
    keys = low_back(low(product(normed_one, key_mat)))
    values = low_back(low(product(normed_one, value_mat)))
    outgate = low_back(product(normed_one, outgate_mat))
    low_rank = low_back(product(normed_one, down_mat))
    decay_logit = product(low_rank, up_mat) + bias_vec
    log_decay = jax.nn.log_sigmoid(decay_logit) / 16.0
    mixed = attention(query, keys, values, log_decay, documents)
    head_normed = rms_scale(mixed.reshape(LEN, HEADS, HV), head_vec)
    gated = low((head_normed * jax.nn.silu(outgate.reshape(LEN, HEADS, HV))).reshape(LEN, HEADS * HV))
    middle = inputs + low_back(product(gated, output_mat))
    normed_two = low(rms_scale(middle, gain_two))
    gate_pre = low_back(product(normed_two, gate_mat))
    lift_pre = low_back(product(normed_two, lift_mat))
    hidden = low(jax.nn.silu(gate_pre) * lift_pre)
    return middle + low_back(product(hidden, lower_mat))

def reference(layer_input, segment_ids, norm1_gain, query_weight, key_weight, value_weight, outgate_weight, decay_down, decay_up, decay_bias, head_gain, out_weight, norm2_gain, swiglu_gate, swiglu_up, swiglu_down, cotangent):
    weights = tuple((member.astype(jnp.float32) for member in (norm1_gain, query_weight, key_weight, value_weight, outgate_weight, decay_down, decay_up, decay_bias, head_gain, out_weight, norm2_gain, swiglu_gate, swiglu_up, swiglu_down)))
    sequences = layer_input.astype(jnp.float32).reshape(SEQS, LEN, D)
    incoming = cotangent.astype(jnp.float32).reshape(SEQS, LEN, D)
    documents = segment_ids.astype(jnp.int32)

    def one_sequence(totals, items):
        inputs_seq, docs_seq, grad_seq = items

        def forward(values, *params):
            return residual_block(values, docs_seq, *params)
        result, pullback = jax.vjp(forward, inputs_seq, *weights)
        grads = pullback(grad_seq)
        summed = tuple((total + grad for total, grad in zip(totals, grads[1:])))
        return (summed, (result.astype(jnp.bfloat16), grads[0]))
    start = tuple((jnp.zeros(member.shape, jnp.float32) for member in weights))
    totals, results = lax.scan(one_sequence, start, (sequences, documents, incoming))
    outputs, input_grads = results
    return (outputs.reshape(TOKENS, D), input_grads.reshape(TOKENS, D), totals[0], totals[1], totals[2], totals[3], totals[4], totals[5], totals[6], totals[7], totals[8], totals[9], totals[10], totals[11], totals[12], totals[13])
```

```python
import functools

import jax
import jax.numpy as jnp
from jax import lax
from jax.experimental import pallas as pl
from jax.experimental.pallas import tpu as pltpu
from jax.sharding import Mesh
from jax.sharding import PartitionSpec as P

HEADS = 4
HK = 128
HV = 256
CH = 64
LOW = 16
D = 1024
K = HEADS * HK
V = HEADS * HV
FF = 2816
HC = FF // 4
TILE = 256

EPS = 1e-05
HIGH = lax.Precision.HIGHEST
F32 = jnp.float32
BF16 = jnp.bfloat16
AXES = ("x", "core", "row", "col")
MIB = 1024 * 1024


def dot(left, right, precision=None):
    return jnp.dot(left, right, preferred_element_type=F32, precision=precision)


def dot_nt(left, right, precision=None):
    return lax.dot_general(
        left, right, (((1,), (1,)), ((), ())), preferred_element_type=F32, precision=precision
    )


def dot_tn(left, right, precision=None):
    return lax.dot_general(
        left, right, (((0,), (0,)), ((), ())), preferred_element_type=F32, precision=precision
    )


def struct(shape, dtype):
    return jax.ShapeDtypeStruct(shape, dtype)


def fixed(shape):
    return pl.BlockSpec(shape, lambda *i: (0,) * len(shape))


def rows(height, width):
    return pl.BlockSpec((height, width), lambda i: (i, 0))


def cost(flops, moved, trans=0):
    return pl.CostEstimate(flops=int(flops), bytes_accessed=int(moved), transcendentals=int(trans))


def params(mib):
    return pltpu.CompilerParams(vmem_limit_bytes=mib * MIB)


def project_kernel(x_ref, gain_ref, w_ref, ddt_ref, du_ref, bias_ref, n_ref, q_ref, k_ref, v_ref, low_ref, logit_ref):
    x = x_ref[...].astype(F32)
    inverse = lax.rsqrt(jnp.mean(x * x, axis=-1, keepdims=True) + EPS)
    normed = (x * inverse * gain_ref[...]).astype(BF16)
    n_ref[...] = normed
    for c in range(HEADS):
        total = None
        for r in range(2):
            for core in range(2):
                at = r * 512 + core * 256
                part = dot(normed[:, at : at + 256], w_ref[core, r, c])
                total = part if total is None else total + part
        q_ref[:, c * HK : (c + 1) * HK] = total[:, :HK].astype(BF16)
        k_ref[:, c * HK : (c + 1) * HK] = total[:, HK : 2 * HK].astype(BF16)
        v_ref[:, c * HV : (c + 1) * HV] = total[:, 2 * HK :].astype(BF16)
    low = dot_nt(normed[:, :512], ddt_ref[0]) + dot_nt(normed[:, 512:], ddt_ref[1])
    low_ref[...] = low
    logit_ref[...] = dot(low, du_ref[...], HIGH) + bias_ref[...]


def project(x, gain, weights, ddt, du, bias):
    tokens = x.shape[0]
    return pl.pallas_call(
        project_kernel,
        grid=(tokens // TILE,),
        in_specs=[
            rows(TILE, D),
            fixed((1, D)),
            fixed((2, 2, 4, 256, 512)),
            fixed((2, LOW, 512)),
            fixed((LOW, K)),
            fixed((1, K)),
        ],
        out_specs=[rows(TILE, D), rows(TILE, K), rows(TILE, K), rows(TILE, V), rows(TILE, LOW), rows(TILE, K)],
        out_shape=[
            struct((tokens, D), BF16),
            struct((tokens, K), BF16),
            struct((tokens, K), BF16),
            struct((tokens, V), BF16),
            struct((tokens, LOW), F32),
            struct((tokens, K), F32),
        ],
        compiler_params=params(40),
        cost_estimate=cost(2 * tokens * D * 2048, 14 * MIB),
        name="project",
    )(x, gain, weights, ddt, du, bias)


def span_parts(logit, doc_c, doc_r, last_doc, prev_doc):
    lower = lax.broadcasted_iota(jnp.int32, (CH, CH), 0) >= lax.broadcasted_iota(jnp.int32, (CH, CH), 1)
    mask = jnp.where(lower & (doc_c == doc_r), HK ** (-0.5), 0.0)
    log_decay = (jnp.minimum(logit, 0.0) - jnp.log1p(jnp.exp(-jnp.abs(logit)))) * (1.0 / 16.0)
    cumul = dot(lower.astype(F32), log_decay, HIGH)
    centre = cumul[CH // 2 - 1 : CH // 2]
    last = cumul[CH - 1 :]
    rise = jnp.exp(cumul - centre)
    fall = jnp.exp(centre - cumul)
    growth = jnp.exp(cumul)
    to_end = jnp.exp(last - cumul)
    enter = jnp.where(doc_c == prev_doc, HK ** (-0.5), 0.0)
    same = jnp.where(doc_c == last_doc, 1.0, 0.0)
    return mask, rise, fall, growth, to_end, enter, same, jnp.exp(last)


def span_docs(seg_ref, at, first):
    last_doc = seg_ref[at + CH - 1]
    prev_doc = jnp.where(first, -1, seg_ref[jnp.maximum(at - 1, 0)])
    return last_doc, prev_doc


def attend_kernel(spans, seg_ref, q_ref, k_ref, v_ref, logit_ref, dc_ref, dr_ref, mixed_ref, states_ref, state):
    i = pl.program_id(1)
    at = (pl.program_id(0) * spans + i) * CH
    last_doc, prev_doc = span_docs(seg_ref, at, i == 0)

    @pl.when(i == 0)
    def _():
        state[...] = jnp.zeros_like(state)

    mask, rise, fall, growth, to_end, enter, same, keep = span_parts(
        logit_ref[...], dc_ref[...], dr_ref[0], last_doc, prev_doc
    )
    query = q_ref[...].astype(F32)
    keys = k_ref[...].astype(F32)
    qs = (query * rise).astype(BF16)
    ks = (keys * fall).astype(BF16)
    qg = (query * growth * enter).astype(BF16)
    kw = (keys * to_end * same).astype(BF16)
    keep = keep * jnp.where(last_doc == prev_doc, 1.0, 0.0)
    for h in range(HEADS):
        a, b = h * HK, (h + 1) * HK
        va = v_ref[:, h * HV : (h + 1) * HV]
        now = state[h]
        low = now.astype(BF16)
        states_ref[0, h] = low
        scores = (dot_nt(qs[:, a:b], ks[:, a:b]) * mask).astype(BF16)
        mixed_ref[:, h * HV : (h + 1) * HV] = dot(scores, va) + dot_nt(qg[:, a:b], low)
        state[h] = now * keep[:, a:b] + dot_tn(va, kw[:, a:b])


def attend(q, k, v, logit, segs, seg_c, seg_r):
    tokens = q.shape[0]
    seqs = segs.shape[0]
    spans = tokens // seqs // CH

    def part(width):
        return pl.BlockSpec((CH, width), lambda s, i, seg: (s * spans + i, 0))

    return pl.pallas_call(
        functools.partial(attend_kernel, spans),
        grid_spec=pltpu.PrefetchScalarGridSpec(
            num_scalar_prefetch=1,
            grid=(seqs, spans),
            in_specs=[
                part(K),
                part(K),
                part(V),
                part(K),
                part(1),
                pl.BlockSpec((1, 1, CH), lambda s, i, seg: (s * spans + i, 0, 0)),
            ],
            out_specs=[
                part(V),
                pl.BlockSpec((1, HEADS, HV, HK), lambda s, i, seg: (s * spans + i, 0, 0, 0)),
            ],
            scratch_shapes=[pltpu.VMEM((HEADS, HV, HK), F32)],
        ),
        out_shape=[struct((tokens, V), F32), struct((seqs * spans, HEADS, HV, HK), BF16)],
        compiler_params=params(32),
        cost_estimate=cost(2e10, 16 * MIB),
        name="attend",
    )(segs.reshape(-1), q, k, v, logit, seg_c, seg_r)


def attend_back_kernel(
    spans, seg_ref, q_ref, k_ref, v_ref, logit_ref, dc_ref, dr_ref, states_ref, g_ref,
    gq_ref, gk_ref, gv_ref, gl_ref, grad_state,
):
    i = spans - 1 - pl.program_id(1)
    at = (pl.program_id(0) * spans + i) * CH
    last_doc, prev_doc = span_docs(seg_ref, at, i == 0)

    @pl.when(pl.program_id(1) == 0)
    def _():
        grad_state[...] = jnp.zeros_like(grad_state)

    mask, rise, fall, growth, to_end, enter, same, keep = span_parts(
        logit_ref[...], dc_ref[...], dr_ref[0], last_doc, prev_doc
    )
    query = q_ref[...].astype(F32)
    keys = k_ref[...].astype(F32)
    qs = (query * rise).astype(BF16)
    ks = (keys * fall).astype(BF16)
    qg = (query * growth * enter).astype(BF16)
    kw = (keys * to_end * same).astype(BF16)
    keep = keep * jnp.where(last_doc == prev_doc, 1.0, 0.0)
    last_row = lax.broadcasted_iota(jnp.int32, (CH, HK), 0) == CH - 1
    upper = lax.broadcasted_iota(jnp.int32, (CH, CH), 0) <= lax.broadcasted_iota(jnp.int32, (CH, CH), 1)
    upper = upper.astype(F32)
    for h in range(HEADS):
        a, b = h * HK, (h + 1) * HK
        va = v_ref[:, h * HV : (h + 1) * HV]
        ga = g_ref[:, h * HV : (h + 1) * HV]
        qh, kh = qs[:, a:b], ks[:, a:b]
        state = states_ref[0, h]
        grad = grad_state[h]
        grad_low = grad.astype(BF16)
        scores = (dot_nt(qh, kh) * mask).astype(BF16)
        grad_scores = (dot_nt(ga, va) * mask).astype(BF16)
        gv_ref[:, h * HV : (h + 1) * HV] = (dot_tn(scores, ga) + dot_nt(kw[:, a:b], grad_low)).astype(BF16)
        wk = dot(va, grad_low) * same * to_end[:, a:b]
        wq = dot(ga, state) * enter * growth[:, a:b]
        query_inner = dot(grad_scores, kh)
        key_inner = dot_tn(grad_scores, qh)
        gq_ref[:, a:b] = (query_inner * rise[:, a:b] + wq).astype(BF16)
        gk_ref[:, a:b] = (key_inner * fall[:, a:b] + wk).astype(BF16)
        ends = wk * keys[:, a:b]
        grad_cumul = qh.astype(F32) * query_inner - kh.astype(F32) * key_inner + query[:, a:b] * wq - ends
        kept = grad * keep[:, a:b]
        at_last = jnp.sum(ends, axis=0, keepdims=True) + jnp.sum(kept * state.astype(F32), axis=0, keepdims=True)
        grad_cumul = grad_cumul + jnp.where(last_row, at_last, 0.0)
        gl_ref[:, a:b] = dot(upper, grad_cumul, HIGH)
        grad_state[h] = kept + dot_tn(ga, qg[:, a:b])


def attend_back(q, k, v, logit, segs, seg_c, seg_r, states, grad):
    tokens = q.shape[0]
    seqs = segs.shape[0]
    spans = tokens // seqs // CH

    def part(width):
        return pl.BlockSpec((CH, width), lambda s, i, seg: (s * spans + spans - 1 - i, 0))

    return pl.pallas_call(
        functools.partial(attend_back_kernel, spans),
        grid_spec=pltpu.PrefetchScalarGridSpec(
            num_scalar_prefetch=1,
            grid=(seqs, spans),
            in_specs=[
                part(K),
                part(K),
                part(V),
                part(K),
                part(1),
                pl.BlockSpec((1, 1, CH), lambda s, i, seg: (s * spans + spans - 1 - i, 0, 0)),
                pl.BlockSpec((1, HEADS, HV, HK), lambda s, i, seg: (s * spans + spans - 1 - i, 0, 0, 0)),
                part(V),
            ],
            out_specs=[part(K), part(K), part(V), part(K)],
            scratch_shapes=[pltpu.VMEM((HEADS, HV, HK), F32)],
        ),
        out_shape=[
            struct((tokens, K), BF16),
            struct((tokens, K), BF16),
            struct((tokens, V), BF16),
            struct((tokens, K), F32),
        ],
        compiler_params=params(32),
        cost_estimate=cost(5e10, 20 * MIB),
        name="attend_back",
    )(segs.reshape(-1), q, k, v, logit, seg_c, seg_r, states, grad)


def mix_kernel(x_ref, n_ref, mixed_ref, w_ref, hg_ref, g2_ref, og_ref, gated_ref, middle_ref, n2_ref):
    normed = n_ref[...]
    outs = [None] * 4
    for c in range(HEADS):
        og = None
        for r in range(2):
            for core in range(2):
                at = r * 512 + core * 256
                part = dot(normed[:, at : at + 256], w_ref[core, r, c, :, :HV])
                og = part if og is None else og + part
        og_ref[:, c * HV : (c + 1) * HV] = og
        mixed = mixed_ref[:, c * HV : (c + 1) * HV]
        inverse = lax.rsqrt(jnp.mean(mixed * mixed, axis=-1, keepdims=True) + EPS)
        gated = (mixed * inverse * hg_ref[...] * (og * jax.nn.sigmoid(og))).astype(BF16)
        gated_ref[:, c * HV : (c + 1) * HV] = gated
        for e in range(4):
            part = dot(gated, w_ref[c % 2, c // 2, e, :, HV:])
            outs[e] = part if outs[e] is None else outs[e] + part
    middle = x_ref[...].astype(F32) + jnp.concatenate(outs, axis=1)
    middle_ref[...] = middle
    inverse = lax.rsqrt(jnp.mean(middle * middle, axis=-1, keepdims=True) + EPS)
    n2_ref[...] = (middle * inverse * g2_ref[...]).astype(BF16)


def mix(x, normed, mixed, weights, head_gain, gain_two):
    tokens = x.shape[0]
    return pl.pallas_call(
        mix_kernel,
        grid=(tokens // TILE,),
        in_specs=[
            rows(TILE, D),
            rows(TILE, D),
            rows(TILE, V),
            fixed((2, 2, 4, 256, 512)),
            fixed((1, HV)),
            fixed((1, D)),
        ],
        out_specs=[rows(TILE, V), rows(TILE, V), rows(TILE, D), rows(TILE, D)],
        out_shape=[
            struct((tokens, V), F32),
            struct((tokens, V), BF16),
            struct((tokens, D), F32),
            struct((tokens, D), BF16),
        ],
        compiler_params=params(48),
        cost_estimate=cost(2 * tokens * D * 2048, 24 * MIB),
        name="mix",
    )(x, normed, mixed, weights, head_gain, gain_two)


def feed_kernel(
    core_ref, n2_ref, dy_ref, middle_ref, gl_ref, dn_ref,
    out_ref, gn_ref, keep_gl, send_gl, keep_dn, send_dn, y_acc, hid, gate_g, lift_g,
):
    step = pl.program_id(0)
    core = core_ref[0]

    @pl.loop(0, n2_ref.shape[0] // TILE)
    def _(t):
        at = pl.ds(pl.multiple_of(t * TILE, TILE), TILE)
        gate = lift = back = None
        for r in range(2):
            n2 = n2_ref[at, r * 512 : (r + 1) * 512]
            a = dot_nt(n2, gl_ref[:, r, 0, :176].reshape(HC, 512))
            b = dot_nt(n2, gl_ref[:, r, 0, 176:].reshape(HC, 512))
            gate = a if r == 0 else gate + a
            lift = b if r == 0 else lift + b
        for c in range(4):
            a = dot_nt(dy_ref[at, c * 256 : (c + 1) * 256], dn_ref[:, 0, c].reshape(HC, 256))
            back = a if c == 0 else back + a
        sig = jax.nn.sigmoid(gate)
        swish = gate * sig
        hidden = (swish * lift).astype(BF16)
        grad_lift = (back * swish).astype(BF16)
        grad_gate = (back * lift * sig * (1.0 + gate * (1.0 - sig))).astype(BF16)
        hid[at, :] = hidden
        gate_g[at, :] = grad_gate
        lift_g[at, :] = grad_lift
        for c in range(4):
            part = dot(hidden, dn_ref[:, 0, c].reshape(HC, 256))
            lanes = slice(c * 256, (c + 1) * 256)

            @pl.when(step == 0)
            def _():
                y_acc[at, lanes] = part

            @pl.when(step > 0)
            def _():
                y_acc[at, lanes] += part

        for r in range(2):
            part = dot(grad_gate, gl_ref[:, r, 0, :176].reshape(HC, 512)) + dot(
                grad_lift, gl_ref[:, r, 0, 176:].reshape(HC, 512)
            )
            lanes = slice(r * 512, (r + 1) * 512)

            @pl.when(step == 0)
            def _():
                gn_ref[at, lanes] = part

            @pl.when(step > 0)
            def _():
                gn_ref[at, lanes] += part

        @pl.when(step == 3)
        def _():
            out_ref[at, :] = (middle_ref[at, :] + y_acc[at, :]).astype(BF16)

    first = core == 0
    for r in range(2):
        n2 = n2_ref[:, r * 512 : (r + 1) * 512]
        for m, source in enumerate((gate_g, lift_g)):
            both = dot_tn(source[...], n2).astype(BF16)
            low, high = both[: HC // 2], both[HC // 2 :]
            mine = jnp.where(first, low, high)
            other = jnp.where(first, high, low)
            for x in range(2):
                keep_gl[x, r, 0, m * 176 : (m + 1) * 176] = mine[x * 176 : (x + 1) * 176]
                send_gl[x, r, 0, m * 176 : (m + 1) * 176] = other[x * 176 : (x + 1) * 176]
    for c in range(4):
        both = dot_tn(hid[...], dy_ref[:, c * 256 : (c + 1) * 256]).astype(BF16)
        low, high = both[: HC // 2], both[HC // 2 :]
        mine = jnp.where(first, low, high)
        other = jnp.where(first, high, low)
        for x in range(2):
            keep_dn[x, 0, c, 0] = mine[x * 176 : (x + 1) * 176]
            send_dn[x, 0, c, 0] = other[x * 176 : (x + 1) * 176]


def feed(core, n2, dy, middle, weights):
    tokens = n2.shape[0]
    gl = pl.BlockSpec((2, 2, 1, 352, 512), lambda i, c: (0, 0, i, 0, 0))
    dn = pl.BlockSpec((2, 1, 4, 1, 176, 256), lambda i, c: (0, i // 2, 0, i % 2, 0, 0))
    once = pl.Buffered(1)
    return pl.pallas_call(
        feed_kernel,
        grid_spec=pltpu.PrefetchScalarGridSpec(
            num_scalar_prefetch=1,
            grid=(4,),
            in_specs=[
                pl.BlockSpec((tokens, D), lambda i, c: (0, 0), pipeline_mode=once),
                pl.BlockSpec((tokens, D), lambda i, c: (0, 0), pipeline_mode=once),
                pl.BlockSpec((tokens, D), lambda i, c: (0, 0), pipeline_mode=once),
                pl.BlockSpec((4, 2, 1, 352, 512), lambda i, c: (0, 0, i, 0, 0)),
                pl.BlockSpec((2, 1, 4, 352, 256), lambda i, c: (i % 2, i // 2, 0, 0, 2)),
            ],
            out_specs=[
                pl.BlockSpec((tokens, D), lambda i, c: (0, 0), pipeline_mode=once),
                pl.BlockSpec((tokens, D), lambda i, c: (0, 0), pipeline_mode=once),
                gl,
                gl,
                dn,
                dn,
            ],
            scratch_shapes=[
                pltpu.VMEM((tokens, D), F32),
                pltpu.VMEM((tokens, HC), BF16),
                pltpu.VMEM((tokens, HC), BF16),
                pltpu.VMEM((tokens, HC), BF16),
            ],
        ),
        out_shape=[
            struct((tokens, D), BF16),
            struct((tokens, D), F32),
            struct((2, 2, 4, 352, 512), BF16),
            struct((2, 2, 4, 352, 512), BF16),
            struct((2, 2, 4, 2, 176, 256), BF16),
            struct((2, 2, 4, 2, 176, 256), BF16),
        ],
        compiler_params=params(60),
        cost_estimate=cost(18 * tokens * D * FF, 60 * MIB),
        name="feed",
    )(core, n2, dy, middle, weights, weights)


def unmix_kernel(
    gn_ref, middle_ref, dy_ref, og_ref, mixed_ref, w_ref, hg_ref, g2_ref,
    gm_ref, gb_ref, gog_ref, gmix_ref, gg2_ref, ghg_ref,
):
    @pl.when(pl.program_id(0) == 0)
    def _():
        gg2_ref[...] = jnp.zeros_like(gg2_ref)
        ghg_ref[...] = jnp.zeros_like(ghg_ref)

    grad = gn_ref[...]
    middle = middle_ref[...]
    inverse = lax.rsqrt(jnp.mean(middle * middle, axis=-1, keepdims=True) + EPS)
    unit = middle * inverse
    gg2_ref[...] += jnp.sum(grad * unit, axis=0, keepdims=True)
    scaled = grad * g2_ref[...]
    grad_middle = dy_ref[...].astype(F32) + inverse * (scaled - unit * jnp.mean(scaled * unit, axis=-1, keepdims=True))
    gm_ref[...] = grad_middle
    branch = grad_middle.astype(BF16)
    gb_ref[...] = branch
    head_gain = hg_ref[...]
    for c in range(HEADS):
        lanes = slice(c * HV, (c + 1) * HV)
        back = None
        for e in range(4):
            part = dot_nt(branch[:, e * 256 : (e + 1) * 256], w_ref[c % 2, c // 2, e, :, HV:])
            back = part if back is None else back + part
        og = og_ref[:, lanes]
        sig = jax.nn.sigmoid(og)
        mixed = mixed_ref[:, lanes]
        inv = lax.rsqrt(jnp.mean(mixed * mixed, axis=-1, keepdims=True) + EPS)
        unit = mixed * inv
        gog_ref[:, lanes] = (back * (unit * head_gain) * sig * (1.0 + og * (1.0 - sig))).astype(BF16)
        incoming = back * (og * sig)
        ghg_ref[...] += jnp.sum(incoming * unit, axis=0, keepdims=True)
        scaled = incoming * head_gain
        gmix_ref[:, lanes] = (inv * (scaled - unit * jnp.mean(scaled * unit, axis=-1, keepdims=True))).astype(BF16)


def unmix(grad, middle, dy, og, mixed, weights, head_gain, gain_two):
    tokens = grad.shape[0]
    return pl.pallas_call(
        unmix_kernel,
        grid=(tokens // TILE,),
        in_specs=[
            rows(TILE, D),
            rows(TILE, D),
            rows(TILE, D),
            rows(TILE, V),
            rows(TILE, V),
            fixed((2, 2, 4, 256, 512)),
            fixed((1, HV)),
            fixed((1, D)),
        ],
        out_specs=[rows(TILE, D), rows(TILE, D), rows(TILE, V), rows(TILE, V), fixed((1, D)), fixed((1, HV))],
        out_shape=[
            struct((tokens, D), F32),
            struct((tokens, D), BF16),
            struct((tokens, V), BF16),
            struct((tokens, V), BF16),
            struct((1, D), F32),
            struct((1, HV), F32),
        ],
        compiler_params=params(56),
        cost_estimate=cost(2 * tokens * D * D, 30 * MIB),
        name="unmix",
    )(grad, middle, dy, og, mixed, weights, head_gain, gain_two)


def weight_grad_kernel(plan, core_ref, *refs):
    count = 2 * len(plan)
    keep_ref, send_ref = refs[-2:]
    lefts, rights = refs[:count], refs[count:-2]
    for j, (lefts_at, groups) in enumerate(plan):
        for start, index, width in groups:
            right = rights[index][...]
            for ref, left in ((keep_ref, lefts[2 * lefts_at]), (send_ref, lefts[2 * lefts_at + 1])):
                part = dot_tn(left[...], right).astype(BF16)
                for x in range(2):
                    ref[x, 0, 0, :, start : start + width] = part[x * 128 : (x + 1) * 128]


def weight_grads(core, lefts, rights, plan):
    tokens = lefts[0].shape[0]
    specs = []
    for left in lefts:
        specs.append(pl.BlockSpec((tokens, 256), lambda r, c, core: (0, r * 2 + core[0])))
        specs.append(pl.BlockSpec((tokens, 256), lambda r, c, core: (0, r * 2 + 1 - core[0])))
    for right in rights:
        specs.append(pl.BlockSpec((tokens, right.shape[1] // 4), lambda r, c, core: (0, c)))
    out = pl.BlockSpec((2, 1, 1, 128, 512), lambda r, c, core: (0, r, c, 0, 0))
    operands = [left for left in lefts for _ in range(2)] + list(rights)
    return pl.pallas_call(
        functools.partial(weight_grad_kernel, plan),
        grid_spec=pltpu.PrefetchScalarGridSpec(
            num_scalar_prefetch=1, grid=(2, 4), in_specs=specs, out_specs=[out, out]
        ),
        out_shape=[struct((2, 2, 4, 128, 512), BF16)] * 2,
        compiler_params=params(40),
        cost_estimate=cost(2 * tokens * D * 2048, 12 * MIB),
        name="weight_grads",
    )(core, *operands)


def unproject_kernel(
    x_ref, n_ref, gq_ref, gk_ref, gv_ref, glog_ref, logit_ref, low_ref, gog_ref, gm_ref,
    w_ref, wo_ref, ddt_ref, du_ref, g1_ref,
    gx_ref, gddt_ref, gdu_ref, gbias_ref, gg1_ref,
):
    @pl.when(pl.program_id(0) == 0)
    def _():
        gddt_ref[...] = jnp.zeros_like(gddt_ref)
        gdu_ref[...] = jnp.zeros_like(gdu_ref)
        gbias_ref[...] = jnp.zeros_like(gbias_ref)
        gg1_ref[...] = jnp.zeros_like(gg1_ref)

    normed = n_ref[...]
    grad_logit = glog_ref[...] * (1.0 / 16.0) * jax.nn.sigmoid(-logit_ref[...])
    gbias_ref[...] += jnp.sum(grad_logit, axis=0, keepdims=True)
    gdu_ref[...] += dot_tn(low_ref[...], grad_logit, HIGH)
    grad_low = dot_nt(grad_logit, du_ref[...], HIGH).astype(BF16)
    gddt_ref[...] += dot_tn(grad_low, normed)
    parts = []
    for r in range(2):
        small = dot(grad_low, ddt_ref[r])
        for core in range(2):
            total = small[:, core * 256 : (core + 1) * 256]
            for c in range(HEADS):
                w = w_ref[core, r, c]
                total = total + dot_nt(gq_ref[:, c * HK : (c + 1) * HK], w[:, :HK])
                total = total + dot_nt(gk_ref[:, c * HK : (c + 1) * HK], w[:, HK : 2 * HK])
                total = total + dot_nt(gv_ref[:, c * HV : (c + 1) * HV], w[:, 2 * HK :])
                total = total + dot_nt(gog_ref[:, c * HV : (c + 1) * HV], wo_ref[core, r, c])
            parts.append(total)
    grad = jnp.concatenate(parts, axis=1)
    x = x_ref[...].astype(F32)
    inverse = lax.rsqrt(jnp.mean(x * x, axis=-1, keepdims=True) + EPS)
    unit = x * inverse
    gg1_ref[...] += jnp.sum(grad * unit, axis=0, keepdims=True)
    scaled = grad * g1_ref[...]
    gx_ref[...] = gm_ref[...] + inverse * (scaled - unit * jnp.mean(scaled * unit, axis=-1, keepdims=True))


def unproject(x, normed, gq, gk, gv, glog, logit, low, gog, gm, weights, out_weights, ddt, du, gain):
    tokens = x.shape[0]
    return pl.pallas_call(
        unproject_kernel,
        grid=(tokens // TILE,),
        in_specs=[
            rows(TILE, D),
            rows(TILE, D),
            rows(TILE, K),
            rows(TILE, K),
            rows(TILE, V),
            rows(TILE, K),
            rows(TILE, K),
            rows(TILE, LOW),
            rows(TILE, V),
            rows(TILE, D),
            fixed((2, 2, 4, 256, 512)),
            fixed((2, 2, 4, 256, HV)),
            fixed((2, LOW, 512)),
            fixed((LOW, K)),
            fixed((1, D)),
        ],
        out_specs=[rows(TILE, D), fixed((LOW, D)), fixed((LOW, K)), fixed((1, K)), fixed((1, D))],
        out_shape=[
            struct((tokens, D), F32),
            struct((LOW, D), F32),
            struct((LOW, K), F32),
            struct((1, K), F32),
            struct((1, D), F32),
        ],
        compiler_params=params(56),
        cost_estimate=cost(2 * tokens * D * 3072, 30 * MIB),
        name="unproject",
    )(x, normed, gq, gk, gv, glog, logit, low, gog, gm, weights, out_weights, ddt, du, gain)


def ring_gather(part, axis, count):
    me = lax.axis_index(axis)
    if count == 2:
        other = lax.ppermute(part, axis, [(0, 1), (1, 0)])
        first = me == 0
        return jnp.stack([jnp.where(first, part, other), jnp.where(first, other, part)])
    whole = jnp.zeros((count,) + part.shape, part.dtype)
    whole = lax.dynamic_update_index_in_dim(whole, part, me, 0)
    moving = part
    for step in range(1, count):
        moving = lax.ppermute(moving, axis, [(i, (i + 1) % count) for i in range(count)])
        whole = lax.dynamic_update_index_in_dim(whole, moving, lax.rem(me + count - step, count), 0)
    return whole


def added(parts):
    total = parts[0].astype(F32)
    for part in parts[1:]:
        total = total + part.astype(F32)
    return total.astype(BF16)


def scatter_add(arrays, axis, count):
    me = lax.axis_index(axis)

    def piece(place):
        return added([lax.dynamic_index_in_dim(array, place, 0, keepdims=False) for array in arrays])

    received = []
    for shift in range(1, count):
        going = piece(lax.rem(me + shift, count))
        received.append(lax.ppermute(going, axis, [(i, (i + shift) % count) for i in range(count)]))
    return [piece(me)] + received


def reduce_pack(keep, send, rows_count, cols_count):
    arrays = [keep, lax.ppermute(send, "core", [(0, 1), (1, 0)])]
    arrays = scatter_add(arrays, "x", 2)
    arrays = scatter_add(arrays, "row", rows_count)
    arrays = scatter_add(arrays, "col", cols_count)
    total = added(arrays)
    return ring_gather(ring_gather(total, "x", 2), "core", 2)


def small_block(ddt, du, bias, g1, hg, g2):
    first = jnp.concatenate([ddt, jnp.pad(du, ((0, 0), (0, 512 - du.shape[1])))], axis=0)
    line = jnp.concatenate([jnp.pad(bias, (0, 64)), g1, jnp.pad(hg, (0, 96)), g2])
    return jnp.concatenate([first, line.reshape(1, 512), jnp.zeros((3, 512), first.dtype)], axis=0)


def per_device(
    layer_input,
    segment_ids,
    norm1_gain,
    query_weight,
    key_weight,
    value_weight,
    outgate_weight,
    decay_down,
    decay_up,
    decay_bias,
    head_gain,
    out_weight,
    norm2_gain,
    swiglu_gate,
    swiglu_up,
    swiglu_down,
    cotangent,
):
    row_count = lax.axis_size("row")
    col_count = lax.axis_size("col")
    fast = row_count == 2 and col_count == 4 and lax.axis_size("x") == 2
    core = lax.axis_index("core")
    quarter = lax.axis_index("x") * 2 + core
    owned = (query_weight, key_weight, value_weight, outgate_weight, out_weight)

    if fast:
        feed_rows = jnp.concatenate(
            [
                jnp.concatenate(
                    [
                        lax.dynamic_slice_in_dim(swiglu_gate.T, quarter * 176, 176, 0),
                        lax.dynamic_slice_in_dim(swiglu_up.T, quarter * 176, 176, 0),
                    ],
                    axis=0,
                ),
                lax.dynamic_slice_in_dim(swiglu_down, quarter * 352, 352, 0),
            ],
            axis=1,
        )
        feed_full = lax.all_gather(feed_rows, AXES, axis=0, tiled=True).reshape(4, 2, 4, 352, 768)

        def gather(part):
            part = ring_gather(ring_gather(part, "col", col_count), "row", row_count)
            return ring_gather(part, "core", 2)

        qkv = jnp.concatenate([query_weight, key_weight, value_weight], axis=1)
        qkv = lax.dynamic_slice_in_dim(qkv, core * 256, 256, 0)
        small = small_block(decay_down.T, decay_up, decay_bias, norm1_gain, head_gain, norm2_gain)
        qkv_full = gather(jnp.concatenate([qkv, small], axis=0))
        ogout = jnp.concatenate([outgate_weight, out_weight], axis=1)
        ogout_full = gather(lax.dynamic_slice_in_dim(ogout, core * 256, 256, 0))
        small = qkv_full[0, :, :, 256:]
        ddt = small[:, :, :4].reshape(2, LOW, 512)
        du = small[:, :, 4:12, :HK].transpose(0, 2, 1, 3).reshape(LOW, K)
        bias = small[:, :, 12, :64].reshape(1, K)
        g1 = small[:, :, 12, 128:256].reshape(1, D)
        hg = small[:, :, 12, 256:288].reshape(1, HV)
        g2 = small[:, :, 12, 384:].reshape(1, D)
    else:

        def whole(shard):
            if shard.ndim == 1:
                return lax.all_gather(shard, ("row", "col"), axis=0, tiled=True)
            wide = lax.all_gather(shard, "col", axis=1, tiled=True)
            return lax.all_gather(wide, "row", axis=0, tiled=True)

        def blocks(full, width):
            return full.reshape(2, 2, 256, 4, width).transpose(1, 0, 3, 2, 4)

        qkv_full = jnp.concatenate(
            [blocks(whole(query_weight), 128), blocks(whole(key_weight), 128), blocks(whole(value_weight), 256)],
            axis=-1,
        )
        ogout_full = jnp.concatenate([blocks(whole(outgate_weight), 256), blocks(whole(out_weight), 256)], axis=-1)
        gate_t, lift_t, down = whole(swiglu_gate).T, whole(swiglu_up).T, whole(swiglu_down)
        feed_gate = gate_t.reshape(4, 4, 176, 2, 512).transpose(1, 3, 0, 2, 4)
        feed_lift = lift_t.reshape(4, 4, 176, 2, 512).transpose(1, 3, 0, 2, 4)
        feed_down = down.reshape(2, 4, 352, 4, 256).transpose(1, 0, 3, 2, 4)
        feed_full = jnp.concatenate([jnp.concatenate([feed_gate, feed_lift], axis=3), feed_down], axis=-1)
        ddt = whole(decay_down).T.reshape(LOW, 2, 512).transpose(1, 0, 2)
        du = whole(decay_up)
        bias = whole(decay_bias).reshape(1, K)
        g1 = whole(norm1_gain).reshape(1, D)
        hg = whole(head_gain).reshape(1, HV)
        g2 = whole(norm2_gain).reshape(1, D)
    du, bias, g1, hg, g2 = (part.astype(F32) for part in (du, bias, g1, hg, g2))

    tokens = layer_input.shape[0]
    seg_c = segment_ids.reshape(tokens, 1)
    seg_r = segment_ids.reshape(tokens // CH, 1, CH)
    core_at = (core if fast else jnp.zeros_like(core)).astype(jnp.int32).reshape(1)

    normed, q, k, v, low, logit = project(layer_input, g1, qkv_full, ddt, du, bias)
    mixed, states = attend(q, k, v, logit, segment_ids, seg_c, seg_r)
    og, gated, middle, normed_two = mix(layer_input, normed, mixed, ogout_full, hg, g2)
    layer_output, grad_normed_two, keep_gl, send_gl, keep_dn, send_dn = feed(
        core_at, normed_two, cotangent, middle, feed_full
    )
    grad_middle, branch, grad_og, grad_mixed, grad_g2, grad_hg = unmix(
        grad_normed_two, middle, cotangent, og, mixed, ogout_full, hg, g2
    )
    keep_oo, send_oo = weight_grads(
        core_at, [normed, gated], [grad_og, branch], ((0, ((0, 0, 256),)), (1, ((256, 1, 256),)))
    )
    gq, gk, gv, glog = attend_back(q, k, v, logit, segment_ids, seg_c, seg_r, states, grad_mixed)
    keep_qkv, send_qkv = weight_grads(
        core_at, [normed], [gq, gk, gv], ((0, ((0, 0, 128), (128, 1, 128), (256, 2, 256))),)
    )
    input_grad, grad_ddt, grad_du, grad_bias, grad_g1 = unproject(
        layer_input, normed, gq, gk, gv, glog, logit, low, grad_og, grad_middle, qkv_full, ogout_full, ddt, du, g1
    )

    tiny = jnp.concatenate(
        [
            grad_ddt,
            jnp.pad(grad_du, ((0, 0), (0, D - K))),
            jnp.concatenate([grad_bias, grad_hg, jnp.zeros((1, D - K - HV), F32)], axis=1),
            grad_g1,
            grad_g2,
            jnp.zeros((5, D), F32),
        ],
        axis=0,
    )
    tiny = lax.psum(tiny, AXES)
    r, c = lax.axis_index("row"), lax.axis_index("col")

    def own(line, size):
        return lax.dynamic_slice_in_dim(line, (r * col_count + c) * size, size, 0)

    def own_block(full, shape):
        return lax.dynamic_slice(full, (r * shape[0], c * shape[1]), shape)

    out_bias = own(tiny[32, :K], decay_bias.shape[0])
    out_hg = own(tiny[32, K : K + HV], head_gain.shape[0])
    out_g1 = own(tiny[33], norm1_gain.shape[0])
    out_g2 = own(tiny[34], norm2_gain.shape[0])
    out_du = own_block(tiny[16:32, :K], decay_up.shape)
    down_rows = decay_down.shape
    out_dd = lax.dynamic_slice(tiny, (c * down_rows[1], r * down_rows[0]), down_rows[::-1]).T

    if fast:
        gl = reduce_pack(keep_gl, send_gl, row_count, col_count)
        dn = reduce_pack(keep_dn, send_dn, row_count, col_count)
        oo = reduce_pack(keep_oo, send_oo, row_count, col_count)
        qkv = reduce_pack(keep_qkv, send_qkv, row_count, col_count)
        gl = gl.reshape(2, 2, 2, 176, 512).transpose(2, 0, 1, 3, 4).reshape(2, HC, 512)
        out_gate, out_lift = gl[0].T, gl[1].T
        out_down = dn.transpose(2, 0, 1, 3, 4).reshape(1408, 256)
        oo = oo.reshape(512, 512)
        qkv = qkv.reshape(512, 512)
        shards = [qkv[:, :128], qkv[:, 128:256], qkv[:, 256:], oo[:, :256], oo[:, 256:], out_gate, out_lift, out_down]
    else:

        def joined(keep, send):
            return jnp.stack([keep, send])

        def matrix(pack):
            return pack.transpose(2, 0, 1, 4, 3, 5).reshape(D, -1)

        oo = joined(keep_oo, send_oo)
        qkv = joined(keep_qkv, send_qkv)
        gl = joined(keep_gl, send_gl).reshape(2, 2, 2, 4, 2, 176, 512).transpose(4, 3, 0, 1, 5, 2, 6)
        gl = gl.reshape(2, FF, D)
        dn = joined(keep_dn, send_dn).transpose(2, 4, 0, 1, 5, 3, 6).reshape(FF, D)
        fulls = [
            matrix(qkv[..., :128]),
            matrix(qkv[..., 128:256]),
            matrix(qkv[..., 256:]),
            matrix(oo[..., :256]),
            matrix(oo[..., 256:]),
            gl[0].T,
            gl[1].T,
            dn,
        ]
        shards = []
        for full in fulls:
            part = lax.psum(full, ("x", "core"))
            part = lax.psum_scatter(part, "row", scatter_dimension=0, tiled=True)
            shards.append(lax.psum_scatter(part, "col", scatter_dimension=1, tiled=True))
    out_q, out_k, out_v, out_og, out_out, out_gate, out_lift, out_down = (part.astype(F32) for part in shards)
    return (
        layer_output,
        input_grad,
        out_g1,
        out_q,
        out_k,
        out_v,
        out_og,
        out_dd,
        out_du,
        out_bias,
        out_hg,
        out_out,
        out_g2,
        out_gate,
        out_lift,
        out_down,
    )


def solution(mesh):
    shape = dict(mesh.shape)
    finer = Mesh(mesh.devices.reshape(shape["dp"] // 2, 2, shape["row"], shape["col"]), AXES)
    tokens = P(AXES, None)
    vector = P(("row", "col"))
    matrix = P("row", "col")
    in_specs = (
        tokens, tokens, vector, matrix, matrix, matrix, matrix, matrix, matrix, vector, vector,
        matrix, vector, matrix, matrix, matrix, tokens,
    )
    out_specs = (
        tokens, tokens, vector, matrix, matrix, matrix, matrix, matrix, matrix, vector, vector,
        matrix, vector, matrix, matrix, matrix,
    )
    return jax.shard_map(per_device, mesh=finer, in_specs=in_specs, out_specs=out_specs, check_vma=False)
```

```python
import functools

import jax
import jax.numpy as jnp
from jax import lax
from jax.experimental import pallas as pl
from jax.experimental.pallas import tpu as pltpu
from jax.sharding import Mesh
from jax.sharding import PartitionSpec as P

HEADS = 4
HK = 128
HV = 256
CH = 64
LOW = 16
D = 1024
K = HEADS * HK
V = HEADS * HV
FF = 2816
HC = FF // 4
TILE = 256
FEED_TILE = 1024

EPS = 1e-05
HIGH = lax.Precision.HIGHEST
F32 = jnp.float32
BF16 = jnp.bfloat16
AXES = ("x", "core", "row", "col")
MIB = 1024 * 1024


def dot(left, right, precision=None):
    return jnp.dot(left, right, preferred_element_type=F32, precision=precision)


def dot_nt(left, right, precision=None):
    return lax.dot_general(
        left, right, (((1,), (1,)), ((), ())), preferred_element_type=F32, precision=precision
    )


def dot_tn(left, right, precision=None):
    return lax.dot_general(
        left, right, (((0,), (0,)), ((), ())), preferred_element_type=F32, precision=precision
    )


def struct(shape, dtype):
    return jax.ShapeDtypeStruct(shape, dtype)


def fixed(shape):
    return pl.BlockSpec(shape, lambda *i: (0,) * len(shape))


def rows(height, width):
    return pl.BlockSpec((height, width), lambda i: (i, 0))


def cost(flops, moved, trans=0):
    return pl.CostEstimate(flops=int(flops), bytes_accessed=int(moved), transcendentals=int(trans))


def params(mib):
    return pltpu.CompilerParams(vmem_limit_bytes=mib * MIB)


def project_kernel(x_ref, gain_ref, w_ref, ddt_ref, du_ref, bias_ref, n_ref, q_ref, k_ref, v_ref, low_ref, logit_ref):
    x = x_ref[...].astype(F32)
    inverse = lax.rsqrt(jnp.mean(x * x, axis=-1, keepdims=True) + EPS)
    normed = (x * inverse * gain_ref[...]).astype(BF16)
    n_ref[...] = normed
    for c in range(HEADS):
        total = None
        for r in range(2):
            for core in range(2):
                at = r * 512 + core * 256
                part = dot(normed[:, at : at + 256], w_ref[core, r, c])
                total = part if total is None else total + part
        q_ref[:, c * HK : (c + 1) * HK] = total[:, :HK].astype(BF16)
        k_ref[:, c * HK : (c + 1) * HK] = total[:, HK : 2 * HK].astype(BF16)
        v_ref[:, c * HV : (c + 1) * HV] = total[:, 2 * HK :].astype(BF16)
    low = dot_nt(normed[:, :512], ddt_ref[0]) + dot_nt(normed[:, 512:], ddt_ref[1])
    low_ref[...] = low
    logit_ref[...] = dot(low, du_ref[...], HIGH) + bias_ref[...]


def project(x, gain, weights, ddt, du, bias):
    tokens = x.shape[0]
    return pl.pallas_call(
        project_kernel,
        grid=(tokens // TILE,),
        in_specs=[
            rows(TILE, D),
            fixed((1, D)),
            fixed((2, 2, 4, 256, 512)),
            fixed((2, LOW, 512)),
            fixed((LOW, K)),
            fixed((1, K)),
        ],
        out_specs=[rows(TILE, D), rows(TILE, K), rows(TILE, K), rows(TILE, V), rows(TILE, LOW), rows(TILE, K)],
        out_shape=[
            struct((tokens, D), BF16),
            struct((tokens, K), BF16),
            struct((tokens, K), BF16),
            struct((tokens, V), BF16),
            struct((tokens, LOW), F32),
            struct((tokens, K), F32),
        ],
        compiler_params=params(40),
        cost_estimate=cost(2 * tokens * D * 2048, 14 * MIB),
        name="project",
    )(x, gain, weights, ddt, du, bias)


def span_parts(logit, doc_c, doc_r, last_doc, prev_doc):
    lower = lax.broadcasted_iota(jnp.int32, (CH, CH), 0) >= lax.broadcasted_iota(jnp.int32, (CH, CH), 1)
    mask = jnp.where(lower & (doc_c == doc_r), HK ** (-0.5), 0.0)
    log_decay = (jnp.minimum(logit, 0.0) - jnp.log1p(jnp.exp(-jnp.abs(logit)))) * (1.0 / 16.0)
    cumul = dot(lower.astype(F32), log_decay, HIGH)
    centre = cumul[CH // 2 - 1 : CH // 2]
    last = cumul[CH - 1 :]
    rise = jnp.exp(cumul - centre)
    fall = jnp.exp(centre - cumul)
    growth = jnp.exp(cumul)
    to_end = jnp.exp(last - cumul)
    enter = jnp.where(doc_c == prev_doc, HK ** (-0.5), 0.0)
    same = jnp.where(doc_c == last_doc, 1.0, 0.0)
    return mask, rise, fall, growth, to_end, enter, same, jnp.exp(last)


def span_docs(seg_ref, at, first):
    last_doc = seg_ref[at + CH - 1]
    prev_doc = jnp.where(first, -1, seg_ref[jnp.maximum(at - 1, 0)])
    return last_doc, prev_doc


def attend_kernel(spans, seg_ref, q_ref, k_ref, v_ref, logit_ref, dc_ref, dr_ref, mixed_ref, states_ref, state):
    i = pl.program_id(1)
    at = (pl.program_id(0) * spans + i) * CH
    last_doc, prev_doc = span_docs(seg_ref, at, i == 0)

    @pl.when(i == 0)
    def _():
        state[...] = jnp.zeros_like(state)

    mask, rise, fall, growth, to_end, enter, same, keep = span_parts(
        logit_ref[...], dc_ref[...], dr_ref[0], last_doc, prev_doc
    )
    query = q_ref[...].astype(F32)
    keys = k_ref[...].astype(F32)
    qs = (query * rise).astype(BF16)
    ks = (keys * fall).astype(BF16)
    qg = (query * growth * enter).astype(BF16)
    kw = (keys * to_end * same).astype(BF16)
    keep = keep * jnp.where(last_doc == prev_doc, 1.0, 0.0)
    for h in range(HEADS):
        a, b = h * HK, (h + 1) * HK
        va = v_ref[:, h * HV : (h + 1) * HV]
        now = state[h]
        low = now.astype(BF16)
        states_ref[0, h] = low
        scores = (dot_nt(qs[:, a:b], ks[:, a:b]) * mask).astype(BF16)
        mixed_ref[:, h * HV : (h + 1) * HV] = dot(scores, va) + dot_nt(qg[:, a:b], low)
        state[h] = now * keep[:, a:b] + dot_tn(va, kw[:, a:b])


def attend(q, k, v, logit, segs, seg_c, seg_r):
    tokens = q.shape[0]
    seqs = segs.shape[0]
    spans = tokens // seqs // CH

    def part(width):
        return pl.BlockSpec((CH, width), lambda s, i, seg: (s * spans + i, 0))

    return pl.pallas_call(
        functools.partial(attend_kernel, spans),
        grid_spec=pltpu.PrefetchScalarGridSpec(
            num_scalar_prefetch=1,
            grid=(seqs, spans),
            in_specs=[
                part(K),
                part(K),
                part(V),
                part(K),
                part(1),
                pl.BlockSpec((1, 1, CH), lambda s, i, seg: (s * spans + i, 0, 0)),
            ],
            out_specs=[
                part(V),
                pl.BlockSpec((1, HEADS, HV, HK), lambda s, i, seg: (s * spans + i, 0, 0, 0)),
            ],
            scratch_shapes=[pltpu.VMEM((HEADS, HV, HK), F32)],
        ),
        out_shape=[struct((tokens, V), F32), struct((seqs * spans, HEADS, HV, HK), BF16)],
        compiler_params=params(32),
        cost_estimate=cost(2e10, 16 * MIB),
        name="attend",
    )(segs.reshape(-1), q, k, v, logit, seg_c, seg_r)


def attend_back_kernel(
    spans, seg_ref, q_ref, k_ref, v_ref, logit_ref, dc_ref, dr_ref, states_ref, g_ref,
    gq_ref, gk_ref, gv_ref, gl_ref, grad_state,
):
    i = spans - 1 - pl.program_id(1)
    at = (pl.program_id(0) * spans + i) * CH
    last_doc, prev_doc = span_docs(seg_ref, at, i == 0)

    @pl.when(pl.program_id(1) == 0)
    def _():
        grad_state[...] = jnp.zeros_like(grad_state)

    mask, rise, fall, growth, to_end, enter, same, keep = span_parts(
        logit_ref[...], dc_ref[...], dr_ref[0], last_doc, prev_doc
    )
    query = q_ref[...].astype(F32)
    keys = k_ref[...].astype(F32)
    qs = (query * rise).astype(BF16)
    ks = (keys * fall).astype(BF16)
    qg = (query * growth * enter).astype(BF16)
    kw = (keys * to_end * same).astype(BF16)
    keep = keep * jnp.where(last_doc == prev_doc, 1.0, 0.0)
    last_row = lax.broadcasted_iota(jnp.int32, (CH, HK), 0) == CH - 1
    upper = lax.broadcasted_iota(jnp.int32, (CH, CH), 0) <= lax.broadcasted_iota(jnp.int32, (CH, CH), 1)
    upper = upper.astype(F32)
    for h in range(HEADS):
        a, b = h * HK, (h + 1) * HK
        va = v_ref[:, h * HV : (h + 1) * HV]
        ga = g_ref[:, h * HV : (h + 1) * HV]
        qh, kh = qs[:, a:b], ks[:, a:b]
        state = states_ref[0, h]
        grad = grad_state[h]
        grad_low = grad.astype(BF16)
        scores = (dot_nt(qh, kh) * mask).astype(BF16)
        grad_scores = (dot_nt(ga, va) * mask).astype(BF16)
        gv_ref[:, h * HV : (h + 1) * HV] = (dot_tn(scores, ga) + dot_nt(kw[:, a:b], grad_low)).astype(BF16)
        wk = dot(va, grad_low) * same * to_end[:, a:b]
        wq = dot(ga, state) * enter * growth[:, a:b]
        query_inner = dot(grad_scores, kh)
        key_inner = dot_tn(grad_scores, qh)
        gq_ref[:, a:b] = (query_inner * rise[:, a:b] + wq).astype(BF16)
        gk_ref[:, a:b] = (key_inner * fall[:, a:b] + wk).astype(BF16)
        ends = wk * keys[:, a:b]
        grad_cumul = qh.astype(F32) * query_inner - kh.astype(F32) * key_inner + query[:, a:b] * wq - ends
        kept = grad * keep[:, a:b]
        at_last = jnp.sum(ends, axis=0, keepdims=True) + jnp.sum(kept * state.astype(F32), axis=0, keepdims=True)
        grad_cumul = grad_cumul + jnp.where(last_row, at_last, 0.0)
        gl_ref[:, a:b] = dot(upper, grad_cumul, HIGH)
        grad_state[h] = kept + dot_tn(ga, qg[:, a:b])


def attend_back(q, k, v, logit, segs, seg_c, seg_r, states, grad):
    tokens = q.shape[0]
    seqs = segs.shape[0]
    spans = tokens // seqs // CH

    def part(width):
        return pl.BlockSpec((CH, width), lambda s, i, seg: (s * spans + spans - 1 - i, 0))

    return pl.pallas_call(
        functools.partial(attend_back_kernel, spans),
        grid_spec=pltpu.PrefetchScalarGridSpec(
            num_scalar_prefetch=1,
            grid=(seqs, spans),
            in_specs=[
                part(K),
                part(K),
                part(V),
                part(K),
                part(1),
                pl.BlockSpec((1, 1, CH), lambda s, i, seg: (s * spans + spans - 1 - i, 0, 0)),
                pl.BlockSpec((1, HEADS, HV, HK), lambda s, i, seg: (s * spans + spans - 1 - i, 0, 0, 0)),
                part(V),
            ],
            out_specs=[part(K), part(K), part(V), part(K)],
            scratch_shapes=[pltpu.VMEM((HEADS, HV, HK), F32)],
        ),
        out_shape=[
            struct((tokens, K), BF16),
            struct((tokens, K), BF16),
            struct((tokens, V), BF16),
            struct((tokens, K), F32),
        ],
        compiler_params=params(32),
        cost_estimate=cost(1, 1),
        name="attend_back",
    )(segs.reshape(-1), q, k, v, logit, seg_c, seg_r, states, grad)


def mix_kernel(x_ref, n_ref, mixed_ref, w_ref, hg_ref, g2_ref, og_ref, gated_ref, middle_ref, n2_ref):
    normed = n_ref[...]
    outs = [None] * 4
    for c in range(HEADS):
        og = None
        for r in range(2):
            for core in range(2):
                at = r * 512 + core * 256
                part = dot(normed[:, at : at + 256], w_ref[core, r, c, :, :HV])
                og = part if og is None else og + part
        og_ref[:, c * HV : (c + 1) * HV] = og
        mixed = mixed_ref[:, c * HV : (c + 1) * HV]
        inverse = lax.rsqrt(jnp.mean(mixed * mixed, axis=-1, keepdims=True) + EPS)
        gated = (mixed * inverse * hg_ref[...] * (og * jax.nn.sigmoid(og))).astype(BF16)
        gated_ref[:, c * HV : (c + 1) * HV] = gated
        for e in range(4):
            part = dot(gated, w_ref[c % 2, c // 2, e, :, HV:])
            outs[e] = part if outs[e] is None else outs[e] + part
    middle = x_ref[...].astype(F32) + jnp.concatenate(outs, axis=1)
    middle_ref[...] = middle
    inverse = lax.rsqrt(jnp.mean(middle * middle, axis=-1, keepdims=True) + EPS)
    n2_ref[...] = (middle * inverse * g2_ref[...]).astype(BF16)


def mix(x, normed, mixed, weights, head_gain, gain_two):
    tokens = x.shape[0]
    return pl.pallas_call(
        mix_kernel,
        grid=(tokens // TILE,),
        in_specs=[
            rows(TILE, D),
            rows(TILE, D),
            rows(TILE, V),
            fixed((2, 2, 4, 256, 512)),
            fixed((1, HV)),
            fixed((1, D)),
        ],
        out_specs=[rows(TILE, V), rows(TILE, V), rows(TILE, D), rows(TILE, D)],
        out_shape=[
            struct((tokens, V), F32),
            struct((tokens, V), BF16),
            struct((tokens, D), F32),
            struct((tokens, D), BF16),
        ],
        compiler_params=params(48),
        cost_estimate=cost(2 * tokens * D * 2048, 24 * MIB),
        name="mix",
    )(x, normed, mixed, weights, head_gain, gain_two)


def feed_kernel(
    core_ref, n2_ref, dy_ref, middle_ref, gl_ref, dn_ref,
    out_ref, gn_ref, keep_gl, send_gl, keep_dn, send_dn, y_acc, hid, gate_g, lift_g,
):
    step = pl.program_id(0)

    @pl.when(step == 0)
    def _():
        y_acc[...] = middle_ref[...]
        gn_ref[...] = jnp.zeros_like(gn_ref)

    @pl.loop(0, n2_ref.shape[0] // FEED_TILE)
    def _(t):
        at = pl.ds(pl.multiple_of(t * FEED_TILE, FEED_TILE), FEED_TILE)
        gate = lift = back = None
        for r in range(2):
            n2 = n2_ref[at, r * 512 : (r + 1) * 512]
            a = dot_nt(n2, gl_ref[:, r, 0, :176].reshape(HC, 512))
            b = dot_nt(n2, gl_ref[:, r, 0, 176:].reshape(HC, 512))
            gate = a if r == 0 else gate + a
            lift = b if r == 0 else lift + b
        for c in range(4):
            a = dot_nt(dy_ref[at, c * 256 : (c + 1) * 256], dn_ref[:, 0, c].reshape(HC, 256))
            back = a if c == 0 else back + a
        sig = jax.nn.sigmoid(gate)
        swish = gate * sig
        hidden = (swish * lift).astype(BF16)
        grad_lift = (back * swish).astype(BF16)
        grad_gate = (back * lift * sig * (1.0 + gate * (1.0 - sig))).astype(BF16)
        hid[at, :] = hidden
        gate_g[at, :] = grad_gate
        lift_g[at, :] = grad_lift
        for c in range(4):
            lanes = slice(c * 256, (c + 1) * 256)
            y_acc[at, lanes] += dot(hidden, dn_ref[:, 0, c].reshape(HC, 256))
        for r in range(2):
            lanes = slice(r * 512, (r + 1) * 512)
            gn_ref[at, lanes] += dot(grad_gate, gl_ref[:, r, 0, :176].reshape(HC, 512)) + dot(
                grad_lift, gl_ref[:, r, 0, 176:].reshape(HC, 512)
            )

    @pl.when(step == 3)
    def _():
        out_ref[...] = y_acc[...].astype(BF16)

    first = core_ref[0] == 0
    for m, (source, right) in enumerate(((gate_g, n2_ref), (lift_g, n2_ref), (hid, dy_ref))):
        both = dot_tn(source[...], right[...]).astype(BF16)
        low, high = both[: HC // 2], both[HC // 2 :]
        mine = jnp.where(first, low, high)
        other = jnp.where(first, high, low)
        for part, gl_out, dn_out in ((mine, keep_gl, keep_dn), (other, send_gl, send_dn)):
            for x in range(2):
                piece = part[x * 176 : (x + 1) * 176]
                if m < 2:
                    for r in range(2):
                        gl_out[x, r, 0, m * 176 : (m + 1) * 176] = piece[:, r * 512 : (r + 1) * 512]
                else:
                    for c in range(4):
                        dn_out[x, 0, c, 0] = piece[:, c * 256 : (c + 1) * 256]


def feed(core, n2, dy, middle, weights):
    tokens = n2.shape[0]
    gl = pl.BlockSpec((2, 2, 1, 352, 512), lambda i, c: (0, 0, i, 0, 0))
    dn = pl.BlockSpec((2, 1, 4, 1, 176, 256), lambda i, c: (0, i // 2, 0, i % 2, 0, 0))
    once = pl.Buffered(1)
    return pl.pallas_call(
        feed_kernel,
        grid_spec=pltpu.PrefetchScalarGridSpec(
            num_scalar_prefetch=1,
            grid=(4,),
            in_specs=[
                pl.BlockSpec((tokens, D), lambda i, c: (0, 0), pipeline_mode=once),
                pl.BlockSpec((tokens, D), lambda i, c: (0, 0), pipeline_mode=once),
                pl.BlockSpec((tokens, D), lambda i, c: (0, 0), pipeline_mode=once),
                pl.BlockSpec((4, 2, 1, 352, 512), lambda i, c: (0, 0, i, 0, 0)),
                pl.BlockSpec((2, 1, 4, 352, 256), lambda i, c: (i % 2, i // 2, 0, 0, 2)),
            ],
            out_specs=[
                pl.BlockSpec((tokens, D), lambda i, c: (0, 0), pipeline_mode=once),
                pl.BlockSpec((tokens, D), lambda i, c: (0, 0), pipeline_mode=once),
                gl,
                gl,
                dn,
                dn,
            ],
            scratch_shapes=[
                pltpu.VMEM((tokens, D), F32),
                pltpu.VMEM((tokens, HC), BF16),
                pltpu.VMEM((tokens, HC), BF16),
                pltpu.VMEM((tokens, HC), BF16),
            ],
        ),
        out_shape=[
            struct((tokens, D), BF16),
            struct((tokens, D), F32),
            struct((2, 2, 4, 352, 512), BF16),
            struct((2, 2, 4, 352, 512), BF16),
            struct((2, 2, 4, 2, 176, 256), BF16),
            struct((2, 2, 4, 2, 176, 256), BF16),
        ],
        compiler_params=params(60),
        cost_estimate=cost(18 * tokens * D * FF, 60 * MIB),
        name="feed",
    )(core, n2, dy, middle, weights, weights)


def unmix_kernel(
    gn_ref, middle_ref, dy_ref, og_ref, mixed_ref, w_ref, hg_ref, g2_ref,
    gm_ref, gb_ref, gog_ref, gmix_ref, gg2_ref, ghg_ref,
):
    @pl.when(pl.program_id(0) == 0)
    def _():
        gg2_ref[...] = jnp.zeros_like(gg2_ref)
        ghg_ref[...] = jnp.zeros_like(ghg_ref)

    grad = gn_ref[...]
    middle = middle_ref[...]
    inverse = lax.rsqrt(jnp.mean(middle * middle, axis=-1, keepdims=True) + EPS)
    unit = middle * inverse
    gg2_ref[...] += jnp.sum(grad * unit, axis=0, keepdims=True)
    scaled = grad * g2_ref[...]
    grad_middle = dy_ref[...].astype(F32) + inverse * (scaled - unit * jnp.mean(scaled * unit, axis=-1, keepdims=True))
    gm_ref[...] = grad_middle
    branch = grad_middle.astype(BF16)
    gb_ref[...] = branch
    head_gain = hg_ref[...]
    for c in range(HEADS):
        lanes = slice(c * HV, (c + 1) * HV)
        back = None
        for e in range(4):
            part = dot_nt(branch[:, e * 256 : (e + 1) * 256], w_ref[c % 2, c // 2, e, :, HV:])
            back = part if back is None else back + part
        og = og_ref[:, lanes]
        sig = jax.nn.sigmoid(og)
        mixed = mixed_ref[:, lanes]
        inv = lax.rsqrt(jnp.mean(mixed * mixed, axis=-1, keepdims=True) + EPS)
        unit = mixed * inv
        gog_ref[:, lanes] = (back * (unit * head_gain) * sig * (1.0 + og * (1.0 - sig))).astype(BF16)
        incoming = back * (og * sig)
        ghg_ref[...] += jnp.sum(incoming * unit, axis=0, keepdims=True)
        scaled = incoming * head_gain
        gmix_ref[:, lanes] = (inv * (scaled - unit * jnp.mean(scaled * unit, axis=-1, keepdims=True))).astype(BF16)


def unmix(grad, middle, dy, og, mixed, weights, head_gain, gain_two):
    tokens = grad.shape[0]
    return pl.pallas_call(
        unmix_kernel,
        grid=(tokens // TILE,),
        in_specs=[
            rows(TILE, D),
            rows(TILE, D),
            rows(TILE, D),
            rows(TILE, V),
            rows(TILE, V),
            fixed((2, 2, 4, 256, 512)),
            fixed((1, HV)),
            fixed((1, D)),
        ],
        out_specs=[rows(TILE, D), rows(TILE, D), rows(TILE, V), rows(TILE, V), fixed((1, D)), fixed((1, HV))],
        out_shape=[
            struct((tokens, D), F32),
            struct((tokens, D), BF16),
            struct((tokens, V), BF16),
            struct((tokens, V), BF16),
            struct((1, D), F32),
            struct((1, HV), F32),
        ],
        compiler_params=params(56),
        cost_estimate=cost(2 * tokens * D * D, 30 * MIB),
        name="unmix",
    )(grad, middle, dy, og, mixed, weights, head_gain, gain_two)


def weight_grad_kernel(plan, row_first, core_ref, *refs):
    count = 2 * len(plan)
    keep_ref, send_ref = refs[-2:]
    lefts, rights = refs[:count], refs[count:-2]
    for j, (lefts_at, groups) in enumerate(plan):
        for start, index, width in groups:
            right = rights[index][...]
            for ref, left in ((keep_ref, lefts[2 * lefts_at]), (send_ref, lefts[2 * lefts_at + 1])):
                part = dot_tn(left[...], right).astype(BF16)
                for x in range(2):
                    at = (0, x, 0) if row_first else (x, 0, 0)
                    ref[(*at, slice(None), slice(start, start + width))] = part[x * 128 : (x + 1) * 128]


def weight_grads(core, lefts, rights, plan, row_first=False):
    tokens = lefts[0].shape[0]
    specs = []
    for left in lefts:
        specs.append(pl.BlockSpec((tokens, 256), lambda r, c, core: (0, r * 2 + core[0])))
        specs.append(pl.BlockSpec((tokens, 256), lambda r, c, core: (0, r * 2 + 1 - core[0])))
    for right in rights:
        specs.append(pl.BlockSpec((tokens, right.shape[1] // 4), lambda r, c, core: (0, c)))
    if row_first:
        out = pl.BlockSpec((1, 2, 1, 128, 512), lambda r, c, core: (r, 0, c, 0, 0))
    else:
        out = pl.BlockSpec((2, 1, 1, 128, 512), lambda r, c, core: (0, r, c, 0, 0))
    operands = [left for left in lefts for _ in range(2)] + list(rights)
    return pl.pallas_call(
        functools.partial(weight_grad_kernel, plan, row_first),
        grid_spec=pltpu.PrefetchScalarGridSpec(
            num_scalar_prefetch=1, grid=(2, 4), in_specs=specs, out_specs=[out, out]
        ),
        out_shape=[struct((2, 2, 4, 128, 512), BF16)] * 2,
        compiler_params=params(40),
        cost_estimate=cost(1, 1),
        name="weight_grads",
    )(core, *operands)


def unproject_kernel(
    x_ref, n_ref, gq_ref, gk_ref, gv_ref, glog_ref, logit_ref, low_ref, gog_ref, gm_ref,
    w_ref, wo_ref, ddt_ref, du_ref, g1_ref,
    gx_ref, gddt_ref, gdu_ref, gbias_ref, gg1_ref,
):
    @pl.when(pl.program_id(0) == 0)
    def _():
        gddt_ref[...] = jnp.zeros_like(gddt_ref)
        gdu_ref[...] = jnp.zeros_like(gdu_ref)
        gbias_ref[...] = jnp.zeros_like(gbias_ref)
        gg1_ref[...] = jnp.zeros_like(gg1_ref)

    normed = n_ref[...]
    grad_logit = glog_ref[...] * (1.0 / 16.0) * jax.nn.sigmoid(-logit_ref[...])
    gbias_ref[...] += jnp.sum(grad_logit, axis=0, keepdims=True)
    gdu_ref[...] += dot_tn(low_ref[...], grad_logit, HIGH)
    grad_low = dot_nt(grad_logit, du_ref[...], HIGH).astype(BF16)
    gddt_ref[...] += dot_tn(grad_low, normed)
    parts = []
    for r in range(2):
        small = dot(grad_low, ddt_ref[r])
        for core in range(2):
            total = small[:, core * 256 : (core + 1) * 256]
            for c in range(HEADS):
                w = w_ref[core, r, c]
                total = total + dot_nt(gq_ref[:, c * HK : (c + 1) * HK], w[:, :HK])
                total = total + dot_nt(gk_ref[:, c * HK : (c + 1) * HK], w[:, HK : 2 * HK])
                total = total + dot_nt(gv_ref[:, c * HV : (c + 1) * HV], w[:, 2 * HK :])
                total = total + dot_nt(gog_ref[:, c * HV : (c + 1) * HV], wo_ref[core, r, c])
            parts.append(total)
    grad = jnp.concatenate(parts, axis=1)
    x = x_ref[...].astype(F32)
    inverse = lax.rsqrt(jnp.mean(x * x, axis=-1, keepdims=True) + EPS)
    unit = x * inverse
    gg1_ref[...] += jnp.sum(grad * unit, axis=0, keepdims=True)
    scaled = grad * g1_ref[...]
    gx_ref[...] = gm_ref[...] + inverse * (scaled - unit * jnp.mean(scaled * unit, axis=-1, keepdims=True))


def unproject(x, normed, gq, gk, gv, glog, logit, low, gog, gm, weights, out_weights, ddt, du, gain):
    tokens = x.shape[0]
    return pl.pallas_call(
        unproject_kernel,
        grid=(tokens // TILE,),
        in_specs=[
            rows(TILE, D),
            rows(TILE, D),
            rows(TILE, K),
            rows(TILE, K),
            rows(TILE, V),
            rows(TILE, K),
            rows(TILE, K),
            rows(TILE, LOW),
            rows(TILE, V),
            rows(TILE, D),
            fixed((2, 2, 4, 256, 512)),
            fixed((2, 2, 4, 256, HV)),
            fixed((2, LOW, 512)),
            fixed((LOW, K)),
            fixed((1, D)),
        ],
        out_specs=[rows(TILE, D), fixed((LOW, D)), fixed((LOW, K)), fixed((1, K)), fixed((1, D))],
        out_shape=[
            struct((tokens, D), F32),
            struct((LOW, D), F32),
            struct((LOW, K), F32),
            struct((1, K), F32),
            struct((1, D), F32),
        ],
        compiler_params=params(56),
        cost_estimate=cost(2 * tokens * D * 3072, 100 * MIB),
        name="unproject",
    )(x, normed, gq, gk, gv, glog, logit, low, gog, gm, weights, out_weights, ddt, du, gain)


def fold_kernel(place_ref, keep_gl, got_gl, keep_dn, got_dn, go_g, st_g, go_l, st_l, *downs):
    i = pl.program_id(0)
    x_at, row_at = place_ref[0], place_ref[1]

    def both(left, right):
        return (left.astype(F32) + right.astype(F32)).astype(BF16)

    for r in range(2):
        for ref, x in ((go_g, 1 - x_at), (st_g, x_at)):
            ref[0, r] = both(keep_gl[x, r, 0, :176], got_gl[x, r, 0, :176])
    for x in range(2):
        for ref, r in ((go_l, 1 - row_at), (st_l, row_at)):
            ref[0, x] = both(keep_gl[x, r, 0, 176:], got_gl[x, r, 0, 176:])
    for shift in range(4):

        @pl.when(i == shift)
        def _():
            downs[shift][...] = both(keep_dn[:, :, 0], got_dn[:, :, 0])


def fold(place, keep_gl, got_gl, keep_dn, got_dn):
    gl = pl.BlockSpec((2, 2, 1, 352, 512), lambda i, p: (0, 0, i, 0, 0))
    dn = pl.BlockSpec((2, 2, 1, 2, 176, 256), lambda i, p: (0, 0, lax.rem(p[2] + i, 4), 0, 0, 0))
    out = pl.BlockSpec((1, 2, 176, 512), lambda i, p: (i, 0, 0, 0))
    down = pl.BlockSpec((2, 2, 2, 176, 256), lambda i, p: (0, 0, 0, 0, 0))
    return pl.pallas_call(
        fold_kernel,
        grid_spec=pltpu.PrefetchScalarGridSpec(
            num_scalar_prefetch=1,
            grid=(4,),
            in_specs=[gl, gl, dn, dn],
            out_specs=[out] * 4 + [down] * 4,
        ),
        out_shape=[struct((4, 2, 176, 512), BF16)] * 4 + [struct((2, 2, 2, 176, 256), BF16)] * 4,
        compiler_params=params(48),
        cost_estimate=cost(1, 26 * MIB),
        name="fold",
    )(place, keep_gl, got_gl, keep_dn, got_dn)


def placed(parts, axis):
    me, count = lax.axis_index(axis), len(parts)
    whole = jnp.zeros((count,) + parts[0].shape, parts[0].dtype)
    for shift, part in enumerate(parts):
        whole = lax.dynamic_update_index_in_dim(whole, part, lax.rem(me + count - shift, count), 0)
    return whole


def ring_gather(part, axis, count):
    parts = [part]
    for _ in range(1, count):
        parts.append(lax.ppermute(parts[-1], axis, [(i, (i + 1) % count) for i in range(count)]))
    return placed(parts, axis)


def added(parts):
    total = parts[0].astype(F32)
    for part in parts[1:]:
        total = total + part.astype(F32)
    return total.astype(BF16)


def tied(*groups):
    flat, tree = jax.tree.flatten(groups)
    return jax.tree.unflatten(tree, lax.optimization_barrier(flat))


def swap(part, axis, bit=1):
    return lax.ppermute(part, axis, [(i, i ^ bit) for i in range(lax.axis_size(axis))])


def piece_of(arrays, place, dim):
    return added([lax.dynamic_index_in_dim(array, place, dim, keepdims=False) for array in arrays])


def going(arrays, axis, dim):
    me, count = lax.axis_index(axis), lax.axis_size(axis)
    return [piece_of(arrays, lax.rem(me + shift, count), dim) for shift in range(1, count)]


def send(pieces, axis):
    count = lax.axis_size(axis)
    return [
        lax.ppermute(piece, axis, [(i, (i + shift) % count) for i in range(count)])
        for shift, piece in enumerate(pieces, 1)
    ]


def staying(arrays, axis, dim):
    return piece_of(arrays, lax.axis_index(axis), dim)


def share(part):
    return ring_gather(ring_gather(part, "x", 2), "core", 2)


def small_block(ddt, du, bias, g1, hg, g2):
    first = jnp.concatenate([ddt, jnp.pad(du, ((0, 0), (0, 512 - du.shape[1])))], axis=0)
    line = jnp.concatenate([jnp.pad(bias, (0, 64)), g1, jnp.pad(hg, (0, 96)), g2])
    return jnp.concatenate([first, line.reshape(1, 512), jnp.zeros((3, 512), first.dtype)], axis=0)


def per_device(
    layer_input,
    segment_ids,
    norm1_gain,
    query_weight,
    key_weight,
    value_weight,
    outgate_weight,
    decay_down,
    decay_up,
    decay_bias,
    head_gain,
    out_weight,
    norm2_gain,
    swiglu_gate,
    swiglu_up,
    swiglu_down,
    cotangent,
):
    row_count = lax.axis_size("row")
    col_count = lax.axis_size("col")
    fast = row_count == 2 and col_count == 4 and lax.axis_size("x") == 2
    core = lax.axis_index("core")
    quarter = lax.axis_index("x") * 2 + core

    if fast:
        feed_rows = jnp.concatenate(
            [
                jnp.concatenate(
                    [
                        lax.dynamic_slice_in_dim(swiglu_gate.T, quarter * 176, 176, 0),
                        lax.dynamic_slice_in_dim(swiglu_up.T, quarter * 176, 176, 0),
                    ],
                    axis=0,
                ),
                lax.dynamic_slice_in_dim(swiglu_down, quarter * 352, 352, 0),
            ],
            axis=1,
        )
        feed_full = lax.all_gather(feed_rows, AXES, axis=0, tiled=True).reshape(4, 2, 4, 352, 768)

        qkv = jnp.concatenate([query_weight, key_weight, value_weight], axis=1)
        qkv = lax.dynamic_slice_in_dim(qkv, core * 256, 256, 0)
        small = small_block(decay_down.T, decay_up, decay_bias, norm1_gain, head_gain, norm2_gain)
        by_col = ring_gather(jnp.concatenate([qkv, small], axis=0), "col", col_count)
        ogout = jnp.concatenate([outgate_weight, out_weight], axis=1)
        ogout = lax.dynamic_slice_in_dim(ogout, core * 256, 256, 0)
        ogout, by_col = tied(ogout, by_col)
        ogout_cols = [ogout, *send([ogout] * (col_count - 1), "col")]
        qkv_full = ring_gather(ring_gather(by_col, "row", row_count), "core", 2)
        small = qkv_full[0, :, :, 256:]
        ddt = small[:, :, :4].reshape(2, LOW, 512)
        du = small[:, :, 4:12, :HK].transpose(0, 2, 1, 3).reshape(LOW, K)
        bias = small[:, :, 12, :64].reshape(1, K)
        g1 = small[:, :, 12, 128:256].reshape(1, D)
        hg = small[:, :, 12, 256:288].reshape(1, HV)
        g2 = small[:, :, 12, 384:].reshape(1, D)
    else:

        def whole(shard):
            if shard.ndim == 1:
                return lax.all_gather(shard, ("row", "col"), axis=0, tiled=True)
            wide = lax.all_gather(shard, "col", axis=1, tiled=True)
            return lax.all_gather(wide, "row", axis=0, tiled=True)

        def blocks(full, width):
            return full.reshape(2, 2, 256, 4, width).transpose(1, 0, 3, 2, 4)

        qkv_full = jnp.concatenate(
            [blocks(whole(query_weight), 128), blocks(whole(key_weight), 128), blocks(whole(value_weight), 256)],
            axis=-1,
        )
        ogout_full = jnp.concatenate([blocks(whole(outgate_weight), 256), blocks(whole(out_weight), 256)], axis=-1)
        gate_t, lift_t, down = whole(swiglu_gate).T, whole(swiglu_up).T, whole(swiglu_down)
        feed_gate = gate_t.reshape(4, 4, 176, 2, 512).transpose(1, 3, 0, 2, 4)
        feed_lift = lift_t.reshape(4, 4, 176, 2, 512).transpose(1, 3, 0, 2, 4)
        feed_down = down.reshape(2, 4, 352, 4, 256).transpose(1, 0, 3, 2, 4)
        feed_full = jnp.concatenate([jnp.concatenate([feed_gate, feed_lift], axis=3), feed_down], axis=-1)
        ddt = whole(decay_down).T.reshape(LOW, 2, 512).transpose(1, 0, 2)
        du = whole(decay_up)
        bias = whole(decay_bias).reshape(1, K)
        g1 = whole(norm1_gain).reshape(1, D)
        hg = whole(head_gain).reshape(1, HV)
        g2 = whole(norm2_gain).reshape(1, D)
    du, bias, g1, hg, g2 = (part.astype(F32) for part in (du, bias, g1, hg, g2))

    tokens = layer_input.shape[0]
    seg_c = segment_ids.reshape(tokens, 1)
    seg_r = segment_ids.reshape(tokens // CH, 1, CH)
    core_at = (core if fast else jnp.zeros_like(core)).astype(jnp.int32).reshape(1)

    normed, q, k, v, low, logit = project(layer_input, g1, qkv_full, ddt, du, bias)
    if fast:
        q, ogout_cols = tied(q, ogout_cols)
        ogout = placed(ogout_cols, "col")
        other_row = swap(ogout, "row")
    mixed, states = attend(q, k, v, logit, segment_ids, seg_c, seg_r)
    if fast:
        mixed, other_row = tied(mixed, other_row)
        ogout = placed([ogout, other_row], "row")
        ogout_full = placed([ogout, swap(ogout, "core")], "core")
    og, gated, middle, normed_two = mix(layer_input, normed, mixed, ogout_full, hg, g2)
    layer_output, grad_normed_two, keep_gl, send_gl, keep_dn, send_dn = feed(
        core_at, normed_two, cotangent, middle, feed_full
    )
    grad_middle, branch, grad_og, grad_mixed, grad_g2, grad_hg = unmix(
        grad_normed_two, middle, cotangent, og, mixed, ogout_full, hg, g2
    )
    if fast:
        got_gl, got_dn = swap(send_gl, "core"), swap(send_dn, "core")
        x_at, row_at = lax.axis_index("x"), lax.axis_index("row")
        place = jnp.stack([x_at, row_at, lax.axis_index("col")]).astype(jnp.int32)
        go_g, st_g, go_l, st_l, st_d, *go_d = fold(place, keep_gl, got_gl, keep_dn, got_dn)
        branch, grad_og, go_g, go_l, go_d = tied(branch, grad_og, go_g, go_l, go_d)
        got_g, got_l, got_d = swap(go_g, "x"), swap(go_l, "row"), send(go_d, "col")
    keep_oo, send_oo = weight_grads(
        core_at, [normed, gated], [grad_og, branch], ((0, ((0, 0, 256),)), (1, ((256, 1, 256),))), True
    )
    if fast:
        grad_mixed, send_oo = tied(grad_mixed, send_oo)
        got_oo = swap(send_oo, "core")
    gq, gk, gv, glog = attend_back(q, k, v, logit, segment_ids, seg_c, seg_r, states, grad_mixed)
    keep_qkv, send_qkv = weight_grads(
        core_at, [normed], [gq, gk, gv], ((0, ((0, 0, 128), (128, 1, 128), (256, 2, 256))),)
    )
    if fast:
        send_qkv, got_g, got_l, got_d = tied(send_qkv, got_g, got_l, got_d)
        got_qkv = swap(send_qkv, "core")
        gate, lift, down = [st_g, got_g], [st_l, got_l], [st_d, *got_d]
        both = [jnp.concatenate(parts, axis=1) for parts in zip(gate, lift)]
        both = [part.reshape(2, 2, *part.shape[1:]) for part in both]
        col_hi, col_lo = lax.axis_index("col") // 2, lax.axis_index("col") % 2
        go_gl, go_d = piece_of(both, 1 - col_lo, 1), piece_of(down, 1 - x_at, 0)
        go_qkv = piece_of([keep_qkv, got_qkv], 1 - x_at, 0)
        go_oo = piece_of([keep_oo, got_oo], 1 - row_at, 0)
        glog, go_gl, go_d, go_qkv, go_oo = tied(glog, go_gl, go_d, go_qkv, go_oo)
        got_gl, got_d = swap(go_gl, "col"), swap(go_d, "x")
        got_qkv_x, got_oo_r = swap(go_qkv, "x"), swap(go_oo, "row")
    input_grad, grad_ddt, grad_du, grad_bias, grad_g1 = unproject(
        layer_input, normed, gq, gk, gv, glog, logit, low, grad_og, grad_middle, qkv_full, ogout_full, ddt, du, g1
    )

    if fast:
        late = (got_gl, got_d, got_oo_r, got_qkv_x)
        input_grad, grad_g1, late = tied(input_grad, grad_g1, late)
        got_gl, got_d, got_oo_r, got_qkv_x = late
        qkv = [piece_of([keep_qkv, got_qkv], x_at, 0), got_qkv_x]
        oo = [piece_of([keep_oo, got_oo], row_at, 0), got_oo_r]
        both = [piece_of(both, col_lo, 1), got_gl]
        go_qkv, go_oo, go_gl = piece_of(qkv, 1 - row_at, 0), piece_of(oo, 1 - x_at, 0), piece_of(both, 1 - col_hi, 0)
        go_qkv, go_oo, go_gl, grad_g1 = tied(go_qkv, go_oo, go_gl, grad_g1)
        qkv = [piece_of(qkv, row_at, 0), swap(go_qkv, "row")]
        oo = [piece_of(oo, x_at, 0), swap(go_oo, "x")]
        both = [piece_of(both, col_hi, 0), swap(go_gl, "col", 2)]
        tiny = jnp.concatenate(
            [
                grad_ddt.reshape(4, 4, 2, 512).transpose(2, 0, 1, 3),
                jnp.pad(grad_du.reshape(2, 8, 4, HK).transpose(0, 2, 1, 3), ((0, 0), (0, 0), (0, 0), (0, 384))),
                jnp.concatenate(
                    [
                        jnp.pad(grad_bias.reshape(2, 4, 64), ((0, 0), (0, 0), (0, 64))),
                        grad_g1.reshape(2, 4, 128),
                        jnp.pad(grad_hg.reshape(2, 4, 32), ((0, 0), (0, 0), (0, 96))),
                        grad_g2.reshape(2, 4, 128),
                    ],
                    axis=-1,
                ).reshape(2, 4, 1, 512),
                jnp.zeros((2, 4, 3, 512), F32),
            ],
            axis=2,
        )
        tiny = tiny + swap(tiny, "core")
        tiny = tiny + swap(tiny, "x")
        tiny = added([staying([tiny], "row", 0), *send(going([tiny], "row", 0), "row")])
        gate, lift = [[part[at : at + 2] for part in both] for at in (0, 2)]
        down = [piece_of(down, x_at, 0), got_d]
        gate = [piece_of(gate, row_at, 0), swap(piece_of(gate, 1 - row_at, 0), "row")]
        down = [piece_of(down, row_at, 0), swap(piece_of(down, 1 - row_at, 0), "row")]
        lift = [piece_of(lift, x_at, 0), swap(piece_of(lift, 1 - x_at, 0), "x")]
        down = added(down)
        feeds = share(jnp.concatenate([added(gate), added(lift), down[0], down[1]], axis=-1))
        rest = jnp.concatenate([added(qkv), added(oo)], axis=-1)
        rest = share(added([staying([rest], "col", 0), *send(going([rest], "col", 0), "col")]))
        tiny = added([staying([tiny], "col", 0), *send(going([tiny], "col", 0), "col")]).astype(F32)
        out_dd, out_du = tiny[:4].T, tiny[4:12, :HK]
        out_bias, out_g1, out_hg, out_g2 = tiny[12, :64], tiny[12, 128:256], tiny[12, 256:288], tiny[12, 384:]
    else:
        tiny = jnp.concatenate(
            [
                grad_ddt,
                jnp.pad(grad_du, ((0, 0), (0, D - K))),
                jnp.concatenate([grad_bias, grad_hg, jnp.zeros((1, D - K - HV), F32)], axis=1),
                grad_g1,
                grad_g2,
                jnp.zeros((5, D), F32),
            ],
            axis=0,
        )
        tiny = lax.psum(tiny, AXES)
        r, c = lax.axis_index("row"), lax.axis_index("col")

        def own(line, size):
            return lax.dynamic_slice_in_dim(line, (r * col_count + c) * size, size, 0)

        def own_block(full, shape):
            return lax.dynamic_slice(full, (r * shape[0], c * shape[1]), shape)

        out_bias = own(tiny[32, :K], decay_bias.shape[0])
        out_hg = own(tiny[32, K : K + HV], head_gain.shape[0])
        out_g1 = own(tiny[33], norm1_gain.shape[0])
        out_g2 = own(tiny[34], norm2_gain.shape[0])
        out_du = own_block(tiny[16:32, :K], decay_up.shape)
        down_rows = decay_down.shape
        out_dd = lax.dynamic_slice(tiny, (c * down_rows[1], r * down_rows[0]), down_rows[::-1]).T

    if fast:
        out_gate = feeds[..., :512].reshape(HC, 512).T
        out_lift = feeds[..., 512:1024].reshape(HC, 512).T
        out_down = jnp.stack([feeds[..., 1024:1280], feeds[..., 1280:]]).reshape(1408, 256)
        qkv = rest[..., :512].reshape(512, 512)
        oo = rest[..., 512:].reshape(512, 512)
        shards = [qkv[:, :128], qkv[:, 128:256], qkv[:, 256:], oo[:, :256], oo[:, 256:], out_gate, out_lift, out_down]
    else:

        def joined(keep, send):
            return jnp.stack([keep, send])

        keep_oo, send_oo = keep_oo.swapaxes(0, 1), send_oo.swapaxes(0, 1)

        def matrix(pack):
            return pack.transpose(2, 0, 1, 4, 3, 5).reshape(D, -1)

        oo = joined(keep_oo, send_oo)
        qkv = joined(keep_qkv, send_qkv)
        gl = joined(keep_gl, send_gl).reshape(2, 2, 2, 4, 2, 176, 512).transpose(4, 3, 0, 1, 5, 2, 6)
        gl = gl.reshape(2, FF, D)
        dn = joined(keep_dn, send_dn).transpose(2, 4, 0, 1, 5, 3, 6).reshape(FF, D)
        fulls = [
            matrix(qkv[..., :128]),
            matrix(qkv[..., 128:256]),
            matrix(qkv[..., 256:]),
            matrix(oo[..., :256]),
            matrix(oo[..., 256:]),
            gl[0].T,
            gl[1].T,
            dn,
        ]
        shards = []
        for full in fulls:
            part = lax.psum(full, ("x", "core"))
            part = lax.psum_scatter(part, "row", scatter_dimension=0, tiled=True)
            shards.append(lax.psum_scatter(part, "col", scatter_dimension=1, tiled=True))
    out_q, out_k, out_v, out_og, out_out, out_gate, out_lift, out_down = (part.astype(F32) for part in shards)
    return (
        layer_output,
        input_grad,
        out_g1,
        out_q,
        out_k,
        out_v,
        out_og,
        out_dd,
        out_du,
        out_bias,
        out_hg,
        out_out,
        out_g2,
        out_gate,
        out_lift,
        out_down,
    )


def solution(mesh):
    shape = dict(mesh.shape)
    finer = Mesh(mesh.devices.reshape(shape["dp"] // 2, 2, shape["row"], shape["col"]), AXES)
    tokens = P(AXES, None)
    vector = P(("row", "col"))
    matrix = P("row", "col")
    in_specs = (
        tokens, tokens, vector, matrix, matrix, matrix, matrix, matrix, matrix, vector, vector,
        matrix, vector, matrix, matrix, matrix, tokens,
    )
    out_specs = (
        tokens, tokens, vector, matrix, matrix, matrix, matrix, matrix, matrix, vector, vector,
        matrix, vector, matrix, matrix, matrix,
    )
    return jax.shard_map(per_device, mesh=finer, in_specs=in_specs, out_specs=out_specs, check_vma=False)
```

```python
import functools

import jax
import jax.numpy as jnp
from jax import lax
from jax.experimental import pallas as pl
from jax.experimental.pallas import tpu as pltpu
from jax.sharding import Mesh
from jax.sharding import PartitionSpec as P

HEADS = 4
HK = 128
HV = 256
CH = 64
LOW = 16
D = 1024
K = HEADS * HK
V = HEADS * HV
FF = 2816
HC = FF // 4
TILE = 256
FEED_TILE = 1024

EPS = 1e-05
HIGH = lax.Precision.HIGHEST
F32 = jnp.float32
BF16 = jnp.bfloat16
AXES = ("x", "core", "row", "col")
MIB = 1024 * 1024


def dot(left, right, precision=None):
    return jnp.dot(left, right, preferred_element_type=F32, precision=precision)


def dot_nt(left, right, precision=None):
    return lax.dot_general(
        left, right, (((1,), (1,)), ((), ())), preferred_element_type=F32, precision=precision
    )


def dot_tn(left, right, precision=None):
    return lax.dot_general(
        left, right, (((0,), (0,)), ((), ())), preferred_element_type=F32, precision=precision
    )


def halves(value):
    high = value.astype(BF16)
    return high, (value - high.astype(F32)).astype(BF16)


def struct(shape, dtype):
    return jax.ShapeDtypeStruct(shape, dtype)


def fixed(shape):
    return pl.BlockSpec(shape, lambda *i: (0,) * len(shape))


def rows(height, width):
    return pl.BlockSpec((height, width), lambda i: (i, 0))


def cost(flops, moved, trans=0):
    return pl.CostEstimate(flops=int(flops), bytes_accessed=int(moved), transcendentals=int(trans))


def params(mib):
    return pltpu.CompilerParams(vmem_limit_bytes=mib * MIB)


def project_kernel(x_ref, gain_ref, wqk_ref, wv_ref, ddt_ref, du_ref, bias_ref, n_ref, q_ref, k_ref, v_ref, low_ref, logit_ref):
    x = x_ref[...].astype(F32)
    inverse = lax.rsqrt(jnp.mean(x * x, axis=-1, keepdims=True) + EPS)
    normed = (x * inverse * gain_ref[...]).astype(BF16)
    n_ref[...] = normed
    for c in range(HEADS):
        wide = value = None
        for r in range(2):
            for core in range(2):
                at = r * 512 + core * 256
                part = dot(normed[:, at : at + 256], wqk_ref[core, r, c])
                wide = part if wide is None else wide + part
                part = dot(normed[:, at : at + 256], wv_ref[core, c, r])
                value = part if value is None else value + part
        q_ref[:, c * HK : (c + 1) * HK] = wide[:, :HK].astype(BF16)
        k_ref[:, c * HK : (c + 1) * HK] = wide[:, HK:].astype(BF16)
        v_ref[:, c * HV : (c + 1) * HV] = value.astype(BF16)
    low = dot_nt(normed[:, :512], ddt_ref[0]) + dot_nt(normed[:, 512:], ddt_ref[1])
    low_ref[...] = low
    high, rest = halves(low)
    du = du_ref[...]
    logit_ref[...] = dot(high, du) + dot(rest, du) + bias_ref[...]


def project(x, gain, qk_weights, v_weights, ddt, du, bias):
    tokens = x.shape[0]
    return pl.pallas_call(
        project_kernel,
        grid=(tokens // TILE,),
        in_specs=[
            rows(TILE, D),
            fixed((1, D)),
            fixed((2, 2, 4, 256, 256)),
            fixed((2, 4, 2, 256, 256)),
            fixed((2, LOW, 512)),
            fixed((LOW, K)),
            fixed((1, K)),
        ],
        out_specs=[rows(TILE, D), rows(TILE, K), rows(TILE, K), rows(TILE, V), rows(TILE, LOW), rows(TILE, K)],
        out_shape=[
            struct((tokens, D), BF16),
            struct((tokens, K), BF16),
            struct((tokens, K), BF16),
            struct((tokens, V), BF16),
            struct((tokens, LOW), F32),
            struct((tokens, K), F32),
        ],
        compiler_params=params(60),
        cost_estimate=cost(2 * tokens * D * 2048, 14 * MIB),
        name="project",
    )(x, gain, qk_weights, v_weights, ddt, du, bias)


def span_parts(logit, doc_c, doc_r, last_doc, prev_doc):
    lower = lax.broadcasted_iota(jnp.int32, (CH, CH), 0) >= lax.broadcasted_iota(jnp.int32, (CH, CH), 1)
    mask = jnp.where(lower & (doc_c == doc_r), HK ** (-0.5), 0.0)
    log_decay = (jnp.minimum(logit, 0.0) - jnp.log1p(jnp.exp(-jnp.abs(logit)))) * (1.0 / 16.0)
    cumul = dot(lower.astype(F32), log_decay, HIGH)
    centre = cumul[CH // 2 - 1 : CH // 2]
    last = cumul[CH - 1 :]
    rise = jnp.exp(cumul - centre)
    fall = jnp.exp(centre - cumul)
    growth = jnp.exp(cumul)
    to_end = jnp.exp(last - cumul)
    enter = jnp.where(doc_c == prev_doc, HK ** (-0.5), 0.0)
    same = jnp.where(doc_c == last_doc, 1.0, 0.0)
    return mask, rise, fall, growth, to_end, enter, same, jnp.exp(last)


def span_docs(seg_ref, at, first):
    last_doc = seg_ref[at + CH - 1]
    prev_doc = jnp.where(first, -1, seg_ref[jnp.maximum(at - 1, 0)])
    return last_doc, prev_doc


def attend_kernel(spans, seg_ref, q_ref, k_ref, v_ref, logit_ref, dc_ref, dr_ref, mixed_ref, states_ref, state):
    i = pl.program_id(1)
    at = (pl.program_id(0) * spans + i) * CH
    last_doc, prev_doc = span_docs(seg_ref, at, i == 0)

    @pl.when(i == 0)
    def _():
        state[...] = jnp.zeros_like(state)

    mask, rise, fall, growth, to_end, enter, same, keep = span_parts(
        logit_ref[...], dc_ref[...], dr_ref[0], last_doc, prev_doc
    )
    query = q_ref[...].astype(F32)
    keys = k_ref[...].astype(F32)
    qs = (query * rise).astype(BF16)
    ks = (keys * fall).astype(BF16)
    qg = (query * growth * enter).astype(BF16)
    kw = (keys * to_end * same).astype(BF16)
    keep = keep * jnp.where(last_doc == prev_doc, 1.0, 0.0)
    for h in range(HEADS):
        a, b = h * HK, (h + 1) * HK
        va = v_ref[:, h * HV : (h + 1) * HV]
        now = state[h]
        low = now.astype(BF16)
        states_ref[0, h] = low
        scores = (dot_nt(qs[:, a:b], ks[:, a:b]) * mask).astype(BF16)
        mixed_ref[:, h * HV : (h + 1) * HV] = dot(scores, va) + dot_nt(qg[:, a:b], low)
        state[h] = now * keep[:, a:b] + dot_tn(va, kw[:, a:b])


def attend(q, k, v, logit, segs, seg_c, seg_r):
    tokens = q.shape[0]
    seqs = segs.shape[0]
    spans = tokens // seqs // CH

    def part(width):
        return pl.BlockSpec((CH, width), lambda s, i, seg: (s * spans + i, 0))

    return pl.pallas_call(
        functools.partial(attend_kernel, spans),
        grid_spec=pltpu.PrefetchScalarGridSpec(
            num_scalar_prefetch=1,
            grid=(seqs, spans),
            in_specs=[
                part(K),
                part(K),
                part(V),
                part(K),
                part(1),
                pl.BlockSpec((1, 1, CH), lambda s, i, seg: (s * spans + i, 0, 0)),
            ],
            out_specs=[
                part(V),
                pl.BlockSpec((1, HEADS, HV, HK), lambda s, i, seg: (s * spans + i, 0, 0, 0)),
            ],
            scratch_shapes=[pltpu.VMEM((HEADS, HV, HK), F32)],
        ),
        out_shape=[struct((tokens, V), F32), struct((seqs * spans, HEADS, HV, HK), BF16)],
        compiler_params=params(60),
        cost_estimate=cost(2e10, 16 * MIB),
        name="attend",
    )(segs.reshape(-1), q, k, v, logit, seg_c, seg_r)


def attend_back_kernel(
    spans, seg_ref, q_ref, k_ref, v_ref, logit_ref, dc_ref, dr_ref, states_ref, g_ref,
    gq_ref, gk_ref, gv_ref, gl_ref, grad_state,
):
    i = spans - 1 - pl.program_id(1)
    at = (pl.program_id(0) * spans + i) * CH
    last_doc, prev_doc = span_docs(seg_ref, at, i == 0)

    @pl.when(pl.program_id(1) == 0)
    def _():
        grad_state[...] = jnp.zeros_like(grad_state)

    mask, rise, fall, growth, to_end, enter, same, keep = span_parts(
        logit_ref[...], dc_ref[...], dr_ref[0], last_doc, prev_doc
    )
    query = q_ref[...].astype(F32)
    keys = k_ref[...].astype(F32)
    qs = (query * rise).astype(BF16)
    ks = (keys * fall).astype(BF16)
    qg = (query * growth * enter).astype(BF16)
    kw = (keys * to_end * same).astype(BF16)
    keep = keep * jnp.where(last_doc == prev_doc, 1.0, 0.0)
    last_row = lax.broadcasted_iota(jnp.int32, (CH, HK), 0) == CH - 1
    upper = lax.broadcasted_iota(jnp.int32, (CH, CH), 0) <= lax.broadcasted_iota(jnp.int32, (CH, CH), 1)
    upper = upper.astype(F32)
    for h in range(HEADS):
        a, b = h * HK, (h + 1) * HK
        va = v_ref[:, h * HV : (h + 1) * HV]
        ga = g_ref[:, h * HV : (h + 1) * HV]
        qh, kh = qs[:, a:b], ks[:, a:b]
        state = states_ref[0, h]
        grad = grad_state[h]
        grad_low = grad.astype(BF16)
        scores = (dot_nt(qh, kh) * mask).astype(BF16)
        grad_scores = (dot_nt(ga, va) * mask).astype(BF16)
        gv_ref[:, h * HV : (h + 1) * HV] = (dot_tn(scores, ga) + dot_nt(kw[:, a:b], grad_low)).astype(BF16)
        wk = dot(va, grad_low) * same * to_end[:, a:b]
        wq = dot(ga, state) * enter * growth[:, a:b]
        query_inner = dot(grad_scores, kh)
        key_inner = dot_tn(grad_scores, qh)
        gq_ref[:, a:b] = (query_inner * rise[:, a:b] + wq).astype(BF16)
        gk_ref[:, a:b] = (key_inner * fall[:, a:b] + wk).astype(BF16)
        ends = wk * keys[:, a:b]
        grad_cumul = qh.astype(F32) * query_inner - kh.astype(F32) * key_inner + query[:, a:b] * wq - ends
        kept = grad * keep[:, a:b]
        at_last = jnp.sum(ends, axis=0, keepdims=True) + jnp.sum(kept * state.astype(F32), axis=0, keepdims=True)
        grad_cumul = grad_cumul + jnp.where(last_row, at_last, 0.0)
        gl_ref[:, a:b] = dot(upper, grad_cumul, HIGH)
        grad_state[h] = kept + dot_tn(ga, qg[:, a:b])


def attend_back(q, k, v, logit, segs, seg_c, seg_r, states, grad):
    tokens = q.shape[0]
    seqs = segs.shape[0]
    spans = tokens // seqs // CH

    def part(width):
        return pl.BlockSpec((CH, width), lambda s, i, seg: (s * spans + spans - 1 - i, 0))

    return pl.pallas_call(
        functools.partial(attend_back_kernel, spans),
        grid_spec=pltpu.PrefetchScalarGridSpec(
            num_scalar_prefetch=1,
            grid=(seqs, spans),
            in_specs=[
                part(K),
                part(K),
                part(V),
                part(K),
                part(1),
                pl.BlockSpec((1, 1, CH), lambda s, i, seg: (s * spans + spans - 1 - i, 0, 0)),
                pl.BlockSpec((1, HEADS, HV, HK), lambda s, i, seg: (s * spans + spans - 1 - i, 0, 0, 0)),
                part(V),
            ],
            out_specs=[part(K), part(K), part(V), part(K)],
            scratch_shapes=[pltpu.VMEM((HEADS, HV, HK), F32)],
        ),
        out_shape=[
            struct((tokens, K), BF16),
            struct((tokens, K), BF16),
            struct((tokens, V), BF16),
            struct((tokens, K), F32),
        ],
        compiler_params=params(60),
        cost_estimate=cost(1, 1),
        name="attend_back",
    )(segs.reshape(-1), q, k, v, logit, seg_c, seg_r, states, grad)


def mix_kernel(x_ref, n_ref, mixed_ref, w_ref, hg_ref, g2_ref, og_ref, gated_ref, middle_ref, n2_ref):
    normed = n_ref[...]
    outs = [None] * 4
    for c in range(HEADS):
        og = None
        for r in range(2):
            for core in range(2):
                at = r * 512 + core * 256
                part = dot(normed[:, at : at + 256], w_ref[core, r, c, :, :HV])
                og = part if og is None else og + part
        og_ref[:, c * HV : (c + 1) * HV] = og
        mixed = mixed_ref[:, c * HV : (c + 1) * HV]
        inverse = lax.rsqrt(jnp.mean(mixed * mixed, axis=-1, keepdims=True) + EPS)
        gated = (mixed * inverse * hg_ref[...] * (og * jax.nn.sigmoid(og))).astype(BF16)
        gated_ref[:, c * HV : (c + 1) * HV] = gated
        for e in range(4):
            part = dot(gated, w_ref[c % 2, c // 2, e, :, HV:])
            outs[e] = part if outs[e] is None else outs[e] + part
    middle = x_ref[...].astype(F32) + jnp.concatenate(outs, axis=1)
    middle_ref[...] = middle
    inverse = lax.rsqrt(jnp.mean(middle * middle, axis=-1, keepdims=True) + EPS)
    n2_ref[...] = (middle * inverse * g2_ref[...]).astype(BF16)


def mix(x, normed, mixed, weights, head_gain, gain_two):
    tokens = x.shape[0]
    return pl.pallas_call(
        mix_kernel,
        grid=(tokens // TILE,),
        in_specs=[
            rows(TILE, D),
            rows(TILE, D),
            rows(TILE, V),
            fixed((2, 2, 4, 256, 512)),
            fixed((1, HV)),
            fixed((1, D)),
        ],
        out_specs=[rows(TILE, V), rows(TILE, V), rows(TILE, D), rows(TILE, D)],
        out_shape=[
            struct((tokens, V), F32),
            struct((tokens, V), BF16),
            struct((tokens, D), F32),
            struct((tokens, D), BF16),
        ],
        compiler_params=params(60),
        cost_estimate=cost(2 * tokens * D * 2048, 24 * MIB),
        name="mix",
    )(x, normed, mixed, weights, head_gain, gain_two)


def feed_kernel(
    core_ref, n2_ref, dy_ref, middle_ref, gl_ref, dn_ref,
    out_ref, gn_ref, keep_gl, send_gl, keep_dn, send_dn, y_acc, hid, gate_g, lift_g,
):
    step = pl.program_id(0)

    @pl.when(step == 0)
    def _():
        y_acc[...] = middle_ref[...]
        gn_ref[...] = jnp.zeros_like(gn_ref)

    @pl.loop(0, n2_ref.shape[0] // FEED_TILE)
    def _(t):
        at = pl.ds(pl.multiple_of(t * FEED_TILE, FEED_TILE), FEED_TILE)
        gate = lift = back = None
        for r in range(2):
            n2 = n2_ref[at, r * 512 : (r + 1) * 512]
            a = dot_nt(n2, gl_ref[:, r, 0, :176].reshape(HC, 512))
            b = dot_nt(n2, gl_ref[:, r, 0, 176:].reshape(HC, 512))
            gate = a if r == 0 else gate + a
            lift = b if r == 0 else lift + b
        for c in range(4):
            a = dot_nt(dy_ref[at, c * 256 : (c + 1) * 256], dn_ref[:, 0, c].reshape(HC, 256))
            back = a if c == 0 else back + a
        sig = jax.nn.sigmoid(gate)
        swish = gate * sig
        hidden = (swish * lift).astype(BF16)
        grad_lift = (back * swish).astype(BF16)
        grad_gate = (back * lift * sig * (1.0 + gate * (1.0 - sig))).astype(BF16)
        hid[at, :] = hidden
        gate_g[at, :] = grad_gate
        lift_g[at, :] = grad_lift
        for c in range(4):
            lanes = slice(c * 256, (c + 1) * 256)
            y_acc[at, lanes] += dot(hidden, dn_ref[:, 0, c].reshape(HC, 256))
        for r in range(2):
            lanes = slice(r * 512, (r + 1) * 512)
            gn_ref[at, lanes] += dot(grad_gate, gl_ref[:, r, 0, :176].reshape(HC, 512)) + dot(
                grad_lift, gl_ref[:, r, 0, 176:].reshape(HC, 512)
            )

    @pl.when(step == 3)
    def _():
        out_ref[...] = y_acc[...].astype(BF16)

    first = core_ref[0] == 0
    for m, (source, right) in enumerate(((gate_g, n2_ref), (lift_g, n2_ref), (hid, dy_ref))):
        both = dot_tn(source[...], right[...]).astype(BF16)
        low, high = both[: HC // 2], both[HC // 2 :]
        mine = jnp.where(first, low, high)
        other = jnp.where(first, high, low)
        for part, gl_out, dn_out in ((mine, keep_gl, keep_dn), (other, send_gl, send_dn)):
            for x in range(2):
                piece = part[x * 176 : (x + 1) * 176]
                if m < 2:
                    for r in range(2):
                        gl_out[x, r, 0, m * 176 : (m + 1) * 176] = piece[:, r * 512 : (r + 1) * 512]
                else:
                    for c in range(4):
                        dn_out[x, 0, c, 0] = piece[:, c * 256 : (c + 1) * 256]


def feed(core, n2, dy, middle, weights):
    tokens = n2.shape[0]
    gl = pl.BlockSpec((2, 2, 1, 352, 512), lambda i, c: (0, 0, i, 0, 0))
    dn = pl.BlockSpec((2, 1, 4, 1, 176, 256), lambda i, c: (0, i // 2, 0, i % 2, 0, 0))
    once = pl.Buffered(1)
    return pl.pallas_call(
        feed_kernel,
        grid_spec=pltpu.PrefetchScalarGridSpec(
            num_scalar_prefetch=1,
            grid=(4,),
            in_specs=[
                pl.BlockSpec((tokens, D), lambda i, c: (0, 0), pipeline_mode=once),
                pl.BlockSpec((tokens, D), lambda i, c: (0, 0), pipeline_mode=once),
                pl.BlockSpec((tokens, D), lambda i, c: (0, 0), pipeline_mode=once),
                pl.BlockSpec((4, 2, 1, 352, 512), lambda i, c: (0, 0, i, 0, 0)),
                pl.BlockSpec((2, 1, 4, 352, 256), lambda i, c: (i % 2, i // 2, 0, 0, 2)),
            ],
            out_specs=[
                pl.BlockSpec((tokens, D), lambda i, c: (0, 0), pipeline_mode=once),
                pl.BlockSpec((tokens, D), lambda i, c: (0, 0), pipeline_mode=once),
                gl,
                gl,
                dn,
                dn,
            ],
            scratch_shapes=[
                pltpu.VMEM((tokens, D), F32),
                pltpu.VMEM((tokens, HC), BF16),
                pltpu.VMEM((tokens, HC), BF16),
                pltpu.VMEM((tokens, HC), BF16),
            ],
        ),
        out_shape=[
            struct((tokens, D), BF16),
            struct((tokens, D), F32),
            struct((2, 2, 4, 352, 512), BF16),
            struct((2, 2, 4, 352, 512), BF16),
            struct((2, 2, 4, 2, 176, 256), BF16),
            struct((2, 2, 4, 2, 176, 256), BF16),
        ],
        compiler_params=params(60),
        cost_estimate=cost(18 * tokens * D * FF, 60 * MIB),
        name="feed",
    )(core, n2, dy, middle, weights, weights)


def unmix_kernel(
    gn_ref, middle_ref, dy_ref, og_ref, mixed_ref, w_ref, hg_ref, g2_ref,
    gm_ref, gb_ref, gog_ref, gmix_ref, gg2_ref, ghg_ref,
):
    @pl.when(pl.program_id(0) == 0)
    def _():
        gg2_ref[...] = jnp.zeros_like(gg2_ref)
        ghg_ref[...] = jnp.zeros_like(ghg_ref)

    grad = gn_ref[...]
    middle = middle_ref[...]
    inverse = lax.rsqrt(jnp.mean(middle * middle, axis=-1, keepdims=True) + EPS)
    unit = middle * inverse
    gg2_ref[...] += jnp.sum(grad * unit, axis=0, keepdims=True)
    scaled = grad * g2_ref[...]
    grad_middle = dy_ref[...].astype(F32) + inverse * (scaled - unit * jnp.mean(scaled * unit, axis=-1, keepdims=True))
    gm_ref[...] = grad_middle
    branch = grad_middle.astype(BF16)
    gb_ref[...] = branch
    head_gain = hg_ref[...]
    for c in range(HEADS):
        lanes = slice(c * HV, (c + 1) * HV)
        back = None
        for e in range(4):
            part = dot_nt(branch[:, e * 256 : (e + 1) * 256], w_ref[c % 2, c // 2, e, :, HV:])
            back = part if back is None else back + part
        og = og_ref[:, lanes]
        sig = jax.nn.sigmoid(og)
        mixed = mixed_ref[:, lanes]
        inv = lax.rsqrt(jnp.mean(mixed * mixed, axis=-1, keepdims=True) + EPS)
        unit = mixed * inv
        gog_ref[:, lanes] = (back * (unit * head_gain) * sig * (1.0 + og * (1.0 - sig))).astype(BF16)
        incoming = back * (og * sig)
        ghg_ref[...] += jnp.sum(incoming * unit, axis=0, keepdims=True)
        scaled = incoming * head_gain
        gmix_ref[:, lanes] = (inv * (scaled - unit * jnp.mean(scaled * unit, axis=-1, keepdims=True))).astype(BF16)


def unmix(grad, middle, dy, og, mixed, weights, head_gain, gain_two):
    tokens = grad.shape[0]
    return pl.pallas_call(
        unmix_kernel,
        grid=(tokens // TILE,),
        in_specs=[
            rows(TILE, D),
            rows(TILE, D),
            rows(TILE, D),
            rows(TILE, V),
            rows(TILE, V),
            fixed((2, 2, 4, 256, 512)),
            fixed((1, HV)),
            fixed((1, D)),
        ],
        out_specs=[rows(TILE, D), rows(TILE, D), rows(TILE, V), rows(TILE, V), fixed((1, D)), fixed((1, HV))],
        out_shape=[
            struct((tokens, D), F32),
            struct((tokens, D), BF16),
            struct((tokens, V), BF16),
            struct((tokens, V), BF16),
            struct((1, D), F32),
            struct((1, HV), F32),
        ],
        compiler_params=params(60),
        cost_estimate=cost(2 * tokens * D * D, 30 * MIB),
        name="unmix",
    )(grad, middle, dy, og, mixed, weights, head_gain, gain_two)


def weight_grad_kernel(plan, row_first, core_ref, *refs):
    count = 2 * len(plan)
    keep_ref, send_ref = refs[-2:]
    lefts, rights = refs[:count], refs[count:-2]
    for lefts_at, start, indices in plan:
        right = [rights[index][...] for index in indices]
        right = right[0] if len(right) == 1 else jnp.concatenate(right, axis=1)
        left = jnp.concatenate([lefts[2 * lefts_at][...], lefts[2 * lefts_at + 1][...]], axis=1)
        both = dot_tn(left, right).astype(BF16)
        for ref, part in ((keep_ref, both[:256]), (send_ref, both[256:])):
            for x in range(2):
                at = (0, x, 0) if row_first else (x, 0, 0)
                ref[(*at, slice(None), slice(start, start + right.shape[1]))] = part[x * 128 : (x + 1) * 128]


def weight_grads(core, lefts, rights, plan, row_first=False):
    tokens = lefts[0].shape[0]
    specs = []
    for left in lefts:
        specs.append(pl.BlockSpec((tokens, 256), lambda r, c, core: (0, r * 2 + core[0])))
        specs.append(pl.BlockSpec((tokens, 256), lambda r, c, core: (0, r * 2 + 1 - core[0])))
    for right in rights:
        specs.append(pl.BlockSpec((tokens, right.shape[1] // 4), lambda r, c, core: (0, c)))
    if row_first:
        out = pl.BlockSpec((1, 2, 1, 128, 512), lambda r, c, core: (r, 0, c, 0, 0))
    else:
        out = pl.BlockSpec((2, 1, 1, 128, 512), lambda r, c, core: (0, r, c, 0, 0))
    operands = [left for left in lefts for _ in range(2)] + list(rights)
    return pl.pallas_call(
        functools.partial(weight_grad_kernel, plan, row_first),
        grid_spec=pltpu.PrefetchScalarGridSpec(
            num_scalar_prefetch=1, grid=(2, 4), in_specs=specs, out_specs=[out, out]
        ),
        out_shape=[struct((2, 2, 4, 128, 512), BF16)] * 2,
        compiler_params=params(60),
        cost_estimate=cost(1, 1),
        name="weight_grads",
    )(core, *operands)


def unproject_kernel(
    x_ref, n_ref, gq_ref, gk_ref, gv_ref, glog_ref, logit_ref, low_ref, gog_ref, gm_ref,
    wqk_ref, wv_ref, wo_ref, ddt_ref, du_ref, g1_ref,
    gx_ref, gddt_ref, gdu_ref, gbias_ref, gg1_ref,
):
    @pl.when(pl.program_id(0) == 0)
    def _():
        gddt_ref[...] = jnp.zeros_like(gddt_ref)
        gdu_ref[...] = jnp.zeros_like(gdu_ref)
        gbias_ref[...] = jnp.zeros_like(gbias_ref)
        gg1_ref[...] = jnp.zeros_like(gg1_ref)

    normed = n_ref[...]
    grad_logit = glog_ref[...] * (1.0 / 16.0) * jax.nn.sigmoid(-logit_ref[...])
    gbias_ref[...] += jnp.sum(grad_logit, axis=0, keepdims=True)
    high, rest = halves(grad_logit)
    low, low_rest = halves(low_ref[...])
    gdu_ref[...] += dot_tn(low, high) + dot_tn(low, rest) + dot_tn(low_rest, high)
    du = du_ref[...]
    grad_low = (dot_nt(high, du) + dot_nt(rest, du)).astype(BF16)
    gddt_ref[...] += dot_tn(grad_low, normed)
    lefts = [
        jnp.concatenate(
            [
                gq_ref[:, c * HK : (c + 1) * HK],
                gk_ref[:, c * HK : (c + 1) * HK],
            ],
            axis=1,
        )
        for c in range(HEADS)
    ]
    parts = []
    for r in range(2):
        small = dot(grad_low, ddt_ref[r])
        for core in range(2):
            total = small[:, core * 256 : (core + 1) * 256]
            for c in range(HEADS):
                total = total + dot_nt(lefts[c], wqk_ref[core, r, c])
                total = total + dot_nt(gv_ref[:, c * HV : (c + 1) * HV], wv_ref[core, c, r])
                total = total + dot_nt(gog_ref[:, c * HV : (c + 1) * HV], wo_ref[core, r, c])
            parts.append(total)
    grad = jnp.concatenate(parts, axis=1)
    x = x_ref[...].astype(F32)
    inverse = lax.rsqrt(jnp.mean(x * x, axis=-1, keepdims=True) + EPS)
    unit = x * inverse
    gg1_ref[...] += jnp.sum(grad * unit, axis=0, keepdims=True)
    scaled = grad * g1_ref[...]
    gx_ref[...] = gm_ref[...] + inverse * (scaled - unit * jnp.mean(scaled * unit, axis=-1, keepdims=True))


def unproject(x, normed, gq, gk, gv, glog, logit, low, gog, gm, qk_weights, v_weights, out_weights, ddt, du, gain):
    tokens = x.shape[0]
    return pl.pallas_call(
        unproject_kernel,
        grid=(tokens // TILE,),
        in_specs=[
            rows(TILE, D),
            rows(TILE, D),
            rows(TILE, K),
            rows(TILE, K),
            rows(TILE, V),
            rows(TILE, K),
            rows(TILE, K),
            rows(TILE, LOW),
            rows(TILE, V),
            rows(TILE, D),
            fixed((2, 2, 4, 256, 256)),
            fixed((2, 4, 2, 256, 256)),
            fixed((2, 2, 4, 256, HV)),
            fixed((2, LOW, 512)),
            fixed((LOW, K)),
            fixed((1, D)),
        ],
        out_specs=[rows(TILE, D), fixed((LOW, D)), fixed((LOW, K)), fixed((1, K)), fixed((1, D))],
        out_shape=[
            struct((tokens, D), F32),
            struct((LOW, D), F32),
            struct((LOW, K), F32),
            struct((1, K), F32),
            struct((1, D), F32),
        ],
        compiler_params=params(60),
        cost_estimate=cost(2 * tokens * D * 3072, 100 * MIB),
        name="unproject",
    )(x, normed, gq, gk, gv, glog, logit, low, gog, gm, qk_weights, v_weights, out_weights, ddt, du, gain)


def fold_kernel(place_ref, keep_gl, got_gl, keep_dn, got_dn, go_g, st_g, go_l, st_l, *downs):
    i = pl.program_id(0)
    x_at, row_at = place_ref[0], place_ref[1]

    def both(left, right):
        return (left.astype(F32) + right.astype(F32)).astype(BF16)

    for r in range(2):
        for ref, x in ((go_g, 1 - x_at), (st_g, x_at)):
            ref[0, r] = both(keep_gl[x, r, 0, :176], got_gl[x, r, 0, :176])
    for x in range(2):
        for ref, r in ((go_l, 1 - row_at), (st_l, row_at)):
            ref[0, x] = both(keep_gl[x, r, 0, 176:], got_gl[x, r, 0, 176:])
    for shift in range(4):

        @pl.when(i == shift)
        def _():
            downs[shift][...] = both(keep_dn[:, :, 0], got_dn[:, :, 0])


def fold(place, keep_gl, got_gl, keep_dn, got_dn):
    gl = pl.BlockSpec((2, 2, 1, 352, 512), lambda i, p: (0, 0, i, 0, 0))
    dn = pl.BlockSpec((2, 2, 1, 2, 176, 256), lambda i, p: (0, 0, lax.rem(p[2] + i, 4), 0, 0, 0))
    out = pl.BlockSpec((1, 2, 176, 512), lambda i, p: (i, 0, 0, 0))
    down = pl.BlockSpec((2, 2, 2, 176, 256), lambda i, p: (0, 0, 0, 0, 0))
    return pl.pallas_call(
        fold_kernel,
        grid_spec=pltpu.PrefetchScalarGridSpec(
            num_scalar_prefetch=1,
            grid=(4,),
            in_specs=[gl, gl, dn, dn],
            out_specs=[out] * 4 + [down] * 4,
        ),
        out_shape=[struct((4, 2, 176, 512), BF16)] * 4 + [struct((2, 2, 2, 176, 256), BF16)] * 4,
        compiler_params=params(60),
        cost_estimate=cost(1, 26 * MIB),
        name="fold",
    )(place, keep_gl, got_gl, keep_dn, got_dn)


def rounded(*parts):
    total = parts[0].astype(F32)
    for part in parts[1:]:
        total = total + part.astype(F32)
    return total.astype(BF16)


def fold_two_kernel(place_ref, g, gg, el, gl, d, d1, d2, d3, go_gl, st_gl, go_d, st_d):
    x_at, low = place_ref[0], place_ref[2] % 2
    for ref, at in ((go_gl, 1 - low), (st_gl, low)):
        for j in range(2):
            ref[0, j] = rounded(g[0, at, j], gg[0, at, j])
            ref[0, 2 + j] = rounded(el[0, at, j], gl[0, at, j])
    for ref, at in ((go_d, 1 - x_at), (st_d, x_at)):
        ref[0] = rounded(d[at, 0], d1[at, 0], d2[at, 0], d3[at, 0])


def fold_two(place, gates, lifts, downs):
    wide = pl.BlockSpec((1, 2, 2, 176, 512), lambda i, p: (i, 0, 0, 0, 0))
    down = pl.BlockSpec((2, 1, 2, 176, 256), lambda i, p: (0, i, 0, 0, 0))
    out = pl.BlockSpec((1, 4, 176, 512), lambda i, p: (i, 0, 0, 0))
    out_d = pl.BlockSpec((1, 2, 176, 256), lambda i, p: (i, 0, 0, 0))
    return pl.pallas_call(
        fold_two_kernel,
        grid_spec=pltpu.PrefetchScalarGridSpec(
            num_scalar_prefetch=1,
            grid=(2,),
            in_specs=[wide] * 4 + [down] * 4,
            out_specs=[out, out, out_d, out_d],
        ),
        out_shape=[struct((2, 4, 176, 512), BF16)] * 2 + [struct((2, 2, 176, 256), BF16)] * 2,
        compiler_params=params(60),
        cost_estimate=cost(1, 13 * MIB),
        name="fold_two",
    )(place, *[part.reshape(2, 2, 2, 176, 512) for part in (*gates, *lifts)], *downs)


def fold_pair_kernel(place_ref, a, ga, b, gb, go_a, st_a, go_b, st_b):
    x_at, row_at = place_ref[0], place_ref[1]
    for j in range(2):
        go_a[j, 0] = rounded(a[1 - x_at, j, 0], ga[1 - x_at, j, 0])
        st_a[j, 0] = rounded(a[x_at, j, 0], ga[x_at, j, 0])
        go_b[j, 0] = rounded(b[1 - row_at, j, 0], gb[1 - row_at, j, 0])
        st_b[j, 0] = rounded(b[row_at, j, 0], gb[row_at, j, 0])


def fold_pair(place, a, ga, b, gb):
    into = pl.BlockSpec((2, 2, 1, 128, 512), lambda i, p: (0, 0, i, 0, 0))
    out = pl.BlockSpec((2, 1, 128, 512), lambda i, p: (0, i, 0, 0))
    return pl.pallas_call(
        fold_pair_kernel,
        grid_spec=pltpu.PrefetchScalarGridSpec(
            num_scalar_prefetch=1, grid=(4,), in_specs=[into] * 4, out_specs=[out] * 4
        ),
        out_shape=[struct((2, 4, 128, 512), BF16)] * 4,
        compiler_params=params(60),
        cost_estimate=cost(1, 13 * MIB),
        name="fold_pair",
    )(place, a, ga, b, gb)


def placed(parts, axis):
    me, count = lax.axis_index(axis), len(parts)
    whole = jnp.zeros((count,) + parts[0].shape, parts[0].dtype)
    for shift, part in enumerate(parts):
        whole = lax.dynamic_update_index_in_dim(whole, part, lax.rem(me + count - shift, count), 0)
    return whole


def ring_gather(part, axis, count):
    parts = [part]
    for _ in range(1, count):
        parts.append(lax.ppermute(parts[-1], axis, [(i, (i + 1) % count) for i in range(count)]))
    return placed(parts, axis)


def added(parts):
    total = parts[0].astype(F32)
    for part in parts[1:]:
        total = total + part.astype(F32)
    return total.astype(BF16)


def tied(*groups):
    flat, tree = jax.tree.flatten(groups)
    return jax.tree.unflatten(tree, lax.optimization_barrier(flat))


def swap(part, axis, bit=1):
    return lax.ppermute(part, axis, [(i, i ^ bit) for i in range(lax.axis_size(axis))])


def piece_of(arrays, place, dim):
    return added([lax.dynamic_index_in_dim(array, place, dim, keepdims=False) for array in arrays])


def going(arrays, axis, dim):
    me, count = lax.axis_index(axis), lax.axis_size(axis)
    return [piece_of(arrays, lax.rem(me + shift, count), dim) for shift in range(1, count)]


def send(pieces, axis):
    count = lax.axis_size(axis)
    return [
        lax.ppermute(piece, axis, [(i, (i + shift) % count) for i in range(count)])
        for shift, piece in enumerate(pieces, 1)
    ]


def staying(arrays, axis, dim):
    return piece_of(arrays, lax.axis_index(axis), dim)


def share(part):
    return ring_gather(ring_gather(part, "x", 2), "core", 2)


def small_block(ddt, du, bias, g1, hg, g2):
    first = jnp.concatenate([ddt, jnp.pad(du, ((0, 0), (0, 512 - du.shape[1])))], axis=0)
    line = jnp.concatenate([jnp.pad(bias, (0, 64)), g1, jnp.pad(hg, (0, 96)), g2])
    return jnp.concatenate([first, line.reshape(1, 512), jnp.zeros((3, 512), first.dtype)], axis=0)


def per_device(
    layer_input,
    segment_ids,
    norm1_gain,
    query_weight,
    key_weight,
    value_weight,
    outgate_weight,
    decay_down,
    decay_up,
    decay_bias,
    head_gain,
    out_weight,
    norm2_gain,
    swiglu_gate,
    swiglu_up,
    swiglu_down,
    cotangent,
):
    row_count = lax.axis_size("row")
    col_count = lax.axis_size("col")
    fast = row_count == 2 and col_count == 4 and lax.axis_size("x") == 2
    core = lax.axis_index("core")
    quarter = lax.axis_index("x") * 2 + core

    if fast:
        feed_rows = jnp.concatenate(
            [
                jnp.concatenate(
                    [
                        lax.dynamic_slice_in_dim(swiglu_gate.T, quarter * 176, 176, 0),
                        lax.dynamic_slice_in_dim(swiglu_up.T, quarter * 176, 176, 0),
                    ],
                    axis=0,
                ),
                lax.dynamic_slice_in_dim(swiglu_down, quarter * 352, 352, 0),
            ],
            axis=1,
        )
        feed_full = lax.all_gather(feed_rows, AXES, axis=0, tiled=True).reshape(4, 2, 4, 352, 768)

        qk = jnp.concatenate([query_weight, key_weight], axis=1)
        qk = lax.dynamic_slice_in_dim(qk, core * 256, 256, 0)
        small = small_block(decay_down.T, decay_up, decay_bias, norm1_gain, head_gain, norm2_gain)
        qk = jnp.concatenate([qk, small[:, :256], small[:, 256:]], axis=0)
        v_part = lax.dynamic_slice_in_dim(value_weight, core * 256, 256, 0)
        by_col = ring_gather(qk, "col", col_count)
        v_full = ring_gather(ring_gather(v_part, "row", row_count), "col", col_count)
        ogout = jnp.concatenate([outgate_weight, out_weight], axis=1)
        ogout = lax.dynamic_slice_in_dim(ogout, core * 256, 256, 0)
        ogout, by_col = tied(ogout, by_col)
        ogout_cols = [ogout, *send([ogout] * (col_count - 1), "col")]
        qk_full = ring_gather(ring_gather(by_col, "row", row_count), "core", 2)
        v_full = ring_gather(v_full, "core", 2)
        small = jnp.concatenate([qk_full[0, :, :, 256:272], qk_full[0, :, :, 272:]], axis=-1)
        ddt = small[:, :, :4].reshape(2, LOW, 512)
        du = small[:, :, 4:12, :HK].transpose(0, 2, 1, 3).reshape(LOW, K)
        bias = small[:, :, 12, :64].reshape(1, K)
        g1 = small[:, :, 12, 128:256].reshape(1, D)
        hg = small[:, :, 12, 256:288].reshape(1, HV)
        g2 = small[:, :, 12, 384:].reshape(1, D)
    else:

        def whole(shard):
            if shard.ndim == 1:
                return lax.all_gather(shard, ("row", "col"), axis=0, tiled=True)
            wide = lax.all_gather(shard, "col", axis=1, tiled=True)
            return lax.all_gather(wide, "row", axis=0, tiled=True)

        def blocks(full, width):
            return full.reshape(2, 2, 256, 4, width).transpose(1, 0, 3, 2, 4)

        qk_full = jnp.concatenate([blocks(whole(query_weight), 128), blocks(whole(key_weight), 128)], axis=-1)
        v_full = blocks(whole(value_weight), 256).swapaxes(1, 2)
        ogout_full = jnp.concatenate([blocks(whole(outgate_weight), 256), blocks(whole(out_weight), 256)], axis=-1)
        gate_t, lift_t, down = whole(swiglu_gate).T, whole(swiglu_up).T, whole(swiglu_down)
        feed_gate = gate_t.reshape(4, 4, 176, 2, 512).transpose(1, 3, 0, 2, 4)
        feed_lift = lift_t.reshape(4, 4, 176, 2, 512).transpose(1, 3, 0, 2, 4)
        feed_down = down.reshape(2, 4, 352, 4, 256).transpose(1, 0, 3, 2, 4)
        feed_full = jnp.concatenate([jnp.concatenate([feed_gate, feed_lift], axis=3), feed_down], axis=-1)
        ddt = whole(decay_down).T.reshape(LOW, 2, 512).transpose(1, 0, 2)
        du = whole(decay_up)
        bias = whole(decay_bias).reshape(1, K)
        g1 = whole(norm1_gain).reshape(1, D)
        hg = whole(head_gain).reshape(1, HV)
        g2 = whole(norm2_gain).reshape(1, D)
    bias, g1, hg, g2 = (part.astype(F32) for part in (bias, g1, hg, g2))

    tokens = layer_input.shape[0]
    seg_c = segment_ids.reshape(tokens, 1)
    seg_r = segment_ids.reshape(tokens // CH, 1, CH)
    core_at = (core if fast else jnp.zeros_like(core)).astype(jnp.int32).reshape(1)

    normed, q, k, v, low, logit = project(layer_input, g1, qk_full, v_full, ddt, du, bias)
    if fast:
        q, ogout_cols = tied(q, ogout_cols)
        ogout = placed(ogout_cols, "col")
        other_row = swap(ogout, "row")
    mixed, states = attend(q, k, v, logit, segment_ids, seg_c, seg_r)
    if fast:
        mixed, other_row = tied(mixed, other_row)
        ogout = placed([ogout, other_row], "row")
        ogout_full = placed([ogout, swap(ogout, "core")], "core")
    og, gated, middle, normed_two = mix(layer_input, normed, mixed, ogout_full, hg, g2)
    layer_output, grad_normed_two, keep_gl, send_gl, keep_dn, send_dn = feed(
        core_at, normed_two, cotangent, middle, feed_full
    )
    grad_middle, branch, grad_og, grad_mixed, grad_g2, grad_hg = unmix(
        grad_normed_two, middle, cotangent, og, mixed, ogout_full, hg, g2
    )
    if fast:
        got_gl, got_dn = swap(send_gl, "core"), swap(send_dn, "core")
        x_at, row_at = lax.axis_index("x"), lax.axis_index("row")
        place = jnp.stack([x_at, row_at, lax.axis_index("col")]).astype(jnp.int32)
        go_g, st_g, go_l, st_l, st_d, *go_d = fold(place, keep_gl, got_gl, keep_dn, got_dn)
        branch, grad_og, go_g, go_l, go_d = tied(branch, grad_og, go_g, go_l, go_d)
        got_g, got_l, got_d = swap(go_g, "x"), swap(go_l, "row"), send(go_d, "col")
    keep_oo, send_oo = weight_grads(
        core_at, [normed, gated], [grad_og, branch], ((0, 0, (0,)), (1, 256, (1,))), True
    )
    if fast:
        grad_mixed, send_oo = tied(grad_mixed, send_oo)
        got_oo = swap(send_oo, "core")
    gq, gk, gv, glog = attend_back(q, k, v, logit, segment_ids, seg_c, seg_r, states, grad_mixed)
    keep_qkv, send_qkv = weight_grads(
        core_at, [normed], [gq, gk, gv], ((0, 0, (0, 1, 2)),)
    )
    if fast:
        send_qkv, got_g, got_l, got_d = tied(send_qkv, got_g, got_l, got_d)
        got_qkv = swap(send_qkv, "core")
        col_hi = lax.axis_index("col") // 2
        go_gl, st_gl, go_d, st_d = fold_two(place, [st_g, got_g], [st_l, got_l], [st_d, *got_d])
        go_qkv, st_qkv, go_oo, st_oo = fold_pair(place, keep_qkv, got_qkv, keep_oo, got_oo)
        glog, go_gl, go_d, go_qkv, go_oo = tied(glog, go_gl, go_d, go_qkv, go_oo)
        got_gl, got_d = swap(go_gl, "col"), swap(go_d, "x")
        got_qkv_x, got_oo_r = swap(go_qkv, "x"), swap(go_oo, "row")
    input_grad, grad_ddt, grad_du, grad_bias, grad_g1 = unproject(
        layer_input, normed, gq, gk, gv, glog, logit, low, grad_og, grad_middle, qk_full, v_full, ogout_full, ddt, du, g1
    )

    if fast:
        late = (got_gl, got_d, got_oo_r, got_qkv_x)
        input_grad, grad_g1, late = tied(input_grad, grad_g1, late)
        got_gl, got_d, got_oo_r, got_qkv_x = late
        qkv, oo, both = [st_qkv, got_qkv_x], [st_oo, got_oo_r], [st_gl, got_gl]
        go_qkv, go_oo, go_gl = piece_of(qkv, 1 - row_at, 0), piece_of(oo, 1 - x_at, 0), piece_of(both, 1 - col_hi, 0)
        go_qkv, go_oo, go_gl, grad_g1 = tied(go_qkv, go_oo, go_gl, grad_g1)
        qkv = [piece_of(qkv, row_at, 0), swap(go_qkv, "row")]
        oo = [piece_of(oo, x_at, 0), swap(go_oo, "x")]
        both = [piece_of(both, col_hi, 0), swap(go_gl, "col", 2)]
        tiny = jnp.concatenate(
            [
                grad_ddt.reshape(4, 4, 2, 512).transpose(2, 0, 1, 3),
                jnp.pad(grad_du.reshape(2, 8, 4, HK).transpose(0, 2, 1, 3), ((0, 0), (0, 0), (0, 0), (0, 384))),
                jnp.concatenate(
                    [
                        jnp.pad(grad_bias.reshape(2, 4, 64), ((0, 0), (0, 0), (0, 64))),
                        grad_g1.reshape(2, 4, 128),
                        jnp.pad(grad_hg.reshape(2, 4, 32), ((0, 0), (0, 0), (0, 96))),
                        grad_g2.reshape(2, 4, 128),
                    ],
                    axis=-1,
                ).reshape(2, 4, 1, 512),
                jnp.zeros((2, 4, 3, 512), F32),
            ],
            axis=2,
        )
        tiny = tiny + swap(tiny, "core")
        tiny = tiny + swap(tiny, "x")
        tiny = added([staying([tiny], "row", 0), *send(going([tiny], "row", 0), "row")])
        gate, lift = [[part[at : at + 2] for part in both] for at in (0, 2)]
        down = [st_d, got_d]
        gate = [piece_of(gate, row_at, 0), swap(piece_of(gate, 1 - row_at, 0), "row")]
        down = [piece_of(down, row_at, 0), swap(piece_of(down, 1 - row_at, 0), "row")]
        lift = [piece_of(lift, x_at, 0), swap(piece_of(lift, 1 - x_at, 0), "x")]
        down = added(down)
        feeds = share(jnp.concatenate([added(gate), added(lift), down[0], down[1]], axis=-1))
        rest = jnp.concatenate([added(qkv), added(oo)], axis=-1)
        rest = share(added([staying([rest], "col", 0), *send(going([rest], "col", 0), "col")]))
        tiny = added([staying([tiny], "col", 0), *send(going([tiny], "col", 0), "col")]).astype(F32)
        out_dd, out_du = tiny[:4].T, tiny[4:12, :HK]
        out_bias, out_g1, out_hg, out_g2 = tiny[12, :64], tiny[12, 128:256], tiny[12, 256:288], tiny[12, 384:]
    else:
        tiny = jnp.concatenate(
            [
                grad_ddt,
                jnp.pad(grad_du, ((0, 0), (0, D - K))),
                jnp.concatenate([grad_bias, grad_hg, jnp.zeros((1, D - K - HV), F32)], axis=1),
                grad_g1,
                grad_g2,
                jnp.zeros((5, D), F32),
            ],
            axis=0,
        )
        tiny = lax.psum(tiny, AXES)
        r, c = lax.axis_index("row"), lax.axis_index("col")

        def own(line, size):
            return lax.dynamic_slice_in_dim(line, (r * col_count + c) * size, size, 0)

        def own_block(full, shape):
            return lax.dynamic_slice(full, (r * shape[0], c * shape[1]), shape)

        out_bias = own(tiny[32, :K], decay_bias.shape[0])
        out_hg = own(tiny[32, K : K + HV], head_gain.shape[0])
        out_g1 = own(tiny[33], norm1_gain.shape[0])
        out_g2 = own(tiny[34], norm2_gain.shape[0])
        out_du = own_block(tiny[16:32, :K], decay_up.shape)
        down_rows = decay_down.shape
        out_dd = lax.dynamic_slice(tiny, (c * down_rows[1], r * down_rows[0]), down_rows[::-1]).T

    if fast:
        out_gate = feeds[..., :512].reshape(HC, 512).T
        out_lift = feeds[..., 512:1024].reshape(HC, 512).T
        out_down = jnp.stack([feeds[..., 1024:1280], feeds[..., 1280:]]).reshape(1408, 256)
        qkv = rest[..., :512].reshape(512, 512)
        oo = rest[..., 512:].reshape(512, 512)
        shards = [qkv[:, :128], qkv[:, 128:256], qkv[:, 256:], oo[:, :256], oo[:, 256:], out_gate, out_lift, out_down]
    else:

        def joined(keep, send):
            return jnp.stack([keep, send])

        keep_oo, send_oo = keep_oo.swapaxes(0, 1), send_oo.swapaxes(0, 1)

        def matrix(pack):
            return pack.transpose(2, 0, 1, 4, 3, 5).reshape(D, -1)

        oo = joined(keep_oo, send_oo)
        qkv = joined(keep_qkv, send_qkv)
        gl = joined(keep_gl, send_gl).reshape(2, 2, 2, 4, 2, 176, 512).transpose(4, 3, 0, 1, 5, 2, 6)
        gl = gl.reshape(2, FF, D)
        dn = joined(keep_dn, send_dn).transpose(2, 4, 0, 1, 5, 3, 6).reshape(FF, D)
        fulls = [
            matrix(qkv[..., :128]),
            matrix(qkv[..., 128:256]),
            matrix(qkv[..., 256:]),
            matrix(oo[..., :256]),
            matrix(oo[..., 256:]),
            gl[0].T,
            gl[1].T,
            dn,
        ]
        shards = []
        for full in fulls:
            part = lax.psum(full, ("x", "core"))
            part = lax.psum_scatter(part, "row", scatter_dimension=0, tiled=True)
            shards.append(lax.psum_scatter(part, "col", scatter_dimension=1, tiled=True))
    out_q, out_k, out_v, out_og, out_out, out_gate, out_lift, out_down = (part.astype(F32) for part in shards)
    return (
        layer_output,
        input_grad,
        out_g1,
        out_q,
        out_k,
        out_v,
        out_og,
        out_dd,
        out_du,
        out_bias,
        out_hg,
        out_out,
        out_g2,
        out_gate,
        out_lift,
        out_down,
    )


def solution(mesh):
    shape = dict(mesh.shape)
    finer = Mesh(mesh.devices.reshape(shape["dp"] // 2, 2, shape["row"], shape["col"]), AXES)
    tokens = P(AXES, None)
    vector = P(("row", "col"))
    matrix = P("row", "col")
    in_specs = (
        tokens, tokens, vector, matrix, matrix, matrix, matrix, matrix, matrix, vector, vector,
        matrix, vector, matrix, matrix, matrix, tokens,
    )
    out_specs = (
        tokens, tokens, vector, matrix, matrix, matrix, matrix, matrix, matrix, vector, vector,
        matrix, vector, matrix, matrix, matrix,
    )
    return jax.shard_map(per_device, mesh=finer, in_specs=in_specs, out_specs=out_specs, check_vma=False)
```

```python
import functools

import jax
import jax.numpy as jnp
from jax import lax
from jax.experimental import pallas as pl
from jax.experimental.pallas import tpu as pltpu
from jax.sharding import Mesh
from jax.sharding import PartitionSpec as P

HEADS = 4
HK = 128
HV = 256
CH = 64
LOW = 16
D = 1024
K = HEADS * HK
V = HEADS * HV
FF = 2816
HC = FF // 4
TILE = 256
FEED_TILE = 1024

EPS = 1e-05
HIGH = lax.Precision.HIGHEST
F32 = jnp.float32
BF16 = jnp.bfloat16
AXES = ("x", "core", "row", "col")
MIB = 1024 * 1024


def dot(left, right, precision=None):
    return jnp.dot(left, right, preferred_element_type=F32, precision=precision)


def dot_nt(left, right, precision=None):
    return lax.dot_general(
        left, right, (((1,), (1,)), ((), ())), preferred_element_type=F32, precision=precision
    )


def dot_tn(left, right, precision=None):
    return lax.dot_general(
        left, right, (((0,), (0,)), ((), ())), preferred_element_type=F32, precision=precision
    )


def halves(value):
    high = value.astype(BF16)
    return high, (value - high.astype(F32)).astype(BF16)


def struct(shape, dtype):
    return jax.ShapeDtypeStruct(shape, dtype)


def fixed(shape):
    return pl.BlockSpec(shape, lambda *i: (0,) * len(shape))


def rows(height, width):
    return pl.BlockSpec((height, width), lambda i: (i, 0))


def cost(flops, moved, trans=0):
    return pl.CostEstimate(flops=int(flops), bytes_accessed=int(moved), transcendentals=int(trans))


def params(mib):
    return pltpu.CompilerParams(vmem_limit_bytes=mib * MIB)


def project_kernel(x_ref, gain_ref, wqk_ref, wv_ref, ddt_ref, du_ref, bias_ref, n_ref, q_ref, k_ref, v_ref, low_ref, logit_ref):
    x = x_ref[...].astype(F32)
    inverse = lax.rsqrt(jnp.mean(x * x, axis=-1, keepdims=True) + EPS)
    normed = (x * inverse * gain_ref[...]).astype(BF16)
    n_ref[...] = normed
    for c in range(HEADS):
        wide = value = None
        for r in range(2):
            for core in range(2):
                at = r * 512 + core * 256
                part = dot(normed[:, at : at + 256], wqk_ref[core, r, c])
                wide = part if wide is None else wide + part
                part = dot(normed[:, at : at + 256], wv_ref[core, c, r])
                value = part if value is None else value + part
        q_ref[:, c * HK : (c + 1) * HK] = wide[:, :HK].astype(BF16)
        k_ref[:, c * HK : (c + 1) * HK] = wide[:, HK:].astype(BF16)
        v_ref[:, c * HV : (c + 1) * HV] = value.astype(BF16)
    low = dot_nt(normed[:, :512], ddt_ref[0]) + dot_nt(normed[:, 512:], ddt_ref[1])
    low_ref[...] = low
    high, rest = halves(low)
    du = du_ref[...]
    logit_ref[...] = dot(high, du) + dot(rest, du) + bias_ref[...]


def project(x, gain, qk_weights, v_weights, ddt, du, bias):
    tokens = x.shape[0]
    return pl.pallas_call(
        project_kernel,
        grid=(tokens // TILE,),
        in_specs=[
            rows(TILE, D),
            fixed((1, D)),
            fixed((2, 2, 4, 256, 256)),
            fixed((2, 4, 2, 256, 256)),
            fixed((2, LOW, 512)),
            fixed((LOW, K)),
            fixed((1, K)),
        ],
        out_specs=[rows(TILE, D), rows(TILE, K), rows(TILE, K), rows(TILE, V), rows(TILE, LOW), rows(TILE, K)],
        out_shape=[
            struct((tokens, D), BF16),
            struct((tokens, K), BF16),
            struct((tokens, K), BF16),
            struct((tokens, V), BF16),
            struct((tokens, LOW), F32),
            struct((tokens, K), F32),
        ],
        compiler_params=params(60),
        cost_estimate=cost(2 * tokens * D * 2048, 14 * MIB),
        name="project",
    )(x, gain, qk_weights, v_weights, ddt, du, bias)


def span_parts(logit, doc_c, doc_r, last_doc, prev_doc):
    lower = lax.broadcasted_iota(jnp.int32, (CH, CH), 0) >= lax.broadcasted_iota(jnp.int32, (CH, CH), 1)
    mask = jnp.where(lower & (doc_c == doc_r), HK ** (-0.5), 0.0)
    log_decay = (jnp.minimum(logit, 0.0) - jnp.log1p(jnp.exp(-jnp.abs(logit)))) * (1.0 / 16.0)
    cumul = dot(lower.astype(F32), log_decay, HIGH)
    centre = cumul[CH // 2 - 1 : CH // 2]
    last = cumul[CH - 1 :]
    rise = jnp.exp(cumul - centre)
    fall = jnp.exp(centre - cumul)
    growth = jnp.exp(cumul)
    to_end = jnp.exp(last - cumul)
    enter = jnp.where(doc_c == prev_doc, HK ** (-0.5), 0.0)
    same = jnp.where(doc_c == last_doc, 1.0, 0.0)
    return mask, rise, fall, growth, to_end, enter, same, jnp.exp(last)


def span_docs(seg_ref, at, first):
    last_doc = seg_ref[at + CH - 1]
    prev_doc = jnp.where(first, -1, seg_ref[jnp.maximum(at - 1, 0)])
    return last_doc, prev_doc


def attend_kernel(spans, seg_ref, q_ref, k_ref, v_ref, logit_ref, dc_ref, dr_ref, mixed_ref, states_ref, state):
    i = pl.program_id(1)
    at = (pl.program_id(0) * spans + i) * CH
    last_doc, prev_doc = span_docs(seg_ref, at, i == 0)

    @pl.when(i == 0)
    def _():
        state[...] = jnp.zeros_like(state)

    mask, rise, fall, growth, to_end, enter, same, keep = span_parts(
        logit_ref[...], dc_ref[...], dr_ref[0], last_doc, prev_doc
    )
    query = q_ref[...].astype(F32)
    keys = k_ref[...].astype(F32)
    qs = (query * rise).astype(BF16)
    ks = (keys * fall).astype(BF16)
    qg = (query * growth * enter).astype(BF16)
    kw = (keys * to_end * same).astype(BF16)
    keep = keep * jnp.where(last_doc == prev_doc, 1.0, 0.0)
    for h in range(HEADS):
        a, b = h * HK, (h + 1) * HK
        va = v_ref[:, h * HV : (h + 1) * HV]
        now = state[h]
        low = now.astype(BF16)
        states_ref[0, h] = low
        scores = (dot_nt(qs[:, a:b], ks[:, a:b]) * mask).astype(BF16)
        mixed_ref[:, h * HV : (h + 1) * HV] = dot(scores, va) + dot_nt(qg[:, a:b], low)
        state[h] = now * keep[:, a:b] + dot_tn(va, kw[:, a:b])


def attend(q, k, v, logit, segs, seg_c, seg_r):
    tokens = q.shape[0]
    seqs = segs.shape[0]
    spans = tokens // seqs // CH

    def part(width):
        return pl.BlockSpec((CH, width), lambda s, i, seg: (s * spans + i, 0))

    return pl.pallas_call(
        functools.partial(attend_kernel, spans),
        grid_spec=pltpu.PrefetchScalarGridSpec(
            num_scalar_prefetch=1,
            grid=(seqs, spans),
            in_specs=[
                part(K),
                part(K),
                part(V),
                part(K),
                part(1),
                pl.BlockSpec((1, 1, CH), lambda s, i, seg: (s * spans + i, 0, 0)),
            ],
            out_specs=[
                part(V),
                pl.BlockSpec((1, HEADS, HV, HK), lambda s, i, seg: (s * spans + i, 0, 0, 0)),
            ],
            scratch_shapes=[pltpu.VMEM((HEADS, HV, HK), F32)],
        ),
        out_shape=[struct((tokens, V), F32), struct((seqs * spans, HEADS, HV, HK), BF16)],
        compiler_params=params(32),
        cost_estimate=cost(2e10, 16 * MIB),
        name="attend",
    )(segs.reshape(-1), q, k, v, logit, seg_c, seg_r)


def attend_back_kernel(
    spans, seg_ref, q_ref, k_ref, v_ref, logit_ref, dc_ref, dr_ref, states_ref, g_ref,
    gq_ref, gk_ref, gv_ref, gl_ref, grad_state,
):
    i = spans - 1 - pl.program_id(1)
    at = (pl.program_id(0) * spans + i) * CH
    last_doc, prev_doc = span_docs(seg_ref, at, i == 0)

    @pl.when(pl.program_id(1) == 0)
    def _():
        grad_state[...] = jnp.zeros_like(grad_state)

    mask, rise, fall, growth, to_end, enter, same, keep = span_parts(
        logit_ref[...], dc_ref[...], dr_ref[0], last_doc, prev_doc
    )
    query = q_ref[...].astype(F32)
    keys = k_ref[...].astype(F32)
    qs = (query * rise).astype(BF16)
    ks = (keys * fall).astype(BF16)
    qg = (query * growth * enter).astype(BF16)
    kw = (keys * to_end * same).astype(BF16)
    keep = keep * jnp.where(last_doc == prev_doc, 1.0, 0.0)
    last_row = lax.broadcasted_iota(jnp.int32, (CH, HK), 0) == CH - 1
    upper = lax.broadcasted_iota(jnp.int32, (CH, CH), 0) <= lax.broadcasted_iota(jnp.int32, (CH, CH), 1)
    upper = upper.astype(F32)
    for h in range(HEADS):
        a, b = h * HK, (h + 1) * HK
        va = v_ref[:, h * HV : (h + 1) * HV]
        ga = g_ref[:, h * HV : (h + 1) * HV]
        qh, kh = qs[:, a:b], ks[:, a:b]
        state = states_ref[0, h]
        grad = grad_state[h]
        grad_low = grad.astype(BF16)
        scores = (dot_nt(qh, kh) * mask).astype(BF16)
        grad_scores = (dot_nt(ga, va) * mask).astype(BF16)
        gv_ref[:, h * HV : (h + 1) * HV] = (dot_tn(scores, ga) + dot_nt(kw[:, a:b], grad_low)).astype(BF16)
        wk = dot(va, grad_low) * same * to_end[:, a:b]
        wq = dot(ga, state) * enter * growth[:, a:b]
        query_inner = dot(grad_scores, kh)
        key_inner = dot_tn(grad_scores, qh)
        gq_ref[:, a:b] = (query_inner * rise[:, a:b] + wq).astype(BF16)
        gk_ref[:, a:b] = (key_inner * fall[:, a:b] + wk).astype(BF16)
        ends = wk * keys[:, a:b]
        grad_cumul = qh.astype(F32) * query_inner - kh.astype(F32) * key_inner + query[:, a:b] * wq - ends
        kept = grad * keep[:, a:b]
        at_last = jnp.sum(ends, axis=0, keepdims=True) + jnp.sum(kept * state.astype(F32), axis=0, keepdims=True)
        grad_cumul = grad_cumul + jnp.where(last_row, at_last, 0.0)
        gl_ref[:, a:b] = dot(upper, grad_cumul, HIGH)
        grad_state[h] = kept + dot_tn(ga, qg[:, a:b])


def attend_back(q, k, v, logit, segs, seg_c, seg_r, states, grad):
    tokens = q.shape[0]
    seqs = segs.shape[0]
    spans = tokens // seqs // CH

    def part(width):
        return pl.BlockSpec((CH, width), lambda s, i, seg: (s * spans + spans - 1 - i, 0))

    return pl.pallas_call(
        functools.partial(attend_back_kernel, spans),
        grid_spec=pltpu.PrefetchScalarGridSpec(
            num_scalar_prefetch=1,
            grid=(seqs, spans),
            in_specs=[
                part(K),
                part(K),
                part(V),
                part(K),
                part(1),
                pl.BlockSpec((1, 1, CH), lambda s, i, seg: (s * spans + spans - 1 - i, 0, 0)),
                pl.BlockSpec((1, HEADS, HV, HK), lambda s, i, seg: (s * spans + spans - 1 - i, 0, 0, 0)),
                part(V),
            ],
            out_specs=[part(K), part(K), part(V), part(K)],
            scratch_shapes=[pltpu.VMEM((HEADS, HV, HK), F32)],
        ),
        out_shape=[
            struct((tokens, K), BF16),
            struct((tokens, K), BF16),
            struct((tokens, V), BF16),
            struct((tokens, K), F32),
        ],
        compiler_params=params(32),
        cost_estimate=cost(1, 1),
        name="attend_back",
    )(segs.reshape(-1), q, k, v, logit, seg_c, seg_r, states, grad)


def mix_kernel(x_ref, n_ref, mixed_ref, w_ref, hg_ref, g2_ref, og_ref, gated_ref, middle_ref, n2_ref):
    normed = n_ref[...]
    outs = [None] * 4
    for c in range(HEADS):
        og = None
        for r in range(2):
            for core in range(2):
                at = r * 512 + core * 256
                part = dot(normed[:, at : at + 256], w_ref[core, r, c, :, :HV])
                og = part if og is None else og + part
        og_ref[:, c * HV : (c + 1) * HV] = og
        mixed = mixed_ref[:, c * HV : (c + 1) * HV]
        inverse = lax.rsqrt(jnp.mean(mixed * mixed, axis=-1, keepdims=True) + EPS)
        gated = (mixed * inverse * hg_ref[...] * (og * jax.nn.sigmoid(og))).astype(BF16)
        gated_ref[:, c * HV : (c + 1) * HV] = gated
        for e in range(4):
            part = dot(gated, w_ref[c % 2, c // 2, e, :, HV:])
            outs[e] = part if outs[e] is None else outs[e] + part
    middle = x_ref[...].astype(F32) + jnp.concatenate(outs, axis=1)
    middle_ref[...] = middle
    inverse = lax.rsqrt(jnp.mean(middle * middle, axis=-1, keepdims=True) + EPS)
    n2_ref[...] = (middle * inverse * g2_ref[...]).astype(BF16)


def mix(x, normed, mixed, weights, head_gain, gain_two):
    tokens = x.shape[0]
    return pl.pallas_call(
        mix_kernel,
        grid=(tokens // TILE,),
        in_specs=[
            rows(TILE, D),
            rows(TILE, D),
            rows(TILE, V),
            fixed((2, 2, 4, 256, 512)),
            fixed((1, HV)),
            fixed((1, D)),
        ],
        out_specs=[rows(TILE, V), rows(TILE, V), rows(TILE, D), rows(TILE, D)],
        out_shape=[
            struct((tokens, V), F32),
            struct((tokens, V), BF16),
            struct((tokens, D), F32),
            struct((tokens, D), BF16),
        ],
        compiler_params=params(60),
        cost_estimate=cost(2 * tokens * D * 2048, 24 * MIB),
        name="mix",
    )(x, normed, mixed, weights, head_gain, gain_two)


def feed_kernel(
    core_ref, n2_ref, dy_ref, middle_ref, gl_ref, dn_ref,
    out_ref, gn_ref, keep_gl, send_gl, keep_dn, send_dn, y_acc, hid, gate_g, lift_g,
):
    step = pl.program_id(0)

    @pl.when(step == 0)
    def _():
        y_acc[...] = middle_ref[...]
        gn_ref[...] = jnp.zeros_like(gn_ref)

    @pl.loop(0, n2_ref.shape[0] // FEED_TILE)
    def _(t):
        at = pl.ds(pl.multiple_of(t * FEED_TILE, FEED_TILE), FEED_TILE)
        gate = lift = back = None
        for r in range(2):
            n2 = n2_ref[at, r * 512 : (r + 1) * 512]
            a = dot_nt(n2, gl_ref[:, r, 0, :176].reshape(HC, 512))
            b = dot_nt(n2, gl_ref[:, r, 0, 176:].reshape(HC, 512))
            gate = a if r == 0 else gate + a
            lift = b if r == 0 else lift + b
        for c in range(4):
            a = dot_nt(dy_ref[at, c * 256 : (c + 1) * 256], dn_ref[:, 0, c].reshape(HC, 256))
            back = a if c == 0 else back + a
        sig = jax.nn.sigmoid(gate)
        swish = gate * sig
        hidden = (swish * lift).astype(BF16)
        grad_lift = (back * swish).astype(BF16)
        grad_gate = (back * lift * sig * (1.0 + gate * (1.0 - sig))).astype(BF16)
        hid[at, :] = hidden
        gate_g[at, :] = grad_gate
        lift_g[at, :] = grad_lift
        for c in range(4):
            lanes = slice(c * 256, (c + 1) * 256)
            y_acc[at, lanes] += dot(hidden, dn_ref[:, 0, c].reshape(HC, 256))
        for r in range(2):
            lanes = slice(r * 512, (r + 1) * 512)
            gn_ref[at, lanes] += dot(grad_gate, gl_ref[:, r, 0, :176].reshape(HC, 512)) + dot(
                grad_lift, gl_ref[:, r, 0, 176:].reshape(HC, 512)
            )

    @pl.when(step == 3)
    def _():
        out_ref[...] = y_acc[...].astype(BF16)

    first = core_ref[0] == 0
    for m, (source, right) in enumerate(((gate_g, n2_ref), (lift_g, n2_ref), (hid, dy_ref))):
        both = dot_tn(source[...], right[...]).astype(BF16)
        low, high = both[: HC // 2], both[HC // 2 :]
        mine = jnp.where(first, low, high)
        other = jnp.where(first, high, low)
        for part, gl_out, dn_out in ((mine, keep_gl, keep_dn), (other, send_gl, send_dn)):
            for x in range(2):
                piece = part[x * 176 : (x + 1) * 176]
                if m < 2:
                    for r in range(2):
                        gl_out[x, r, 0, m * 176 : (m + 1) * 176] = piece[:, r * 512 : (r + 1) * 512]
                else:
                    for c in range(4):
                        dn_out[x, 0, c, 0] = piece[:, c * 256 : (c + 1) * 256]


def feed(core, n2, dy, middle, weights):
    tokens = n2.shape[0]
    gl = pl.BlockSpec((2, 2, 1, 352, 512), lambda i, c: (0, 0, i, 0, 0))
    dn = pl.BlockSpec((2, 1, 4, 1, 176, 256), lambda i, c: (0, i // 2, 0, i % 2, 0, 0))
    once = pl.Buffered(1)
    return pl.pallas_call(
        feed_kernel,
        grid_spec=pltpu.PrefetchScalarGridSpec(
            num_scalar_prefetch=1,
            grid=(4,),
            in_specs=[
                pl.BlockSpec((tokens, D), lambda i, c: (0, 0), pipeline_mode=once),
                pl.BlockSpec((tokens, D), lambda i, c: (0, 0), pipeline_mode=once),
                pl.BlockSpec((tokens, D), lambda i, c: (0, 0), pipeline_mode=once),
                pl.BlockSpec((4, 2, 1, 352, 512), lambda i, c: (0, 0, i, 0, 0)),
                pl.BlockSpec((2, 1, 4, 352, 256), lambda i, c: (i % 2, i // 2, 0, 0, 2)),
            ],
            out_specs=[
                pl.BlockSpec((tokens, D), lambda i, c: (0, 0), pipeline_mode=once),
                pl.BlockSpec((tokens, D), lambda i, c: (0, 0), pipeline_mode=once),
                gl,
                gl,
                dn,
                dn,
            ],
            scratch_shapes=[
                pltpu.VMEM((tokens, D), F32),
                pltpu.VMEM((tokens, HC), BF16),
                pltpu.VMEM((tokens, HC), BF16),
                pltpu.VMEM((tokens, HC), BF16),
            ],
        ),
        out_shape=[
            struct((tokens, D), BF16),
            struct((tokens, D), F32),
            struct((2, 2, 4, 352, 512), BF16),
            struct((2, 2, 4, 352, 512), BF16),
            struct((2, 2, 4, 2, 176, 256), BF16),
            struct((2, 2, 4, 2, 176, 256), BF16),
        ],
        compiler_params=params(60),
        cost_estimate=cost(18 * tokens * D * FF, 60 * MIB),
        name="feed",
    )(core, n2, dy, middle, weights, weights)


def unmix_kernel(
    gn_ref, middle_ref, dy_ref, og_ref, mixed_ref, w_ref, hg_ref, g2_ref,
    gm_ref, gb_ref, gog_ref, gmix_ref, gg2_ref, ghg_ref,
):
    @pl.when(pl.program_id(0) == 0)
    def _():
        gg2_ref[...] = jnp.zeros_like(gg2_ref)
        ghg_ref[...] = jnp.zeros_like(ghg_ref)

    grad = gn_ref[...]
    middle = middle_ref[...]
    inverse = lax.rsqrt(jnp.mean(middle * middle, axis=-1, keepdims=True) + EPS)
    unit = middle * inverse
    gg2_ref[...] += jnp.sum(grad * unit, axis=0, keepdims=True)
    scaled = grad * g2_ref[...]
    grad_middle = dy_ref[...].astype(F32) + inverse * (scaled - unit * jnp.mean(scaled * unit, axis=-1, keepdims=True))
    gm_ref[...] = grad_middle
    branch = grad_middle.astype(BF16)
    gb_ref[...] = branch
    head_gain = hg_ref[...]
    for c in range(HEADS):
        lanes = slice(c * HV, (c + 1) * HV)
        back = None
        for e in range(4):
            part = dot_nt(branch[:, e * 256 : (e + 1) * 256], w_ref[c % 2, c // 2, e, :, HV:])
            back = part if back is None else back + part
        og = og_ref[:, lanes]
        sig = jax.nn.sigmoid(og)
        mixed = mixed_ref[:, lanes]
        inv = lax.rsqrt(jnp.mean(mixed * mixed, axis=-1, keepdims=True) + EPS)
        unit = mixed * inv
        gog_ref[:, lanes] = (back * (unit * head_gain) * sig * (1.0 + og * (1.0 - sig))).astype(BF16)
        incoming = back * (og * sig)
        ghg_ref[...] += jnp.sum(incoming * unit, axis=0, keepdims=True)
        scaled = incoming * head_gain
        gmix_ref[:, lanes] = (inv * (scaled - unit * jnp.mean(scaled * unit, axis=-1, keepdims=True))).astype(BF16)


def unmix(grad, middle, dy, og, mixed, weights, head_gain, gain_two):
    tokens = grad.shape[0]
    return pl.pallas_call(
        unmix_kernel,
        grid=(tokens // TILE,),
        in_specs=[
            rows(TILE, D),
            rows(TILE, D),
            rows(TILE, D),
            rows(TILE, V),
            rows(TILE, V),
            fixed((2, 2, 4, 256, 512)),
            fixed((1, HV)),
            fixed((1, D)),
        ],
        out_specs=[rows(TILE, D), rows(TILE, D), rows(TILE, V), rows(TILE, V), fixed((1, D)), fixed((1, HV))],
        out_shape=[
            struct((tokens, D), F32),
            struct((tokens, D), BF16),
            struct((tokens, V), BF16),
            struct((tokens, V), BF16),
            struct((1, D), F32),
            struct((1, HV), F32),
        ],
        compiler_params=params(60),
        cost_estimate=cost(2 * tokens * D * D, 30 * MIB),
        name="unmix",
    )(grad, middle, dy, og, mixed, weights, head_gain, gain_two)


def weight_grad_kernel(plan, row_first, core_ref, *refs):
    count = 2 * len(plan)
    keep_ref, send_ref = refs[-2:]
    lefts, rights = refs[:count], refs[count:-2]
    for lefts_at, start, indices in plan:
        right = [rights[index][...] for index in indices]
        right = right[0] if len(right) == 1 else jnp.concatenate(right, axis=1)
        left = jnp.concatenate([lefts[2 * lefts_at][...], lefts[2 * lefts_at + 1][...]], axis=1)
        both = dot_tn(left, right).astype(BF16)
        for ref, part in ((keep_ref, both[:256]), (send_ref, both[256:])):
            for x in range(2):
                at = (0, x, 0) if row_first else (x, 0, 0)
                ref[(*at, slice(None), slice(start, start + right.shape[1]))] = part[x * 128 : (x + 1) * 128]


def weight_grads(core, lefts, rights, plan, row_first=False):
    tokens = lefts[0].shape[0]
    specs = []
    for left in lefts:
        specs.append(pl.BlockSpec((tokens, 256), lambda r, c, core: (0, r * 2 + core[0])))
        specs.append(pl.BlockSpec((tokens, 256), lambda r, c, core: (0, r * 2 + 1 - core[0])))
    for right in rights:
        specs.append(pl.BlockSpec((tokens, right.shape[1] // 4), lambda r, c, core: (0, c)))
    if row_first:
        out = pl.BlockSpec((1, 2, 1, 128, 512), lambda r, c, core: (r, 0, c, 0, 0))
    else:
        out = pl.BlockSpec((2, 1, 1, 128, 512), lambda r, c, core: (0, r, c, 0, 0))
    operands = [left for left in lefts for _ in range(2)] + list(rights)
    return pl.pallas_call(
        functools.partial(weight_grad_kernel, plan, row_first),
        grid_spec=pltpu.PrefetchScalarGridSpec(
            num_scalar_prefetch=1, grid=(2, 4), in_specs=specs, out_specs=[out, out]
        ),
        out_shape=[struct((2, 2, 4, 128, 512), BF16)] * 2,
        compiler_params=params(40),
        cost_estimate=cost(1, 1),
        name="weight_grads",
    )(core, *operands)


def unproject_kernel(
    x_ref, n_ref, gq_ref, gk_ref, gv_ref, glog_ref, logit_ref, low_ref, gog_ref, gm_ref,
    wqk_ref, wv_ref, wo_ref, ddt_ref, du_ref, g1_ref,
    gx_ref, gddt_ref, gdu_ref, gbias_ref, gg1_ref,
):
    @pl.when(pl.program_id(0) == 0)
    def _():
        gddt_ref[...] = jnp.zeros_like(gddt_ref)
        gdu_ref[...] = jnp.zeros_like(gdu_ref)
        gbias_ref[...] = jnp.zeros_like(gbias_ref)
        gg1_ref[...] = jnp.zeros_like(gg1_ref)

    normed = n_ref[...]
    grad_logit = glog_ref[...] * (1.0 / 16.0) * jax.nn.sigmoid(-logit_ref[...])
    gbias_ref[...] += jnp.sum(grad_logit, axis=0, keepdims=True)
    high, rest = halves(grad_logit)
    low, low_rest = halves(low_ref[...])
    gdu_ref[...] += dot_tn(low, high) + dot_tn(low, rest) + dot_tn(low_rest, high)
    du = du_ref[...]
    grad_low = (dot_nt(high, du) + dot_nt(rest, du)).astype(BF16)
    gddt_ref[...] += dot_tn(grad_low, normed)
    lefts = [
        jnp.concatenate(
            [
                gq_ref[:, c * HK : (c + 1) * HK],
                gk_ref[:, c * HK : (c + 1) * HK],
            ],
            axis=1,
        )
        for c in range(HEADS)
    ]
    parts = []
    for r in range(2):
        small = dot(grad_low, ddt_ref[r])
        for core in range(2):
            total = small[:, core * 256 : (core + 1) * 256]
            for c in range(HEADS):
                total = total + dot_nt(lefts[c], wqk_ref[core, r, c])
                total = total + dot_nt(gv_ref[:, c * HV : (c + 1) * HV], wv_ref[core, c, r])
                total = total + dot_nt(gog_ref[:, c * HV : (c + 1) * HV], wo_ref[core, r, c])
            parts.append(total)
    grad = jnp.concatenate(parts, axis=1)
    x = x_ref[...].astype(F32)
    inverse = lax.rsqrt(jnp.mean(x * x, axis=-1, keepdims=True) + EPS)
    unit = x * inverse
    gg1_ref[...] += jnp.sum(grad * unit, axis=0, keepdims=True)
    scaled = grad * g1_ref[...]
    gx_ref[...] = gm_ref[...] + inverse * (scaled - unit * jnp.mean(scaled * unit, axis=-1, keepdims=True))


def unproject(x, normed, gq, gk, gv, glog, logit, low, gog, gm, qk_weights, v_weights, out_weights, ddt, du, gain):
    tokens = x.shape[0]
    return pl.pallas_call(
        unproject_kernel,
        grid=(tokens // TILE,),
        in_specs=[
            rows(TILE, D),
            rows(TILE, D),
            rows(TILE, K),
            rows(TILE, K),
            rows(TILE, V),
            rows(TILE, K),
            rows(TILE, K),
            rows(TILE, LOW),
            rows(TILE, V),
            rows(TILE, D),
            fixed((2, 2, 4, 256, 256)),
            fixed((2, 4, 2, 256, 256)),
            fixed((2, 2, 4, 256, HV)),
            fixed((2, LOW, 512)),
            fixed((LOW, K)),
            fixed((1, D)),
        ],
        out_specs=[rows(TILE, D), fixed((LOW, D)), fixed((LOW, K)), fixed((1, K)), fixed((1, D))],
        out_shape=[
            struct((tokens, D), F32),
            struct((LOW, D), F32),
            struct((LOW, K), F32),
            struct((1, K), F32),
            struct((1, D), F32),
        ],
        compiler_params=params(60),
        cost_estimate=cost(2 * tokens * D * 3072, 100 * MIB),
        name="unproject",
    )(x, normed, gq, gk, gv, glog, logit, low, gog, gm, qk_weights, v_weights, out_weights, ddt, du, gain)


def fold_kernel(place_ref, keep_gl, got_gl, keep_dn, got_dn, go_g, st_g, go_l, st_l, *downs):
    i = pl.program_id(0)
    x_at, row_at = place_ref[0], place_ref[1]

    def both(left, right):
        return (left.astype(F32) + right.astype(F32)).astype(BF16)

    for r in range(2):
        for ref, x in ((go_g, 1 - x_at), (st_g, x_at)):
            ref[0, r] = both(keep_gl[x, r, 0, :176], got_gl[x, r, 0, :176])
    for x in range(2):
        for ref, r in ((go_l, 1 - row_at), (st_l, row_at)):
            ref[0, x] = both(keep_gl[x, r, 0, 176:], got_gl[x, r, 0, 176:])
    for shift in range(4):

        @pl.when(i == shift)
        def _():
            downs[shift][...] = both(keep_dn[:, :, 0], got_dn[:, :, 0])


def fold(place, keep_gl, got_gl, keep_dn, got_dn):
    gl = pl.BlockSpec((2, 2, 1, 352, 512), lambda i, p: (0, 0, i, 0, 0))
    dn = pl.BlockSpec((2, 2, 1, 2, 176, 256), lambda i, p: (0, 0, lax.rem(p[2] + i, 4), 0, 0, 0))
    out = pl.BlockSpec((1, 2, 176, 512), lambda i, p: (i, 0, 0, 0))
    down = pl.BlockSpec((2, 2, 2, 176, 256), lambda i, p: (0, 0, 0, 0, 0))
    return pl.pallas_call(
        fold_kernel,
        grid_spec=pltpu.PrefetchScalarGridSpec(
            num_scalar_prefetch=1,
            grid=(4,),
            in_specs=[gl, gl, dn, dn],
            out_specs=[out] * 4 + [down] * 4,
        ),
        out_shape=[struct((4, 2, 176, 512), BF16)] * 4 + [struct((2, 2, 2, 176, 256), BF16)] * 4,
        compiler_params=params(60),
        cost_estimate=cost(1, 26 * MIB),
        name="fold",
    )(place, keep_gl, got_gl, keep_dn, got_dn)


def rounded(*parts):
    total = parts[0].astype(F32)
    for part in parts[1:]:
        total = total + part.astype(F32)
    return total.astype(BF16)


def fold_two_kernel(place_ref, g, gg, el, gl, d, d1, d2, d3, go_gl, st_gl, go_d, st_d):
    x_at, low = place_ref[0], place_ref[2] % 2
    for ref, at in ((go_gl, 1 - low), (st_gl, low)):
        for j in range(2):
            ref[0, j] = rounded(g[0, at, j], gg[0, at, j])
            ref[0, 2 + j] = rounded(el[0, at, j], gl[0, at, j])
    for ref, at in ((go_d, 1 - x_at), (st_d, x_at)):
        ref[0] = rounded(d[at, 0], d1[at, 0], d2[at, 0], d3[at, 0])


def fold_two(place, gates, lifts, downs):
    wide = pl.BlockSpec((1, 2, 2, 176, 512), lambda i, p: (i, 0, 0, 0, 0))
    down = pl.BlockSpec((2, 1, 2, 176, 256), lambda i, p: (0, i, 0, 0, 0))
    out = pl.BlockSpec((1, 4, 176, 512), lambda i, p: (i, 0, 0, 0))
    out_d = pl.BlockSpec((1, 2, 176, 256), lambda i, p: (i, 0, 0, 0))
    return pl.pallas_call(
        fold_two_kernel,
        grid_spec=pltpu.PrefetchScalarGridSpec(
            num_scalar_prefetch=1,
            grid=(2,),
            in_specs=[wide] * 4 + [down] * 4,
            out_specs=[out, out, out_d, out_d],
        ),
        out_shape=[struct((2, 4, 176, 512), BF16)] * 2 + [struct((2, 2, 176, 256), BF16)] * 2,
        compiler_params=params(60),
        cost_estimate=cost(1, 13 * MIB),
        name="fold_two",
    )(place, *[part.reshape(2, 2, 2, 176, 512) for part in (*gates, *lifts)], *downs)


def fold_pair_kernel(place_ref, a, ga, b, gb, go_a, st_a, go_b, st_b):
    x_at, row_at = place_ref[0], place_ref[1]
    for j in range(2):
        go_a[j, 0] = rounded(a[1 - x_at, j, 0], ga[1 - x_at, j, 0])
        st_a[j, 0] = rounded(a[x_at, j, 0], ga[x_at, j, 0])
        go_b[j, 0] = rounded(b[1 - row_at, j, 0], gb[1 - row_at, j, 0])
        st_b[j, 0] = rounded(b[row_at, j, 0], gb[row_at, j, 0])


def fold_pair(place, a, ga, b, gb):
    into = pl.BlockSpec((2, 2, 1, 128, 512), lambda i, p: (0, 0, i, 0, 0))
    out = pl.BlockSpec((2, 1, 128, 512), lambda i, p: (0, i, 0, 0))
    return pl.pallas_call(
        fold_pair_kernel,
        grid_spec=pltpu.PrefetchScalarGridSpec(
            num_scalar_prefetch=1, grid=(4,), in_specs=[into] * 4, out_specs=[out] * 4
        ),
        out_shape=[struct((2, 4, 128, 512), BF16)] * 4,
        compiler_params=params(60),
        cost_estimate=cost(1, 13 * MIB),
        name="fold_pair",
    )(place, a, ga, b, gb)


def placed(parts, axis):
    me, count = lax.axis_index(axis), len(parts)
    whole = jnp.zeros((count,) + parts[0].shape, parts[0].dtype)
    for shift, part in enumerate(parts):
        whole = lax.dynamic_update_index_in_dim(whole, part, lax.rem(me + count - shift, count), 0)
    return whole


def ring_gather(part, axis, count):
    parts = [part]
    for _ in range(1, count):
        parts.append(lax.ppermute(parts[-1], axis, [(i, (i + 1) % count) for i in range(count)]))
    return placed(parts, axis)


def added(parts):
    total = parts[0].astype(F32)
    for part in parts[1:]:
        total = total + part.astype(F32)
    return total.astype(BF16)


def tied(*groups):
    flat, tree = jax.tree.flatten(groups)
    return jax.tree.unflatten(tree, lax.optimization_barrier(flat))


def swap(part, axis, bit=1):
    return lax.ppermute(part, axis, [(i, i ^ bit) for i in range(lax.axis_size(axis))])


def piece_of(arrays, place, dim):
    return added([lax.dynamic_index_in_dim(array, place, dim, keepdims=False) for array in arrays])


def going(arrays, axis, dim):
    me, count = lax.axis_index(axis), lax.axis_size(axis)
    return [piece_of(arrays, lax.rem(me + shift, count), dim) for shift in range(1, count)]


def send(pieces, axis):
    count = lax.axis_size(axis)
    return [
        lax.ppermute(piece, axis, [(i, (i + shift) % count) for i in range(count)])
        for shift, piece in enumerate(pieces, 1)
    ]


def staying(arrays, axis, dim):
    return piece_of(arrays, lax.axis_index(axis), dim)


def share(part):
    return ring_gather(ring_gather(part, "x", 2), "core", 2)


def small_block(ddt, du, bias, g1, hg, g2):
    first = jnp.concatenate([ddt, jnp.pad(du, ((0, 0), (0, 512 - du.shape[1])))], axis=0)
    line = jnp.concatenate([jnp.pad(bias, (0, 64)), g1, jnp.pad(hg, (0, 96)), g2])
    return jnp.concatenate([first, line.reshape(1, 512), jnp.zeros((3, 512), first.dtype)], axis=0)


def per_device(
    layer_input,
    segment_ids,
    norm1_gain,
    query_weight,
    key_weight,
    value_weight,
    outgate_weight,
    decay_down,
    decay_up,
    decay_bias,
    head_gain,
    out_weight,
    norm2_gain,
    swiglu_gate,
    swiglu_up,
    swiglu_down,
    cotangent,
):
    row_count = lax.axis_size("row")
    col_count = lax.axis_size("col")
    fast = row_count == 2 and col_count == 4 and lax.axis_size("x") == 2
    core = lax.axis_index("core")
    quarter = lax.axis_index("x") * 2 + core

    if fast:
        feed_rows = jnp.concatenate(
            [
                jnp.concatenate(
                    [
                        lax.dynamic_slice_in_dim(swiglu_gate.T, quarter * 176, 176, 0),
                        lax.dynamic_slice_in_dim(swiglu_up.T, quarter * 176, 176, 0),
                    ],
                    axis=0,
                ),
                lax.dynamic_slice_in_dim(swiglu_down, quarter * 352, 352, 0),
            ],
            axis=1,
        )
        feed_full = lax.all_gather(feed_rows, AXES, axis=0, tiled=True).reshape(4, 2, 4, 352, 768)

        qk = jnp.concatenate([query_weight, key_weight], axis=1)
        qk = lax.dynamic_slice_in_dim(qk, core * 256, 256, 0)
        small = small_block(decay_down.T, decay_up, decay_bias, norm1_gain, head_gain, norm2_gain)
        qk = jnp.concatenate([qk, small[:, :256], small[:, 256:]], axis=0)
        v_part = lax.dynamic_slice_in_dim(value_weight, core * 256, 256, 0)
        by_col = ring_gather(qk, "col", col_count)
        v_full = ring_gather(ring_gather(v_part, "row", row_count), "col", col_count)
        ogout = jnp.concatenate([outgate_weight, out_weight], axis=1)
        ogout = lax.dynamic_slice_in_dim(ogout, core * 256, 256, 0)
        ogout, by_col = tied(ogout, by_col)
        ogout_cols = [ogout, *send([ogout] * (col_count - 1), "col")]
        qk_full = ring_gather(ring_gather(by_col, "row", row_count), "core", 2)
        v_full = ring_gather(v_full, "core", 2)
        small = jnp.concatenate([qk_full[0, :, :, 256:272], qk_full[0, :, :, 272:]], axis=-1)
        ddt = small[:, :, :4].reshape(2, LOW, 512)
        du = small[:, :, 4:12, :HK].transpose(0, 2, 1, 3).reshape(LOW, K)
        bias = small[:, :, 12, :64].reshape(1, K)
        g1 = small[:, :, 12, 128:256].reshape(1, D)
        hg = small[:, :, 12, 256:288].reshape(1, HV)
        g2 = small[:, :, 12, 384:].reshape(1, D)
    else:

        def whole(shard):
            if shard.ndim == 1:
                return lax.all_gather(shard, ("row", "col"), axis=0, tiled=True)
            wide = lax.all_gather(shard, "col", axis=1, tiled=True)
            return lax.all_gather(wide, "row", axis=0, tiled=True)

        def blocks(full, width):
            return full.reshape(2, 2, 256, 4, width).transpose(1, 0, 3, 2, 4)

        qk_full = jnp.concatenate([blocks(whole(query_weight), 128), blocks(whole(key_weight), 128)], axis=-1)
        v_full = blocks(whole(value_weight), 256).swapaxes(1, 2)
        ogout_full = jnp.concatenate([blocks(whole(outgate_weight), 256), blocks(whole(out_weight), 256)], axis=-1)
        gate_t, lift_t, down = whole(swiglu_gate).T, whole(swiglu_up).T, whole(swiglu_down)
        feed_gate = gate_t.reshape(4, 4, 176, 2, 512).transpose(1, 3, 0, 2, 4)
        feed_lift = lift_t.reshape(4, 4, 176, 2, 512).transpose(1, 3, 0, 2, 4)
        feed_down = down.reshape(2, 4, 352, 4, 256).transpose(1, 0, 3, 2, 4)
        feed_full = jnp.concatenate([jnp.concatenate([feed_gate, feed_lift], axis=3), feed_down], axis=-1)
        ddt = whole(decay_down).T.reshape(LOW, 2, 512).transpose(1, 0, 2)
        du = whole(decay_up)
        bias = whole(decay_bias).reshape(1, K)
        g1 = whole(norm1_gain).reshape(1, D)
        hg = whole(head_gain).reshape(1, HV)
        g2 = whole(norm2_gain).reshape(1, D)
    bias, g1, hg, g2 = (part.astype(F32) for part in (bias, g1, hg, g2))

    tokens = layer_input.shape[0]
    seg_c = segment_ids.reshape(tokens, 1)
    seg_r = segment_ids.reshape(tokens // CH, 1, CH)
    core_at = (core if fast else jnp.zeros_like(core)).astype(jnp.int32).reshape(1)

    normed, q, k, v, low, logit = project(layer_input, g1, qk_full, v_full, ddt, du, bias)
    if fast:
        q, ogout_cols = tied(q, ogout_cols)
        ogout = placed(ogout_cols, "col")
        other_row = swap(ogout, "row")
    mixed, states = attend(q, k, v, logit, segment_ids, seg_c, seg_r)
    if fast:
        mixed, other_row = tied(mixed, other_row)
        ogout = placed([ogout, other_row], "row")
        ogout_full = placed([ogout, swap(ogout, "core")], "core")
    og, gated, middle, normed_two = mix(layer_input, normed, mixed, ogout_full, hg, g2)
    layer_output, grad_normed_two, keep_gl, send_gl, keep_dn, send_dn = feed(
        core_at, normed_two, cotangent, middle, feed_full
    )
    grad_middle, branch, grad_og, grad_mixed, grad_g2, grad_hg = unmix(
        grad_normed_two, middle, cotangent, og, mixed, ogout_full, hg, g2
    )
    if fast:
        got_gl, got_dn = swap(send_gl, "core"), swap(send_dn, "core")
        x_at, row_at = lax.axis_index("x"), lax.axis_index("row")
        place = jnp.stack([x_at, row_at, lax.axis_index("col")]).astype(jnp.int32)
        go_g, st_g, go_l, st_l, st_d, *go_d = fold(place, keep_gl, got_gl, keep_dn, got_dn)
        branch, grad_og, go_g, go_l, go_d = tied(branch, grad_og, go_g, go_l, go_d)
        got_g, got_l, got_d = swap(go_g, "x"), swap(go_l, "row"), send(go_d, "col")
    keep_oo, send_oo = weight_grads(
        core_at, [normed, gated], [grad_og, branch], ((0, 0, (0,)), (1, 256, (1,))), True
    )
    if fast:
        grad_mixed, send_oo = tied(grad_mixed, send_oo)
        got_oo = swap(send_oo, "core")
    gq, gk, gv, glog = attend_back(q, k, v, logit, segment_ids, seg_c, seg_r, states, grad_mixed)
    keep_qkv, send_qkv = weight_grads(
        core_at, [normed], [gq, gk, gv], ((0, 0, (0, 1, 2)),)
    )
    if fast:
        send_qkv, got_g, got_l, got_d = tied(send_qkv, got_g, got_l, got_d)
        got_qkv = swap(send_qkv, "core")
        col_hi = lax.axis_index("col") // 2
        go_gl, st_gl, go_d, st_d = fold_two(place, [st_g, got_g], [st_l, got_l], [st_d, *got_d])
        go_qkv, st_qkv, go_oo, st_oo = fold_pair(place, keep_qkv, got_qkv, keep_oo, got_oo)
        glog, go_gl, go_d, go_qkv, go_oo = tied(glog, go_gl, go_d, go_qkv, go_oo)
        got_gl, got_d = swap(go_gl, "col"), swap(go_d, "x")
        got_qkv_x, got_oo_r = swap(go_qkv, "x"), swap(go_oo, "row")
    input_grad, grad_ddt, grad_du, grad_bias, grad_g1 = unproject(
        layer_input, normed, gq, gk, gv, glog, logit, low, grad_og, grad_middle, qk_full, v_full, ogout_full, ddt, du, g1
    )

    if fast:
        late = (got_gl, got_d, got_oo_r, got_qkv_x)
        input_grad, grad_g1, late = tied(input_grad, grad_g1, late)
        got_gl, got_d, got_oo_r, got_qkv_x = late
        qkv, oo, both = [st_qkv, got_qkv_x], [st_oo, got_oo_r], [st_gl, got_gl]
        go_qkv, go_oo, go_gl = piece_of(qkv, 1 - row_at, 0), piece_of(oo, 1 - x_at, 0), piece_of(both, 1 - col_hi, 0)
        go_qkv, go_oo, go_gl, grad_g1 = tied(go_qkv, go_oo, go_gl, grad_g1)
        qkv = [piece_of(qkv, row_at, 0), swap(go_qkv, "row")]
        oo = [piece_of(oo, x_at, 0), swap(go_oo, "x")]
        both = [piece_of(both, col_hi, 0), swap(go_gl, "col", 2)]
        tiny = jnp.concatenate(
            [
                grad_ddt.reshape(4, 4, 2, 512).transpose(2, 0, 1, 3),
                jnp.pad(grad_du.reshape(2, 8, 4, HK).transpose(0, 2, 1, 3), ((0, 0), (0, 0), (0, 0), (0, 384))),
                jnp.concatenate(
                    [
                        jnp.pad(grad_bias.reshape(2, 4, 64), ((0, 0), (0, 0), (0, 64))),
                        grad_g1.reshape(2, 4, 128),
                        jnp.pad(grad_hg.reshape(2, 4, 32), ((0, 0), (0, 0), (0, 96))),
                        grad_g2.reshape(2, 4, 128),
                    ],
                    axis=-1,
                ).reshape(2, 4, 1, 512),
                jnp.zeros((2, 4, 3, 512), F32),
            ],
            axis=2,
        )
        tiny = tiny + swap(tiny, "core")
        tiny = tiny + swap(tiny, "x")
        tiny = added([staying([tiny], "row", 0), *send(going([tiny], "row", 0), "row")])
        gate, lift = [[part[at : at + 2] for part in both] for at in (0, 2)]
        down = [st_d, got_d]
        gate = [piece_of(gate, row_at, 0), swap(piece_of(gate, 1 - row_at, 0), "row")]
        down = [piece_of(down, row_at, 0), swap(piece_of(down, 1 - row_at, 0), "row")]
        lift = [piece_of(lift, x_at, 0), swap(piece_of(lift, 1 - x_at, 0), "x")]
        down = added(down)
        feeds = share(jnp.concatenate([added(gate), added(lift), down[0], down[1]], axis=-1))
        rest = jnp.concatenate([added(qkv), added(oo)], axis=-1)
        rest = share(added([staying([rest], "col", 0), *send(going([rest], "col", 0), "col")]))
        tiny = added([staying([tiny], "col", 0), *send(going([tiny], "col", 0), "col")]).astype(F32)
        out_dd, out_du = tiny[:4].T, tiny[4:12, :HK]
        out_bias, out_g1, out_hg, out_g2 = tiny[12, :64], tiny[12, 128:256], tiny[12, 256:288], tiny[12, 384:]
    else:
        tiny = jnp.concatenate(
            [
                grad_ddt,
                jnp.pad(grad_du, ((0, 0), (0, D - K))),
                jnp.concatenate([grad_bias, grad_hg, jnp.zeros((1, D - K - HV), F32)], axis=1),
                grad_g1,
                grad_g2,
                jnp.zeros((5, D), F32),
            ],
            axis=0,
        )
        tiny = lax.psum(tiny, AXES)
        r, c = lax.axis_index("row"), lax.axis_index("col")

        def own(line, size):
            return lax.dynamic_slice_in_dim(line, (r * col_count + c) * size, size, 0)

        def own_block(full, shape):
            return lax.dynamic_slice(full, (r * shape[0], c * shape[1]), shape)

        out_bias = own(tiny[32, :K], decay_bias.shape[0])
        out_hg = own(tiny[32, K : K + HV], head_gain.shape[0])
        out_g1 = own(tiny[33], norm1_gain.shape[0])
        out_g2 = own(tiny[34], norm2_gain.shape[0])
        out_du = own_block(tiny[16:32, :K], decay_up.shape)
        down_rows = decay_down.shape
        out_dd = lax.dynamic_slice(tiny, (c * down_rows[1], r * down_rows[0]), down_rows[::-1]).T

    if fast:
        out_gate = feeds[..., :512].reshape(HC, 512).T
        out_lift = feeds[..., 512:1024].reshape(HC, 512).T
        out_down = jnp.stack([feeds[..., 1024:1280], feeds[..., 1280:]]).reshape(1408, 256)
        qkv = rest[..., :512].reshape(512, 512)
        oo = rest[..., 512:].reshape(512, 512)
        shards = [qkv[:, :128], qkv[:, 128:256], qkv[:, 256:], oo[:, :256], oo[:, 256:], out_gate, out_lift, out_down]
    else:

        def joined(keep, send):
            return jnp.stack([keep, send])

        keep_oo, send_oo = keep_oo.swapaxes(0, 1), send_oo.swapaxes(0, 1)

        def matrix(pack):
            return pack.transpose(2, 0, 1, 4, 3, 5).reshape(D, -1)

        oo = joined(keep_oo, send_oo)
        qkv = joined(keep_qkv, send_qkv)
        gl = joined(keep_gl, send_gl).reshape(2, 2, 2, 4, 2, 176, 512).transpose(4, 3, 0, 1, 5, 2, 6)
        gl = gl.reshape(2, FF, D)
        dn = joined(keep_dn, send_dn).transpose(2, 4, 0, 1, 5, 3, 6).reshape(FF, D)
        fulls = [
            matrix(qkv[..., :128]),
            matrix(qkv[..., 128:256]),
            matrix(qkv[..., 256:]),
            matrix(oo[..., :256]),
            matrix(oo[..., 256:]),
            gl[0].T,
            gl[1].T,
            dn,
        ]
        shards = []
        for full in fulls:
            part = lax.psum(full, ("x", "core"))
            part = lax.psum_scatter(part, "row", scatter_dimension=0, tiled=True)
            shards.append(lax.psum_scatter(part, "col", scatter_dimension=1, tiled=True))
    out_q, out_k, out_v, out_og, out_out, out_gate, out_lift, out_down = (part.astype(F32) for part in shards)
    return (
        layer_output,
        input_grad,
        out_g1,
        out_q,
        out_k,
        out_v,
        out_og,
        out_dd,
        out_du,
        out_bias,
        out_hg,
        out_out,
        out_g2,
        out_gate,
        out_lift,
        out_down,
    )


def solution(mesh):
    shape = dict(mesh.shape)
    finer = Mesh(mesh.devices.reshape(shape["dp"] // 2, 2, shape["row"], shape["col"]), AXES)
    tokens = P(AXES, None)
    vector = P(("row", "col"))
    matrix = P("row", "col")
    in_specs = (
        tokens, tokens, vector, matrix, matrix, matrix, matrix, matrix, matrix, vector, vector,
        matrix, vector, matrix, matrix, matrix, tokens,
    )
    out_specs = (
        tokens, tokens, vector, matrix, matrix, matrix, matrix, matrix, matrix, vector, vector,
        matrix, vector, matrix, matrix, matrix,
    )
    return jax.shard_map(per_device, mesh=finer, in_specs=in_specs, out_specs=out_specs, check_vma=False)
```
